128 devices in a mesh: row: 8 (over z, core), col: 16 (over y, x).
Axes of the slice: x: 4, y: 4, z: 4, core: 2. Of those that a mesh axis runs over, the one named last changes fastest.
Arguments:
- child_blocks: float32 [256, 64, 3072], P(('row', 'col'))
- home_child: int32 [256], P(('row', 'col')), may hold values from 0 to 255, each once
- col_tiles: int32 [256, 12], replicated, may hold values from 0 to 31, as said below
- tile_owner: int32 [32], replicated, may hold values from 0 to 31, each once
Outputs:
- r_rows: float32 [1024, 8192], P(None, 'col')
The draws below stay inside these ranges and needn't reach their ends.
Inputs may be any that keep to these rules, and one draw needn't show every extreme that they name: `home_child`: a permutation of the storage slots. `col_tiles`: the tiles of one row are distinct; every row names the tiles 0 to 3; every tile is named by some row. `tile_owner`: a permutation of the tiles.
All inputs are finite; a program needn't handle non-finite values.
Results may differ from the reference program's by a relative error of at most 0.00018.
Values sent between devices are 32-bit elements; how exact they have to be, the bound alone decides.
A program may use at most 192 MiB of HBM per device.

```python
import jax
import jax.numpy as jnp
from jax import lax

TILE_WIDTH = 256
FRONT_COLS = 8192
COL_TILES = 32
CHILD_TILES = 12
CHILD_ROWS = 64
PANELS = 4
CHILDREN = 256
FRONT_ROWS = 16384


def draw_child_blocks(key, part):
    key = jax.random.fold_in(key, 11)
    common_key, own_key = jax.random.split(key)
    shape = (CHILDREN, CHILD_ROWS, CHILD_TILES, TILE_WIDTH)
    weight = 1.5
    own = jax.random.normal(own_key, shape, jnp.float32)
    common = jax.random.normal(common_key, (CHILDREN, CHILD_ROWS, 1, TILE_WIDTH), jnp.float32)
    factor = (FRONT_ROWS * (1.0 + weight * weight)) ** (-0.5)
    blocks = factor * (weight * common + own)
    return blocks.reshape(CHILDREN, CHILD_ROWS, CHILD_TILES * TILE_WIDTH).astype(jnp.float32)


def draw_col_tiles(key, part):
    key = jax.random.fold_in(key, 23)
    order_key, start_key, shuffle_key = jax.random.split(key, 3)
    others = COL_TILES - PANELS
    extra = CHILD_TILES - PANELS
    ordering = (jax.random.permutation(order_key, others) + PANELS).astype(jnp.int32)
    child_index = jnp.arange(CHILDREN, dtype=jnp.int32)
    random_start = jax.random.randint(start_key, (CHILDREN,), 0, others).astype(jnp.int32)
    start = jnp.where(child_index * extra < others, child_index * extra, random_start)
    window = (start[:, None] + jnp.arange(extra, dtype=jnp.int32)[None, :]) % others
    picked = ordering[window]
    leading = jnp.broadcast_to(jnp.arange(PANELS, dtype=jnp.int32)[None, :], (CHILDREN, PANELS))
    tiles = jnp.concatenate([leading, picked], axis=1).astype(jnp.int32)
    scores = jax.random.randint(shuffle_key, (CHILDREN, CHILD_TILES), 0, 1 << 20) * CHILD_TILES
    scores = scores + jnp.arange(CHILD_TILES, dtype=jnp.int32)[None, :]
    order = jnp.argsort(scores, axis=1, stable=True)
    return jnp.take_along_axis(tiles, order, axis=1).astype(jnp.int32)


def setup_inputs(seed: int = 0) -> dict:
    keys = jax.random.split(jax.random.key(seed), 5)
    child_blocks = draw_child_blocks(jax.random.fold_in(keys[4], 71), 0)
    home_child = jax.random.permutation(keys[1], CHILDREN).astype(jnp.int32)
    col_tiles = draw_col_tiles(jax.random.fold_in(keys[4], 71), 0)
    tile_owner = jax.random.permutation(keys[3], COL_TILES).astype(jnp.int32)
    return dict(child_blocks=child_blocks, home_child=home_child, col_tiles=col_tiles, tile_owner=tile_owner)


def storage_positions(home_child, col_tiles, tile_owner):
    count = col_tiles.shape[0]
    tiles_all = tile_owner.shape[0]
    picked = home_child[:, None] == jnp.arange(count, dtype=jnp.int32)[None, :]
    child_tiles = jnp.sum(jnp.where(picked[:, :, None], col_tiles[None, :, :], 0), axis=1).astype(jnp.int32)
    matches = child_tiles[:, :, None] == jnp.arange(tiles_all, dtype=jnp.int32)[None, None, :]
    return jnp.sum(jnp.where(matches, tile_owner[None, None, :], 0), axis=2).astype(jnp.int32)

def reference(child_blocks, home_child, col_tiles, tile_owner):
    highest = lax.Precision.HIGHEST
    position = storage_positions(home_child, col_tiles, tile_owner)
    onehot = (position[:, :, None] == jnp.arange(COL_TILES, dtype=jnp.int32)[None, None, :]).astype(jnp.float32)
    shaped = child_blocks.reshape(CHILDREN, CHILD_ROWS, CHILD_TILES, TILE_WIDTH)
    front = jnp.einsum('nrjc,njk->nrkc', shaped, onehot, precision=highest)
    front = front.reshape(FRONT_ROWS, FRONT_COLS)
    results = []
    for step in range(PANELS):
        start = (tile_owner[step] * TILE_WIDTH).astype(jnp.int32)
        panel = lax.dynamic_slice_in_dim(front, start, TILE_WIDTH, 1)
        gram = jnp.dot(panel.T.astype(jnp.float32), panel.astype(jnp.float32), precision=highest, preferred_element_type=jnp.float32)
        lower = jnp.linalg.cholesky(gram)
        basis = jax.scipy.linalg.solve_triangular(lower, panel.T, lower=True).T
        projected = jnp.dot(basis.T.astype(jnp.float32), front.astype(jnp.float32), precision=highest, preferred_element_type=jnp.float32)
        front = front - jnp.dot(basis.astype(jnp.float32), projected.astype(jnp.float32), precision=highest, preferred_element_type=jnp.float32)
        results.append(projected)
    return jnp.concatenate(results, axis=0)
```

```python
import jax
import jax.numpy as jnp
from jax import lax
from jax.experimental import pallas as pl
from jax.experimental.pallas import tpu as pltpu
from jax.sharding import PartitionSpec as P

T = 256
TILES = 32
CT = 12
ROWS = 64
FRONT_COLS = 8192
PANELS = 4
OWN = 2
REST = CT - PANELS
H = 2
HW = T // H
NEWTON = 4
RESIDUAL = 1e-5
SHARE = 0.1
F32 = jnp.float32
BF = jnp.bfloat16
MESH = pl.DeviceIdType.MESH
BLOCKS = [(q, r) for q in range(PANELS) for r in range(q, PANELS)]
BLK = {qr: i for i, qr in enumerate(BLOCKS)}
GROWS = len(BLOCKS) * T
GHALF = GROWS // 2
GQ = GHALF // 2
GC = GQ // 4
GS = GC // 4


def split(x):
    hi = x.astype(BF)
    lo = (x - hi.astype(F32)).astype(BF)
    return hi, lo


def dg(a, b, ca, cb):
    return lax.dot_general(a, b, (((ca,), (cb,)), ((), ())), preferred_element_type=F32)


def dot3(a, b, ca=1, cb=0):
    ah, al = a
    bh, bl = b
    return dg(ah, bh, ca, cb) + (dg(ah, bl, ca, cb) + dg(al, bh, ca, cb))


def sort_kernel(home_ref, tiles_ref, owner_ref, blocks_ref, panels_ref, packed_ref, table_ref):
    lane = lax.broadcasted_iota(jnp.int32, (8, 128), 1)
    sub = lax.broadcasted_iota(jnp.int32, (8, 128), 0)
    table = jnp.full((8, 128), REST, jnp.int32)
    place = []
    for c in range(OWN):
        home = home_ref[c]
        panel_at = [jnp.int32(0)] * PANELS
        rest_at = [jnp.int32(0)] * REST
        count = jnp.int32(0)
        for j in range(CT):
            t = tiles_ref[home, j]
            p = owner_ref[t]
            rest = t >= PANELS
            for m in range(PANELS):
                panel_at[m] = jnp.where(t == m, j, panel_at[m])
            for i in range(min(j + 1, REST)):
                rest_at[i] = jnp.where(jnp.logical_and(rest, count == i), j, rest_at[i])
            table = jnp.where(
                jnp.logical_and(jnp.logical_and(lane == p, sub == c), rest), count, table)
            count = count + rest.astype(jnp.int32)
        place.append((panel_at, rest_at))
    table_ref[...] = table
    for c in range(OWN):
        for m in range(PANELS):
            at = pl.multiple_of(place[c][0][m] * T, T)
            panels_ref[m, c * ROWS:(c + 1) * ROWS, :] = blocks_ref[c, :, pl.ds(at, T)]
        for i in range(REST):
            at = pl.multiple_of(place[c][1][i] * T, T)
            got = blocks_ref[c, :, pl.ds(at, T)]
            for h in range(H):
                packed_ref[h, c * ROWS:(c + 1) * ROWS, i * HW:(i + 1) * HW] = (
                    got[:, h * HW:(h + 1) * HW])


def kernel(
    owner_ref, pown, packed_ref, table_ref,
    out_ref, good_ref,
    ag, pg, tab, tab_s, agh, agl, pth, ptl, bh, bl, sp,
    ra, rb, sa, sb, ra2, rb2, sfull,
    gbuf, grc, ga, gb, gsa, gsb, ga2, gb2, gza, gzb,
    wref, wh_ref, wl_ref, cw, uth, utl, rp,
    xsem_s, xsem_r, lsem,
):
    row = lax.axis_index("row")
    col = lax.axis_index("col")
    z = row // 2
    k = row % 2
    y = col // 4
    x = col % 4
    sib = (z * 2 + (1 - k), col)

    def zp(d):
        return (lax.rem(z + d, 4) * 2 + k, col)

    def xp(d):
        return (row, y * 4 + lax.rem(x + d, 4))

    def yp(d):
        return (row, lax.rem(y + d, 4) * 4 + x)

    barrier = pltpu.get_barrier_semaphore()
    partners = [sib] + [f(d) for f in (zp, xp, yp) for d in (1, 2, 3)]
    for dev in partners:
        pl.semaphore_signal(barrier, inc=1, device_id=dev, device_id_type=MESH)

    counter = [0]

    def rcopy(src, dst, dev):
        i = counter[0]
        counter[0] += 1
        return pltpu.make_async_remote_copy(
            src_ref=src, dst_ref=dst, send_sem=xsem_s.at[i], recv_sem=xsem_r.at[i],
            device_id=dev, device_id_type=MESH,
        )

    sends = []
    left_early = []

    def go(copy):
        copy.start()
        sends.append(copy)
        return copy

    pg[z, k] = pown[z]
    tab[z, k] = table_ref[...]
    for h in range(H):
        ag[z, k, h] = packed_ref[h]
    pl.semaphore_wait(barrier, len(partners))

    pz, tz = [], []
    for d in (1, 2, 3):
        pz.append(go(rcopy(pown.at[lax.rem(z + d, 4)], pg.at[z, k], zp(d))))
        tz.append(go(rcopy(tab.at[z, k], tab.at[z, k], zp(d))))
    psib = [go(rcopy(pown.at[z], pg.at[z, k], sib))]
    tsib = [go(rcopy(tab.at[z, k], tab.at[z, k], sib))]

    def rows(c):
        return pl.ds(c * ROWS, ROWS)

    ar, al_, asib = {}, {}, {}

    def start_a(h):
        for c in range(OWN):
            me = ag.at[z, k, h, rows(c)]
            ar[h, c] = go(rcopy(me, me, zp(1)))
            other = ag.at[z, k, h, rows(1 - c)]
            al_[h, 1 - c] = go(rcopy(other, other, zp(3)))
        mine = ag.at[z, k, h]
        asib[h] = [go(rcopy(mine, mine, sib))]

    start_a(0)
    fr, fl = {}, {}

    def forward_a(h):
        left = lax.rem(z + 3, 4)
        right = lax.rem(z + 1, 4)
        ar[h, 0].wait_recv()
        v = ag.at[left, k, h, rows(0)]
        fr[h] = go(rcopy(v, v, zp(1)))
        al_[h, 1].wait_recv()
        v = ag.at[right, k, h, rows(1)]
        fl[h] = go(rcopy(v, v, zp(3)))
        ar[h, 1].wait_recv()
        v = ag.at[left, k, h]
        asib[h].append(go(rcopy(v, v, sib)))
        al_[h, 0].wait_recv()
        v = ag.at[right, k, h]
        asib[h].append(go(rcopy(v, v, sib)))

    def finish_a(h):
        far = lax.rem(z + 2, 4)
        fr[h].wait_recv()
        fl[h].wait_recv()
        v = ag.at[far, k, h]
        asib[h].append(go(rcopy(v, v, sib)))

    def forward_p():
        for i, d in enumerate((1, 2, 3)):
            src = lax.rem(z + 4 - d, 4)
            pz[i].wait_recv()
            tz[i].wait_recv()
            v = pg.at[src, k]
            psib.append(go(rcopy(v, v, sib)))
            t = tab.at[src, k]
            tsib.append(go(rcopy(t, t, sib)))

    def gram():
        halves = [split(pown[m]) for m in range(PANELS)]
        for i, (q, r) in enumerate(BLOCKS):
            gbuf[i * T:(i + 1) * T, :] = dot3(halves[q], halves[r], 0, 0)

    gram()
    gk = pl.multiple_of(k * GHALF, GHALF)
    go_ = pl.multiple_of((1 - k) * GHALF, GHALF)
    g0 = go(rcopy(gbuf.at[pl.ds(go_, GHALF)], grc, sib))
    g0.wait_recv()

    def add_rows(dst, off, n, srcs):
        step = 160 if n % 160 == 0 else n

        def body(i, carry):
            o = pl.multiple_of(i * step, 8)
            acc = dst[pl.ds(off + o, step), :]
            for s in srcs:
                acc = acc + s[pl.ds(o, step), :]
            dst[pl.ds(off + o, step), :] = acc
            return carry

        lax.fori_loop(0, n // step, body, 0)

    add_rows(gbuf, gk, GHALF, [grc])
    base_a = gk
    base_b = pl.multiple_of(gk + GQ, GQ)
    g1a, g1b = [], []
    for d in (1, 2, 3):
        ox = pl.multiple_of(base_a + lax.rem(x + d, 4) * GC, GC)
        oy = pl.multiple_of(base_b + lax.rem(y + d, 4) * GC, GC)
        g1a.append(go(rcopy(gbuf.at[pl.ds(ox, GC)], ga.at[d - 1], xp(d))))
        g1b.append(go(rcopy(gbuf.at[pl.ds(oy, GC)], gb.at[d - 1], yp(d))))
    forward_p()
    for c in g1a + g1b:
        c.wait_recv()
    my_a = pl.multiple_of(base_a + x * GC, GC)
    my_b = pl.multiple_of(base_b + y * GC, GC)
    gsa[...] = gbuf[pl.ds(my_a, GC), :] + ga[0] + ga[1] + ga[2]
    gsb[...] = gbuf[pl.ds(my_b, GC), :] + gb[0] + gb[1] + gb[2]
    g2a, g2b = [], []
    for d in (1, 2, 3):
        oy = pl.multiple_of(lax.rem(y + d, 4) * GS, GS)
        ox = pl.multiple_of(lax.rem(x + d, 4) * GS, GS)
        g2a.append(go(rcopy(gsa.at[pl.ds(oy, GS)], ga2.at[d - 1], yp(d))))
        g2b.append(go(rcopy(gsb.at[pl.ds(ox, GS)], gb2.at[d - 1], xp(d))))
    for c in g2a + g2b:
        c.wait_recv()
    oya = pl.multiple_of(y * GS, GS)
    oxb = pl.multiple_of(x * GS, GS)
    gza[z] = gsa[pl.ds(oya, GS), :] + ga2[0] + ga2[1] + ga2[2]
    gzb[z] = gsb[pl.ds(oxb, GS), :] + gb2[0] + gb2[1] + gb2[2]
    g3 = []
    for d in (1, 2, 3):
        g3.append(go(rcopy(gza.at[z], gza.at[z], zp(d))))
        g3.append(go(rcopy(gzb.at[z], gzb.at[z], zp(d))))
    forward_a(0)
    for c in g3:
        c.wait_recv()
    fa = pl.multiple_of(my_a + y * GS, GS)
    fb = pl.multiple_of(my_b + x * GS, GS)
    gfin_a = gza[0] + gza[1] + gza[2] + gza[3]
    gfin_b = gzb[0] + gzb[1] + gzb[2] + gzb[3]
    cw[pl.ds(fa, GS), :] = gfin_a
    cw[pl.ds(fb, GS), :] = gfin_b
    g4 = []
    for d in (1, 2, 3):
        v = cw.at[pl.ds(fa, GS)]
        g4.append(go(rcopy(v, v, yp(d))))
        v = cw.at[pl.ds(fb, GS)]
        g4.append(go(rcopy(v, v, xp(d))))
    for c in g4:
        c.wait_recv()
    g5 = []
    for d in (1, 2, 3):
        v = cw.at[pl.ds(my_a, GC)]
        g5.append(go(rcopy(v, v, xp(d))))
        v = cw.at[pl.ds(my_b, GC)]
        g5.append(go(rcopy(v, v, yp(d))))
    finish_a(0)
    for c in g5:
        c.wait_recv()
    v = cw.at[pl.ds(gk, GHALF)]
    g6 = go(rcopy(v, v, sib))
    start_a(1)

    for c in psib + tsib:
        c.wait_recv()
    tcopy = pltpu.make_async_copy(tab, tab_s, lsem.at[0])
    tcopy.start()
    for i in range(8):
        hi, lo = split(jnp.transpose(pg[i // 2, i % 2]))
        pth[:, i * 128:(i + 1) * 128] = hi
        ptl[:, i * 128:(i + 1) * 128] = lo
    tcopy.wait()
    zero = jnp.zeros((8 * 128, HW), BF)
    agh[REST] = zero
    agl[REST] = zero

    def products(h):
        for c in asib[h]:
            c.wait_recv()

        def conv(i, carry):
            o = pl.multiple_of(i * 128, 128)
            hi, lo = split(ag[i // 2, lax.rem(i, 2), h])
            for t in range(REST):
                agh[t, pl.ds(o, 128), :] = hi[:, t * HW:(t + 1) * HW]
                agl[t, pl.ds(o, 128), :] = lo[:, t * HW:(t + 1) * HW]
            return carry

        lax.fori_loop(0, 8, conv, 0)

        def pair(i, carry):
            for s in range(2):
                slot = (2 * i + s) * 2 + k
                for n in range(16):
                    at = tab_s[n // 4, (n // 2) % 2, n % 2, slot]
                    bh[n * ROWS:(n + 1) * ROWS, s * HW:(s + 1) * HW] = (
                        agh[at, n * ROWS:(n + 1) * ROWS, :])
                    bl[n * ROWS:(n + 1) * ROWS, s * HW:(s + 1) * HW] = (
                        agl[at, n * ROWS:(n + 1) * ROWS, :])
            got = dot3((pth[...], ptl[...]), (bh[...], bl[...]))
            yy = (2 * i) // 4
            xx = lax.rem(2 * i, 4)
            sp[h, yy, xx] = got[:, 0:HW]
            sp[h, yy, xx + 1] = got[:, HW:]
            return carry

        lax.fori_loop(0, 8, pair, 0)

    s1, s2, s3 = {}, {}, {}

    def reduce1(h):
        s1[h] = []
        for d in (1, 2, 3):
            s1[h].append(go(rcopy(
                sp.at[h, :, lax.rem(x + d, 4), pl.ds(0, 128)], ra.at[h, d - 1], xp(d))))
            s1[h].append(go(rcopy(
                sp.at[h, lax.rem(y + d, 4), :, pl.ds(128, 128)], rb.at[h, d - 1], yp(d))))

    def reduce2(h):
        for c in s1[h]:
            c.wait_recv()
        for i in range(4):
            sa[h, i] = sp[h, i, x, 0:128, :] + ra[h, 0, i] + ra[h, 1, i] + ra[h, 2, i]
            sb[h, i] = sp[h, y, i, 128:256, :] + rb[h, 0, i] + rb[h, 1, i] + rb[h, 2, i]
        s2[h] = []
        for d in (1, 2, 3):
            s2[h].append(go(rcopy(sa.at[h, lax.rem(y + d, 4)], ra2.at[h, d - 1], yp(d))))
            s2[h].append(go(rcopy(sb.at[h, lax.rem(x + d, 4)], rb2.at[h, d - 1], xp(d))))

    def gather1(h):
        for c in s2[h]:
            c.wait_recv()
        sfull[z, k, h, 0:128, :] = sa[h, y] + ra2[h, 0] + ra2[h, 1] + ra2[h, 2]
        sfull[z, k, h, 128:256, :] = sb[h, x] + rb2[h, 0] + rb2[h, 1] + rb2[h, 2]
        v = sfull.at[z, k, h]
        s3[h] = [go(rcopy(v, v, zp(d))) for d in (1, 2, 3)]
        s3[h].append(go(rcopy(v, v, sib)))

    def gather2(h):
        for d in (1, 2, 3):
            s3[h][d - 1].wait_recv()
            v = sfull.at[lax.rem(z + 4 - d, 4), k, h]
            s3[h].append(go(rcopy(v, v, sib)))

    rr = lax.broadcasted_iota(jnp.int32, (T, T), 0)
    cc = lax.broadcasted_iota(jnp.int32, (T, T), 1)
    eye = rr == cc
    phi = jnp.where(eye, 0.5, jnp.where(rr > cc, 1.0, 0.0)).astype(F32)
    ident = jnp.where(eye, 1.0, 0.0).astype(F32)
    checks = []
    lengths = []

    def block(q, r):
        i = BLK[q, r]
        return pl.ds(i * T, T)

    def factor(p):
        if p == 0:
            for q in range(PANELS):
                diag = jnp.where(eye, cw[block(q, q), :], 0.0)
                lengths.append(jnp.sum(diag, axis=0, keepdims=True))
        c0 = cw[block(p, p), :]
        diag = jnp.where(eye, c0, 0.0)
        left = jnp.sum(diag, axis=0, keepdims=True)
        dr = lax.rsqrt(left)
        dc = lax.rsqrt(jnp.sum(diag, axis=1, keepdims=True))
        scaled = c0 * dr * dc
        sh, sl = split(scaled)
        n0 = phi * (scaled - ident)
        wref[...] = ident - n0

        def it(i, carry):
            w = split(wref[...])
            t = split(dot3(w, (sh, sl)))
            e = dot3(t, w, 1, 1) - ident
            n = phi * e
            wref[...] = wref[...] - dot3(split(n), w)
            return jnp.sum(e * e, axis=0, keepdims=True)

        err = lax.fori_loop(0, NEWTON - 1, it, jnp.zeros((1, T), F32))
        checks.append(jnp.sum(err) < RESIDUAL)
        checks.append(jnp.min(left - SHARE * lengths[p]) > 0.0)
        w = wref[...] * dr
        hi, lo = split(w)
        wh_ref[p] = hi
        wl_ref[p] = lo
        for r in range(p, PANELS):
            c = split(cw[block(p, r), :])
            u = dot3((hi, lo), c)
            rp[r, p] = u
            if r > p:
                uh, ul = split(jnp.transpose(u))
                uth[BLK[p, r]] = uh
                utl[BLK[p, r]] = ul
        for q in range(p + 1, PANELS):
            for r in range(q, PANELS):
                upd = dot3((uth[BLK[p, q]], utl[BLK[p, q]]), split(rp[r, p]))
                cw[block(q, r), :] = cw[block(q, r), :] - upd
        for r in range(p):
            rp[r, p] = jnp.zeros((T, T), F32)

    products(0)
    reduce1(0)
    g6.wait_recv()
    forward_a(1)
    for c in g4 + g5 + [g6]:
        c.wait_send()
        left_early.append(id(c))
    factor(0)
    reduce2(0)
    finish_a(1)
    factor(1)
    gather1(0)
    products(1)
    reduce1(1)
    gather2(0)
    factor(2)
    factor(3)
    reduce2(1)
    gather1(1)
    gather2(1)
    for c in s3[0][3:] + s3[1][3:]:
        c.wait_recv()

    for s in range(2):
        xs = []
        slot = col * 2 + s
        which = jnp.int32(0)
        is_panel = jnp.int32(0)
        for m in range(PANELS):
            hit = owner_ref[m] == slot
            which = jnp.where(hit, m, which)
            is_panel = jnp.where(hit, 1, is_panel)
        mask = jnp.full((T, T), is_panel, jnp.int32) == 1
        for p in range(PANELS):
            acc = jnp.concatenate([sfull[p, s, h] for h in range(H)], axis=1)
            for q in range(p):
                acc = acc - dot3((uth[BLK[q, p]], utl[BLK[q, p]]), xs[q])
            got = dot3((wh_ref[p], wl_ref[p]), split(acc))
            xs.append(split(got))
            out_ref[p * T:(p + 1) * T, s * T:(s + 1) * T] = jnp.where(mask, rp[which, p], got)
    good = checks[0]
    for c in checks[1:]:
        good = jnp.logical_and(good, c)
    good_ref[0] = good.astype(jnp.int32)
    for c in sends:
        if id(c) not in left_early:
            c.wait_send()


def fast(child_blocks, home_child, col_tiles, tile_owner):
    sem = 120
    vm = pltpu.VMEM
    vmem = pl.BlockSpec(memory_space=pltpu.VMEM)
    smem = pl.BlockSpec(memory_space=pltpu.SMEM)
    panels, packed, table = pl.pallas_call(
        sort_kernel,
        out_shape=(
            jax.ShapeDtypeStruct((PANELS, OWN * ROWS, T), F32),
            jax.ShapeDtypeStruct((H, OWN * ROWS, REST * HW), F32),
            jax.ShapeDtypeStruct((8, 128), jnp.int32),
        ),
        in_specs=[smem, smem, smem, vmem],
        out_specs=(vmem, vmem, vmem),
        name="sort_tiles",
    )(home_child, col_tiles, tile_owner, child_blocks)
    return pl.pallas_call(
        kernel,
        out_shape=(
            jax.ShapeDtypeStruct((PANELS * T, 2 * T), F32),
            jax.ShapeDtypeStruct((1,), jnp.int32),
        ),
        in_specs=[smem, vmem, vmem, vmem],
        out_specs=(vmem, smem),
        scratch_shapes=[
            vm((4, 2, H, OWN * ROWS, REST * HW), F32),
            vm((4, 2, OWN * ROWS, T), F32),
            vm((4, 2, 8, 128), jnp.int32),
            pltpu.SMEM((4, 2, 8, 128), jnp.int32),
            vm((REST + 1, 8 * 128, HW), BF),
            vm((REST + 1, 8 * 128, HW), BF),
            vm((T, 1024), BF),
            vm((T, 1024), BF),
            vm((1024, T), BF),
            vm((1024, T), BF),
            vm((H, 4, 4, T, HW), F32),
            vm((H, 3, 4, 128, HW), F32),
            vm((H, 3, 4, 128, HW), F32),
            vm((H, 4, 128, HW), F32),
            vm((H, 4, 128, HW), F32),
            vm((H, 3, 128, HW), F32),
            vm((H, 3, 128, HW), F32),
            vm((4, 2, H, T, HW), F32),
            vm((GROWS, T), F32),
            vm((GHALF, T), F32),
            vm((3, GC, T), F32),
            vm((3, GC, T), F32),
            vm((GC, T), F32),
            vm((GC, T), F32),
            vm((3, GS, T), F32),
            vm((3, GS, T), F32),
            vm((4, GS, T), F32),
            vm((4, GS, T), F32),
            vm((T, T), F32),
            vm((PANELS, T, T), BF),
            vm((PANELS, T, T), BF),
            vm((GROWS, T), F32),
            vm((len(BLOCKS), T, T), BF),
            vm((len(BLOCKS), T, T), BF),
            vm((PANELS, PANELS, T, T), F32),
            pltpu.SemaphoreType.DMA((sem,)),
            pltpu.SemaphoreType.DMA((sem,)),
            pltpu.SemaphoreType.DMA((1,)),
        ],
        compiler_params=pltpu.CompilerParams(
            collective_id=0, has_side_effects=True, vmem_limit_bytes=60 * 1024 * 1024
        ),
        cost_estimate=pl.CostEstimate(flops=10**10, bytes_accessed=10**7, transcendentals=0),
        name="front",
    )(tile_owner, panels, packed, table)


def broadcast(x, axis, root):
    mine = lax.axis_index(axis) == root
    return lax.psum(jnp.where(mine, x, jnp.zeros_like(x)), axis)


def storage_positions(home_child, col_tiles, tile_owner):
    count = col_tiles.shape[0]
    tiles_all = tile_owner.shape[0]
    picked = home_child[:, None] == jnp.arange(count, dtype=jnp.int32)[None, :]
    child_tiles = jnp.sum(jnp.where(picked[:, :, None], col_tiles[None, :, :], 0), axis=1)
    matches = child_tiles[:, :, None] == jnp.arange(tiles_all, dtype=jnp.int32)[None, None, :]
    return jnp.sum(jnp.where(matches, tile_owner[None, None, :], 0), axis=2)


def general(child_blocks, home_child, col_tiles, tile_owner):
    highest = lax.Precision.HIGHEST
    col_count = lax.axis_size("col")
    local_cols = FRONT_COLS // col_count
    held = local_cols // T
    my_col = lax.axis_index("col")
    first_held = my_col * held
    position = storage_positions(home_child, col_tiles, tile_owner)
    piece_blocks = lax.all_gather(child_blocks, "col", axis=0, tiled=True)
    piece_slots = lax.all_gather(position, "col", axis=0, tiled=True)
    count = piece_blocks.shape[0]
    local_tile = piece_slots - first_held
    mine = (local_tile[:, :, None] == jnp.arange(held, dtype=jnp.int32)[None, None, :]).astype(
        jnp.float32
    )
    shaped = piece_blocks.reshape(count, ROWS, CT, T)
    placed = jnp.einsum("nrjc,njk->nrkc", shaped, mine, precision=highest)
    placed = placed.reshape(count * ROWS, local_cols)
    front = placed
    identity = jnp.eye(T, dtype=jnp.float32)
    results = []
    for step in range(PANELS):
        stored_at = tile_owner[step]
        holder = stored_at // held
        offset = (stored_at - holder * held) * T
        is_holder = holder == my_col
        panel = lax.dynamic_slice_in_dim(front, offset, T, 1)
        panel = jnp.where(is_holder, panel, 0.0)
        gram_part = jnp.dot(panel.T, panel, precision=highest, preferred_element_type=jnp.float32)
        gram = lax.psum(gram_part, "row")
        gram = gram + jnp.where(is_holder, 0.0, identity)
        lower = jnp.linalg.cholesky(gram)
        basis = jax.scipy.linalg.solve_triangular(lower, panel.T, lower=True).T
        basis = broadcast(basis, "col", holder)
        local_proj = jnp.dot(basis.T, front, precision=highest, preferred_element_type=jnp.float32)
        projected = lax.psum(local_proj, "row")
        front = front - jnp.dot(
            basis, projected, precision=highest, preferred_element_type=jnp.float32
        )
        results.append(projected)
    stacked = jnp.concatenate(results, axis=0)
    return stacked


def body(child_blocks, home_child, col_tiles, tile_owner):
    args = (child_blocks, home_child, col_tiles, tile_owner)
    out, good = fast(*args)
    return lax.cond(good[0] == 1, lambda *a: out, general, *args)


def solution(mesh):
    return jax.shard_map(
        body,
        mesh=mesh,
        in_specs=(P(("row", "col"), None, None), P(("row", "col")), P(), P()),
        out_specs=P(None, "col"),
        check_vma=False,
    )
```

```python
import jax
import jax.numpy as jnp
from jax import lax
from jax.experimental import pallas as pl
from jax.experimental.pallas import tpu as pltpu
from jax.sharding import PartitionSpec as P

T = 256
TILES = 32
CT = 12
ROWS = 64
FRONT_COLS = 8192
PANELS = 4
OWN = 2
REST = CT - PANELS
H = 2
HW = T // H
NEWTON = 4
RESIDUAL = 1e-5
SHARE = 0.1
F32 = jnp.float32
BF = jnp.bfloat16
MESH = pl.DeviceIdType.MESH
BLOCKS = [(q, r) for q in range(PANELS) for r in range(q, PANELS)]
BLK = {qr: i for i, qr in enumerate(BLOCKS)}
GROWS = len(BLOCKS) * T
GHALF = GROWS // 2
GQ = GHALF // 2
GC = GQ // 4
GS = GC // 4


def split(x):
    hi = x.astype(BF)
    lo = (x - hi.astype(F32)).astype(BF)
    return hi, lo


def dg(a, b, ca, cb):
    return lax.dot_general(a, b, (((ca,), (cb,)), ((), ())), preferred_element_type=F32)


def dot3(a, b, ca=1, cb=0):
    ah, al = a
    bh, bl = b
    return dg(ah, bh, ca, cb) + (dg(ah, bl, ca, cb) + dg(al, bh, ca, cb))


def kernel(
    home_ref, tiles_ref, owner_ref, blocks_ref,
    out_ref, good_ref,
    ag, pown, pg, tab, tab_s, agh, agl, pth, ptl, bh, bl, sp,
    ra, rb, sa, sb, ra2, rb2, sfull,
    gbuf, grc, ga, gb, gsa, gsb, ga2, gb2, gza, gzb,
    wref, wh_ref, wl_ref, cw, uth, utl, rp,
    xsem_s, xsem_r, lsem,
):
    row = lax.axis_index("row")
    col = lax.axis_index("col")
    z = row // 2
    k = row % 2
    y = col // 4
    x = col % 4
    sib = (z * 2 + (1 - k), col)

    def zp(d):
        return (lax.rem(z + d, 4) * 2 + k, col)

    def xp(d):
        return (row, y * 4 + lax.rem(x + d, 4))

    def yp(d):
        return (row, lax.rem(y + d, 4) * 4 + x)

    barrier = pltpu.get_barrier_semaphore()
    partners = [sib] + [f(d) for f in (zp, xp, yp) for d in (1, 2, 3)]
    for dev in partners:
        pl.semaphore_signal(barrier, inc=1, device_id=dev, device_id_type=MESH)

    counter = [0]

    def rcopy(src, dst, dev):
        i = counter[0]
        counter[0] += 1
        return pltpu.make_async_remote_copy(
            src_ref=src, dst_ref=dst, send_sem=xsem_s.at[i], recv_sem=xsem_r.at[i],
            device_id=dev, device_id_type=MESH,
        )

    sends = []
    left_early = []

    def go(copy):
        copy.start()
        sends.append(copy)
        return copy

    lane = lax.broadcasted_iota(jnp.int32, (8, 128), 1)
    sub = lax.broadcasted_iota(jnp.int32, (8, 128), 0)
    table = jnp.full((8, 128), REST, jnp.int32)
    place = []
    for c in range(OWN):
        home = home_ref[c]
        panel_at = [jnp.int32(0)] * PANELS
        rest_at = [jnp.int32(0)] * REST
        count = jnp.int32(0)
        for j in range(CT):
            t = tiles_ref[home, j]
            p = owner_ref[t]
            rest = t >= PANELS
            for m in range(PANELS):
                panel_at[m] = jnp.where(t == m, j, panel_at[m])
            for i in range(min(j + 1, REST)):
                rest_at[i] = jnp.where(jnp.logical_and(rest, count == i), j, rest_at[i])
            table = jnp.where(
                jnp.logical_and(jnp.logical_and(lane == p, sub == c), rest), count, table)
            count = count + rest.astype(jnp.int32)
        place.append((panel_at, rest_at))
    tab[z, k] = table
    for c in range(OWN):
        for m in range(PANELS):
            pown[m, c * ROWS:(c + 1) * ROWS, :] = blocks_ref[c, :, pl.ds(place[c][0][m] * T, T)]

    def pack(h):
        for c in range(OWN):
            for i in range(REST):
                at = place[c][1][i] * T + h * HW
                ag[z, k, h, c * ROWS:(c + 1) * ROWS, i * HW:(i + 1) * HW] = (
                    blocks_ref[c, :, pl.ds(at, HW)])

    pack(0)
    pg[z, k] = pown[z]
    pl.semaphore_wait(barrier, len(partners))

    pz, tz = [], []
    for d in (1, 2, 3):
        pz.append(go(rcopy(pown.at[lax.rem(z + d, 4)], pg.at[z, k], zp(d))))
        tz.append(go(rcopy(tab.at[z, k], tab.at[z, k], zp(d))))
    psib = [go(rcopy(pown.at[z], pg.at[z, k], sib))]
    tsib = [go(rcopy(tab.at[z, k], tab.at[z, k], sib))]

    def rows(c):
        return pl.ds(c * ROWS, ROWS)

    ar, al_, asib = {}, {}, {}

    def start_a(h):
        for c in range(OWN):
            me = ag.at[z, k, h, rows(c)]
            ar[h, c] = go(rcopy(me, me, zp(1)))
            other = ag.at[z, k, h, rows(1 - c)]
            al_[h, 1 - c] = go(rcopy(other, other, zp(3)))
        mine = ag.at[z, k, h]
        asib[h] = [go(rcopy(mine, mine, sib))]

    start_a(0)
    fr, fl = {}, {}

    def forward_a(h):
        left = lax.rem(z + 3, 4)
        right = lax.rem(z + 1, 4)
        ar[h, 0].wait_recv()
        v = ag.at[left, k, h, rows(0)]
        fr[h] = go(rcopy(v, v, zp(1)))
        al_[h, 1].wait_recv()
        v = ag.at[right, k, h, rows(1)]
        fl[h] = go(rcopy(v, v, zp(3)))
        ar[h, 1].wait_recv()
        v = ag.at[left, k, h]
        asib[h].append(go(rcopy(v, v, sib)))
        al_[h, 0].wait_recv()
        v = ag.at[right, k, h]
        asib[h].append(go(rcopy(v, v, sib)))

    def finish_a(h):
        far = lax.rem(z + 2, 4)
        fr[h].wait_recv()
        fl[h].wait_recv()
        v = ag.at[far, k, h]
        asib[h].append(go(rcopy(v, v, sib)))

    def forward_p():
        for i, d in enumerate((1, 2, 3)):
            src = lax.rem(z + 4 - d, 4)
            pz[i].wait_recv()
            tz[i].wait_recv()
            v = pg.at[src, k]
            psib.append(go(rcopy(v, v, sib)))
            t = tab.at[src, k]
            tsib.append(go(rcopy(t, t, sib)))

    def gram():
        halves = [split(pown[m]) for m in range(PANELS)]
        for i, (q, r) in enumerate(BLOCKS):
            gbuf[i * T:(i + 1) * T, :] = dot3(halves[q], halves[r], 0, 0)

    gram()
    gk = pl.multiple_of(k * GHALF, GHALF)
    go_ = pl.multiple_of((1 - k) * GHALF, GHALF)
    g0 = go(rcopy(gbuf.at[pl.ds(go_, GHALF)], grc, sib))
    pack(1)
    g0.wait_recv()

    def add_rows(dst, off, n, srcs):
        step = 160 if n % 160 == 0 else n

        def body(i, carry):
            o = pl.multiple_of(i * step, 8)
            acc = dst[pl.ds(off + o, step), :]
            for s in srcs:
                acc = acc + s[pl.ds(o, step), :]
            dst[pl.ds(off + o, step), :] = acc
            return carry

        lax.fori_loop(0, n // step, body, 0)

    add_rows(gbuf, gk, GHALF, [grc])
    base_a = gk
    base_b = pl.multiple_of(gk + GQ, GQ)
    g1a, g1b = [], []
    for d in (1, 2, 3):
        ox = pl.multiple_of(base_a + lax.rem(x + d, 4) * GC, GC)
        oy = pl.multiple_of(base_b + lax.rem(y + d, 4) * GC, GC)
        g1a.append(go(rcopy(gbuf.at[pl.ds(ox, GC)], ga.at[d - 1], xp(d))))
        g1b.append(go(rcopy(gbuf.at[pl.ds(oy, GC)], gb.at[d - 1], yp(d))))
    forward_p()
    for c in g1a + g1b:
        c.wait_recv()
    my_a = pl.multiple_of(base_a + x * GC, GC)
    my_b = pl.multiple_of(base_b + y * GC, GC)
    gsa[...] = gbuf[pl.ds(my_a, GC), :] + ga[0] + ga[1] + ga[2]
    gsb[...] = gbuf[pl.ds(my_b, GC), :] + gb[0] + gb[1] + gb[2]
    g2a, g2b = [], []
    for d in (1, 2, 3):
        oy = pl.multiple_of(lax.rem(y + d, 4) * GS, GS)
        ox = pl.multiple_of(lax.rem(x + d, 4) * GS, GS)
        g2a.append(go(rcopy(gsa.at[pl.ds(oy, GS)], ga2.at[d - 1], yp(d))))
        g2b.append(go(rcopy(gsb.at[pl.ds(ox, GS)], gb2.at[d - 1], xp(d))))
    forward_a(0)
    for c in g2a + g2b:
        c.wait_recv()
    oya = pl.multiple_of(y * GS, GS)
    oxb = pl.multiple_of(x * GS, GS)
    gza[z] = gsa[pl.ds(oya, GS), :] + ga2[0] + ga2[1] + ga2[2]
    gzb[z] = gsb[pl.ds(oxb, GS), :] + gb2[0] + gb2[1] + gb2[2]
    g3 = []
    for d in (1, 2, 3):
        g3.append(go(rcopy(gza.at[z], gza.at[z], zp(d))))
        g3.append(go(rcopy(gzb.at[z], gzb.at[z], zp(d))))
    start_a(1)
    for c in g3:
        c.wait_recv()
    fa = pl.multiple_of(my_a + y * GS, GS)
    fb = pl.multiple_of(my_b + x * GS, GS)
    gfin_a = gza[0] + gza[1] + gza[2] + gza[3]
    gfin_b = gzb[0] + gzb[1] + gzb[2] + gzb[3]
    cw[pl.ds(fa, GS), :] = gfin_a
    cw[pl.ds(fb, GS), :] = gfin_b
    g4 = []
    for d in (1, 2, 3):
        v = cw.at[pl.ds(fa, GS)]
        g4.append(go(rcopy(v, v, yp(d))))
        v = cw.at[pl.ds(fb, GS)]
        g4.append(go(rcopy(v, v, xp(d))))
    finish_a(0)
    for c in g4:
        c.wait_recv()
    g5 = []
    for d in (1, 2, 3):
        v = cw.at[pl.ds(my_a, GC)]
        g5.append(go(rcopy(v, v, xp(d))))
        v = cw.at[pl.ds(my_b, GC)]
        g5.append(go(rcopy(v, v, yp(d))))

    for c in psib + tsib:
        c.wait_recv()
    tcopy = pltpu.make_async_copy(tab, tab_s, lsem.at[0])
    tcopy.start()
    for i in range(8):
        hi, lo = split(jnp.transpose(pg[i // 2, i % 2]))
        pth[:, i * 128:(i + 1) * 128] = hi
        ptl[:, i * 128:(i + 1) * 128] = lo
    tcopy.wait()
    zero = jnp.zeros((8 * 128, HW), BF)
    agh[REST] = zero
    agl[REST] = zero

    def products(h):
        for c in asib[h]:
            c.wait_recv()

        def conv(i, carry):
            o = pl.multiple_of(i * 128, 128)
            hi, lo = split(ag[i // 2, lax.rem(i, 2), h])
            for t in range(REST):
                agh[t, pl.ds(o, 128), :] = hi[:, t * HW:(t + 1) * HW]
                agl[t, pl.ds(o, 128), :] = lo[:, t * HW:(t + 1) * HW]
            return carry

        lax.fori_loop(0, 8, conv, 0)

        def pair(i, carry):
            for s in range(2):
                slot = (2 * i + s) * 2 + k
                for n in range(16):
                    at = tab_s[n // 4, (n // 2) % 2, n % 2, slot]
                    bh[n * ROWS:(n + 1) * ROWS, s * HW:(s + 1) * HW] = (
                        agh[at, n * ROWS:(n + 1) * ROWS, :])
                    bl[n * ROWS:(n + 1) * ROWS, s * HW:(s + 1) * HW] = (
                        agl[at, n * ROWS:(n + 1) * ROWS, :])
            got = dot3((pth[...], ptl[...]), (bh[...], bl[...]))
            yy = (2 * i) // 4
            xx = lax.rem(2 * i, 4)
            sp[h, yy, xx] = got[:, 0:HW]
            sp[h, yy, xx + 1] = got[:, HW:]
            return carry

        lax.fori_loop(0, 8, pair, 0)

    s1, s2, s3 = {}, {}, {}

    def reduce1(h):
        s1[h] = []
        for d in (1, 2, 3):
            s1[h].append(go(rcopy(
                sp.at[h, :, lax.rem(x + d, 4), pl.ds(0, 128)], ra.at[h, d - 1], xp(d))))
            s1[h].append(go(rcopy(
                sp.at[h, lax.rem(y + d, 4), :, pl.ds(128, 128)], rb.at[h, d - 1], yp(d))))

    def reduce2(h):
        for c in s1[h]:
            c.wait_recv()
        for i in range(4):
            sa[h, i] = sp[h, i, x, 0:128, :] + ra[h, 0, i] + ra[h, 1, i] + ra[h, 2, i]
            sb[h, i] = sp[h, y, i, 128:256, :] + rb[h, 0, i] + rb[h, 1, i] + rb[h, 2, i]
        s2[h] = []
        for d in (1, 2, 3):
            s2[h].append(go(rcopy(sa.at[h, lax.rem(y + d, 4)], ra2.at[h, d - 1], yp(d))))
            s2[h].append(go(rcopy(sb.at[h, lax.rem(x + d, 4)], rb2.at[h, d - 1], xp(d))))

    def gather1(h):
        for c in s2[h]:
            c.wait_recv()
        sfull[z, k, h, 0:128, :] = sa[h, y] + ra2[h, 0] + ra2[h, 1] + ra2[h, 2]
        sfull[z, k, h, 128:256, :] = sb[h, x] + rb2[h, 0] + rb2[h, 1] + rb2[h, 2]
        v = sfull.at[z, k, h]
        s3[h] = [go(rcopy(v, v, zp(d))) for d in (1, 2, 3)]
        s3[h].append(go(rcopy(v, v, sib)))

    def gather2(h):
        for d in (1, 2, 3):
            s3[h][d - 1].wait_recv()
            v = sfull.at[lax.rem(z + 4 - d, 4), k, h]
            s3[h].append(go(rcopy(v, v, sib)))

    rr = lax.broadcasted_iota(jnp.int32, (T, T), 0)
    cc = lax.broadcasted_iota(jnp.int32, (T, T), 1)
    eye = rr == cc
    phi = jnp.where(eye, 0.5, jnp.where(rr > cc, 1.0, 0.0)).astype(F32)
    ident = jnp.where(eye, 1.0, 0.0).astype(F32)
    checks = []
    lengths = []

    def block(q, r):
        i = BLK[q, r]
        return pl.ds(i * T, T)

    def factor(p):
        if p == 0:
            for q in range(PANELS):
                diag = jnp.where(eye, cw[block(q, q), :], 0.0)
                lengths.append(jnp.sum(diag, axis=0, keepdims=True))
        c0 = cw[block(p, p), :]
        diag = jnp.where(eye, c0, 0.0)
        left = jnp.sum(diag, axis=0, keepdims=True)
        dr = lax.rsqrt(left)
        dc = lax.rsqrt(jnp.sum(diag, axis=1, keepdims=True))
        scaled = c0 * dr * dc
        sh, sl = split(scaled)
        n0 = phi * (scaled - ident)
        wref[...] = ident - n0

        def it(i, carry):
            w = split(wref[...])
            t = split(dot3(w, (sh, sl)))
            e = dot3(t, w, 1, 1) - ident
            n = phi * e
            wref[...] = wref[...] - dot3(split(n), w)
            return jnp.sum(e * e, axis=0, keepdims=True)

        err = lax.fori_loop(0, NEWTON - 1, it, jnp.zeros((1, T), F32))
        checks.append(jnp.sum(err) < RESIDUAL)
        checks.append(jnp.min(left - SHARE * lengths[p]) > 0.0)
        w = wref[...] * dr
        hi, lo = split(w)
        wh_ref[p] = hi
        wl_ref[p] = lo
        for r in range(p, PANELS):
            c = split(cw[block(p, r), :])
            u = dot3((hi, lo), c)
            rp[r, p] = u
            if r > p:
                uh, ul = split(jnp.transpose(u))
                uth[BLK[p, r]] = uh
                utl[BLK[p, r]] = ul
        for q in range(p + 1, PANELS):
            for r in range(q, PANELS):
                upd = dot3((uth[BLK[p, q]], utl[BLK[p, q]]), split(rp[r, p]))
                cw[block(q, r), :] = cw[block(q, r), :] - upd
        for r in range(p):
            rp[r, p] = jnp.zeros((T, T), F32)

    def solve(h):
        xs = []
        for p in range(PANELS):
            acc = jnp.concatenate([sfull[p, s, h] for s in range(2)], axis=1)
            for q in range(p):
                acc = acc - dot3((uth[BLK[q, p]], utl[BLK[q, p]]), xs[q])
            got = dot3((wh_ref[p], wl_ref[p]), split(acc))
            if p < PANELS - 1:
                xs.append(split(got))
            for s in range(2):
                slot = col * 2 + s
                which = jnp.int32(0)
                is_panel = jnp.int32(0)
                for m in range(PANELS):
                    hit = owner_ref[m] == slot
                    which = jnp.where(hit, m, which)
                    is_panel = jnp.where(hit, 1, is_panel)
                mask = jnp.full((T, HW), is_panel, jnp.int32) == 1
                at = s * T + h * HW
                out_ref[p * T:(p + 1) * T, at:at + HW] = jnp.where(
                    mask, rp[which, p, :, h * HW:(h + 1) * HW], got[:, s * HW:(s + 1) * HW])

    products(0)
    reduce1(0)
    for c in g5:
        c.wait_recv()
    v = cw.at[pl.ds(gk, GHALF)]
    g6 = go(rcopy(v, v, sib))
    forward_a(1)
    g6.wait_recv()
    for c in g4 + g5 + [g6]:
        c.wait_send()
        left_early.append(id(c))
    factor(0)
    finish_a(1)
    reduce2(0)
    factor(1)
    gather1(0)
    products(1)
    reduce1(1)
    gather2(0)
    factor(2)
    factor(3)
    for c in s3[0][3:]:
        c.wait_recv()
    reduce2(1)
    solve(0)
    gather1(1)
    gather2(1)
    for c in s3[1][3:]:
        c.wait_recv()
    solve(1)
    good = checks[0]
    for c in checks[1:]:
        good = jnp.logical_and(good, c)
    good_ref[0] = good.astype(jnp.int32)
    for c in sends:
        if id(c) not in left_early:
            c.wait_send()


def fast(child_blocks, home_child, col_tiles, tile_owner):
    sem = 120
    vm = pltpu.VMEM
    vmem = pl.BlockSpec(memory_space=pltpu.VMEM)
    smem = pl.BlockSpec(memory_space=pltpu.SMEM)
    return pl.pallas_call(
        kernel,
        out_shape=(
            jax.ShapeDtypeStruct((PANELS * T, 2 * T), F32),
            jax.ShapeDtypeStruct((1,), jnp.int32),
        ),
        in_specs=[smem, smem, smem, vmem],
        out_specs=(vmem, smem),
        scratch_shapes=[
            vm((4, 2, H, OWN * ROWS, REST * HW), F32),
            vm((PANELS, OWN * ROWS, T), F32),
            vm((4, 2, OWN * ROWS, T), F32),
            vm((4, 2, 8, 128), jnp.int32),
            pltpu.SMEM((4, 2, 8, 128), jnp.int32),
            vm((REST + 1, 8 * 128, HW), BF),
            vm((REST + 1, 8 * 128, HW), BF),
            vm((T, 1024), BF),
            vm((T, 1024), BF),
            vm((1024, T), BF),
            vm((1024, T), BF),
            vm((H, 4, 4, T, HW), F32),
            vm((H, 3, 4, 128, HW), F32),
            vm((H, 3, 4, 128, HW), F32),
            vm((H, 4, 128, HW), F32),
            vm((H, 4, 128, HW), F32),
            vm((H, 3, 128, HW), F32),
            vm((H, 3, 128, HW), F32),
            vm((4, 2, H, T, HW), F32),
            vm((GROWS, T), F32),
            vm((GHALF, T), F32),
            vm((3, GC, T), F32),
            vm((3, GC, T), F32),
            vm((GC, T), F32),
            vm((GC, T), F32),
            vm((3, GS, T), F32),
            vm((3, GS, T), F32),
            vm((4, GS, T), F32),
            vm((4, GS, T), F32),
            vm((T, T), F32),
            vm((PANELS, T, T), BF),
            vm((PANELS, T, T), BF),
            vm((GROWS, T), F32),
            vm((len(BLOCKS), T, T), BF),
            vm((len(BLOCKS), T, T), BF),
            vm((PANELS, PANELS, T, T), F32),
            pltpu.SemaphoreType.DMA((sem,)),
            pltpu.SemaphoreType.DMA((sem,)),
            pltpu.SemaphoreType.DMA((1,)),
        ],
        compiler_params=pltpu.CompilerParams(
            collective_id=0, has_side_effects=True, vmem_limit_bytes=60 * 1024 * 1024
        ),
        cost_estimate=pl.CostEstimate(flops=10**10, bytes_accessed=10**7, transcendentals=0),
        name="front",
    )(home_child, col_tiles, tile_owner, child_blocks)


def total(x, axis):
    size = lax.axis_size(axis)
    step = 1
    while step < size:
        x = x + lax.ppermute(x, axis, [(i, i ^ step) for i in range(size)])
        step *= 2
    return x


def gathered(x, axis):
    size = lax.axis_size(axis)
    me = lax.axis_index(axis)
    step = 1
    while step < size:
        other = lax.ppermute(x, axis, [(i, i ^ step) for i in range(size)])
        low = (me // step) % 2 == 0
        x = jnp.concatenate([jnp.where(low, x, other), jnp.where(low, other, x)], axis=0)
        step *= 2
    return x


def broadcast(x, axis, root):
    mine = lax.axis_index(axis) == root
    return total(jnp.where(mine, x, jnp.zeros_like(x)), axis)


def storage_positions(home_child, col_tiles, tile_owner):
    count = col_tiles.shape[0]
    tiles_all = tile_owner.shape[0]
    picked = home_child[:, None] == jnp.arange(count, dtype=jnp.int32)[None, :]
    child_tiles = jnp.sum(jnp.where(picked[:, :, None], col_tiles[None, :, :], 0), axis=1)
    matches = child_tiles[:, :, None] == jnp.arange(tiles_all, dtype=jnp.int32)[None, None, :]
    return jnp.sum(jnp.where(matches, tile_owner[None, None, :], 0), axis=2)


def general(child_blocks, home_child, col_tiles, tile_owner):
    highest = lax.Precision.HIGHEST
    col_count = lax.axis_size("col")
    local_cols = FRONT_COLS // col_count
    held = local_cols // T
    my_col = lax.axis_index("col")
    first_held = my_col * held
    position = storage_positions(home_child, col_tiles, tile_owner)
    piece_blocks = gathered(child_blocks, "col")
    piece_slots = gathered(position, "col")
    count = piece_blocks.shape[0]
    local_tile = piece_slots - first_held
    mine = (local_tile[:, :, None] == jnp.arange(held, dtype=jnp.int32)[None, None, :]).astype(
        jnp.float32
    )
    shaped = piece_blocks.reshape(count, ROWS, CT, T)
    placed = jnp.einsum("nrjc,njk->nrkc", shaped, mine, precision=highest)
    placed = placed.reshape(count * ROWS, local_cols)
    front = placed
    identity = jnp.eye(T, dtype=jnp.float32)
    results = []
    for step in range(PANELS):
        stored_at = tile_owner[step]
        holder = stored_at // held
        offset = (stored_at - holder * held) * T
        is_holder = holder == my_col
        panel = lax.dynamic_slice_in_dim(front, offset, T, 1)
        panel = jnp.where(is_holder, panel, 0.0)
        gram_part = jnp.dot(panel.T, panel, precision=highest, preferred_element_type=jnp.float32)
        gram = total(gram_part, "row")
        gram = gram + jnp.where(is_holder, 0.0, identity)
        lower = jnp.linalg.cholesky(gram)
        basis = jax.scipy.linalg.solve_triangular(lower, panel.T, lower=True).T
        basis = broadcast(basis, "col", holder)
        local_proj = jnp.dot(basis.T, front, precision=highest, preferred_element_type=jnp.float32)
        projected = total(local_proj, "row")
        front = front - jnp.dot(
            basis, projected, precision=highest, preferred_element_type=jnp.float32
        )
        results.append(projected)
    stacked = jnp.concatenate(results, axis=0)
    return stacked


def body(child_blocks, home_child, col_tiles, tile_owner):
    args = (child_blocks, home_child, col_tiles, tile_owner)
    out, good = fast(*args)
    return lax.cond(good[0] == 1, lambda *a: out, general, *args)


def solution(mesh):
    return jax.shard_map(
        body,
        mesh=mesh,
        in_specs=(P(("row", "col"), None, None), P(("row", "col")), P(), P()),
        out_specs=P(None, "col"),
        check_vma=False,
    )
```

```python
import jax
import jax.numpy as jnp
from jax import lax
from jax.experimental import pallas as pl
from jax.experimental.pallas import tpu as pltpu
from jax.sharding import PartitionSpec as P

T = 256
TILES = 32
CT = 12
ROWS = 64
FRONT_COLS = 8192
PANELS = 4
OWN = 2
REST = CT - PANELS
H = 2
HW = T // H
NEWTON = 3
SEM_FIX = 120
RESIDUAL = 8e-5
SHARE = 0.1
F32 = jnp.float32
BF = jnp.bfloat16
MESH = pl.DeviceIdType.MESH
BLOCKS = [(q, r) for q in range(PANELS) for r in range(q, PANELS)]
BLK = {qr: i for i, qr in enumerate(BLOCKS)}
GROWS = len(BLOCKS) * T
GHALF = GROWS // 2
GQ = GHALF // 2
GC = GQ // 4
GS = GC // 4


def split(x):
    hi = x.astype(BF)
    lo = (x - hi.astype(F32)).astype(BF)
    return hi, lo


def dg(a, b, ca, cb):
    return lax.dot_general(a, b, (((ca,), (cb,)), ((), ())), preferred_element_type=F32)


def dot3(a, b, ca=1, cb=0):
    ah, al = a
    bh, bl = b
    return dg(ah, bh, ca, cb) + (dg(ah, bl, ca, cb) + dg(al, bh, ca, cb))


def kernel(
    home_ref, tiles_ref, owner_ref, blocks_ref,
    out_ref, good_ref,
    ag, pown, pg, tab, tab_s, agh, agl, pth, ptl, bh, bl, sp,
    ra, rb, sa, sb, ra2, rb2, sfull,
    gbuf, grc, ga, gb, gsa, gsb, ga2, gb2, gza, gzb,
    wref, wh_ref, wl_ref, cw, uth, utl, rp,
    xsem_s, xsem_r, lsem,
):
    row = lax.axis_index("row")
    col = lax.axis_index("col")
    z = row // 2
    k = row % 2
    y = col // 4
    x = col % 4
    sib = (z * 2 + (1 - k), col)

    def zp(d):
        return (lax.rem(z + d, 4) * 2 + k, col)

    def xp(d):
        return (row, y * 4 + lax.rem(x + d, 4))

    def yp(d):
        return (row, lax.rem(y + d, 4) * 4 + x)

    barrier = pltpu.get_barrier_semaphore()
    partners = [sib] + [f(d) for f in (zp, xp, yp) for d in (1, 2, 3)]
    for dev in partners:
        pl.semaphore_signal(barrier, inc=1, device_id=dev, device_id_type=MESH)

    counter = [0]

    def rcopy(src, dst, dev):
        i = counter[0]
        counter[0] += 1
        return pltpu.make_async_remote_copy(
            src_ref=src, dst_ref=dst, send_sem=xsem_s.at[i], recv_sem=xsem_r.at[i],
            device_id=dev, device_id_type=MESH,
        )

    sends = []
    left_early = []

    def go(copy):
        copy.start()
        sends.append(copy)
        return copy

    lane = lax.broadcasted_iota(jnp.int32, (8, 128), 1)
    sub = lax.broadcasted_iota(jnp.int32, (8, 128), 0)
    table = jnp.full((8, 128), REST, jnp.int32)
    place = []
    for c in range(OWN):
        home = home_ref[c]
        panel_at = [jnp.int32(0)] * PANELS
        rest_at = [jnp.int32(0)] * REST
        count = jnp.int32(0)
        for j in range(CT):
            t = tiles_ref[home, j]
            p = owner_ref[t]
            rest = t >= PANELS
            for m in range(PANELS):
                panel_at[m] = jnp.where(t == m, j, panel_at[m])
            for i in range(min(j + 1, REST)):
                rest_at[i] = jnp.where(jnp.logical_and(rest, count == i), j, rest_at[i])
            table = jnp.where(
                jnp.logical_and(jnp.logical_and(lane == p, sub == c), rest), count, table)
            count = count + rest.astype(jnp.int32)
        place.append((panel_at, rest_at))
    tab[z, k] = table
    for c in range(OWN):
        for m in range(PANELS):
            pown[m, c * ROWS:(c + 1) * ROWS, :] = blocks_ref[c, :, pl.ds(place[c][0][m] * T, T)]

    def pack(h):
        for c in range(OWN):
            for i in range(REST):
                at = place[c][1][i] * T + h * HW
                ag[z, k, h, c * ROWS:(c + 1) * ROWS, i * HW:(i + 1) * HW] = (
                    blocks_ref[c, :, pl.ds(at, HW)])

    pack(0)
    pg[z, k] = pown[z]
    pl.semaphore_wait(barrier, len(partners))

    def rows(c):
        return pl.ds(c * ROWS, ROWS)

    ar, al_, asib = {}, {}, {}

    def start_sib(h):
        mine = ag.at[z, k, h]
        asib[h] = [go(rcopy(mine, mine, sib))]

    def start_near(h, c):
        me = ag.at[z, k, h, rows(c)]
        ar[h, c] = go(rcopy(me, me, zp(1)))
        other = ag.at[z, k, h, rows(1 - c)]
        al_[h, 1 - c] = go(rcopy(other, other, zp(3)))

    fr, fl = {}, {}
    left = lax.rem(z + 3, 4)
    right = lax.rem(z + 1, 4)
    far = lax.rem(z + 2, 4)

    def forward_a(h):
        ar[h, 0].wait_recv()
        v = ag.at[left, k, h, rows(0)]
        fr[h] = go(rcopy(v, v, zp(1)))
        al_[h, 1].wait_recv()
        v = ag.at[right, k, h, rows(1)]
        fl[h] = go(rcopy(v, v, zp(3)))

    def sib_a(h):
        ar[h, 1].wait_recv()
        v = ag.at[left, k, h]
        asib[h].append(go(rcopy(v, v, sib)))
        al_[h, 0].wait_recv()
        v = ag.at[right, k, h]
        asib[h].append(go(rcopy(v, v, sib)))

    def finish_a(h):
        fr[h].wait_recv()
        fl[h].wait_recv()
        v = ag.at[far, k, h]
        asib[h].append(go(rcopy(v, v, sib)))

    start_near(0, 0)
    start_near(0, 1)
    start_sib(0)

    pz, tz = [], []
    for d in (1, 2, 3):
        pz.append(go(rcopy(pown.at[lax.rem(z + d, 4)], pg.at[z, k], zp(d))))
        tz.append(go(rcopy(tab.at[z, k], tab.at[z, k], zp(d))))
    psib = [go(rcopy(pown.at[z], pg.at[z, k], sib))]
    tsib = [go(rcopy(tab.at[z, k], tab.at[z, k], sib))]

    def forward_p():
        for i, d in enumerate((1, 2, 3)):
            src = lax.rem(z + 4 - d, 4)
            pz[i].wait_recv()
            tz[i].wait_recv()
            v = pg.at[src, k]
            psib.append(go(rcopy(v, v, sib)))
            t = tab.at[src, k]
            tsib.append(go(rcopy(t, t, sib)))

    def gram():
        halves = [split(pown[m]) for m in range(PANELS)]
        for i, (q, r) in enumerate(BLOCKS):
            gbuf[i * T:(i + 1) * T, :] = dot3(halves[q], halves[r], 0, 0)

    gram()
    gk = pl.multiple_of(k * GHALF, GHALF)
    go_ = pl.multiple_of((1 - k) * GHALF, GHALF)
    g0 = go(rcopy(gbuf.at[pl.ds(go_, GHALF)], grc, sib))
    pack(1)
    g0.wait_recv()

    def add_rows(dst, off, n, srcs):
        step = 160 if n % 160 == 0 else n

        def body(i, carry):
            o = pl.multiple_of(i * step, 8)
            acc = dst[pl.ds(off + o, step), :]
            for s in srcs:
                acc = acc + s[pl.ds(o, step), :]
            dst[pl.ds(off + o, step), :] = acc
            return carry

        lax.fori_loop(0, n // step, body, 0)

    add_rows(gbuf, gk, GHALF, [grc])
    base_a = gk
    base_b = pl.multiple_of(gk + GQ, GQ)
    g1a, g1b = [], []
    for d in (1, 2, 3):
        ox = pl.multiple_of(base_a + lax.rem(x + d, 4) * GC, GC)
        oy = pl.multiple_of(base_b + lax.rem(y + d, 4) * GC, GC)
        g1a.append(go(rcopy(gbuf.at[pl.ds(ox, GC)], ga.at[d - 1], xp(d))))
        g1b.append(go(rcopy(gbuf.at[pl.ds(oy, GC)], gb.at[d - 1], yp(d))))
    start_sib(1)
    forward_a(0)
    start_near(1, 0)
    for c in g1a + g1b:
        c.wait_recv()
    my_a = pl.multiple_of(base_a + x * GC, GC)
    my_b = pl.multiple_of(base_b + y * GC, GC)
    gsa[...] = gbuf[pl.ds(my_a, GC), :] + ga[0] + ga[1] + ga[2]
    gsb[...] = gbuf[pl.ds(my_b, GC), :] + gb[0] + gb[1] + gb[2]
    g2a, g2b = [], []
    for d in (1, 2, 3):
        oy = pl.multiple_of(lax.rem(y + d, 4) * GS, GS)
        ox = pl.multiple_of(lax.rem(x + d, 4) * GS, GS)
        g2a.append(go(rcopy(gsa.at[pl.ds(oy, GS)], ga2.at[d - 1], yp(d))))
        g2b.append(go(rcopy(gsb.at[pl.ds(ox, GS)], gb2.at[d - 1], xp(d))))
    sib_a(0)
    forward_p()
    for c in g2a + g2b:
        c.wait_recv()
    oya = pl.multiple_of(y * GS, GS)
    oxb = pl.multiple_of(x * GS, GS)
    gza[z] = gsa[pl.ds(oya, GS), :] + ga2[0] + ga2[1] + ga2[2]
    gzb[z] = gsb[pl.ds(oxb, GS), :] + gb2[0] + gb2[1] + gb2[2]
    g3 = []
    for d in (1, 2, 3):
        g3.append(go(rcopy(gza.at[z], gza.at[z], zp(d))))
        g3.append(go(rcopy(gzb.at[z], gzb.at[z], zp(d))))
    start_near(1, 1)
    finish_a(0)

    for c in psib + tsib:
        c.wait_recv()
    tcopy = pltpu.make_async_copy(tab, tab_s, lsem.at[0])
    tcopy.start()
    for i in range(8):
        hi, lo = split(jnp.transpose(pg[i // 2, i % 2]))
        pth[:, i * 128:(i + 1) * 128] = hi
        ptl[:, i * 128:(i + 1) * 128] = lo
    tcopy.wait()
    zero = jnp.zeros((8 * 128, HW), BF)
    agh[REST] = zero
    agl[REST] = zero

    def products(h):
        for c in asib[h]:
            c.wait_recv()

        def conv(i, carry):
            o = pl.multiple_of(i * 128, 128)
            hi, lo = split(ag[i // 2, lax.rem(i, 2), h])
            for t in range(REST):
                agh[t, pl.ds(o, 128), :] = hi[:, t * HW:(t + 1) * HW]
                agl[t, pl.ds(o, 128), :] = lo[:, t * HW:(t + 1) * HW]
            return carry

        lax.fori_loop(0, 8, conv, 0)

        for part in range(2):
            j = x // 2 if part else 1 - x // 2

            def pair(a, carry, part=part, j=j):
                yy = lax.rem(y + a, 4)
                for s in range(2):
                    slot = (yy * 4 + 2 * j + s) * 2 + k
                    for n in range(16):
                        at = tab_s[n // 4, (n // 2) % 2, n % 2, slot]
                        bh[n * ROWS:(n + 1) * ROWS, s * HW:(s + 1) * HW] = (
                            agh[at, n * ROWS:(n + 1) * ROWS, :])
                        bl[n * ROWS:(n + 1) * ROWS, s * HW:(s + 1) * HW] = (
                            agl[at, n * ROWS:(n + 1) * ROWS, :])
                got = dot3((pth[...], ptl[...]), (bh[...], bl[...]))
                sp[h, yy, 2 * j] = got[:, 0:HW]
                sp[h, yy, 2 * j + 1] = got[:, HW:]
                if part:
                    first(h, 2 * j + 1 - lax.rem(x, 2), yy).start()
                else:
                    first(h, 2 * j, yy).start()
                    first(h, 2 * j + 1, yy).start()

                @pl.when(a < 4)
                def _():
                    second(h, yy, j).start()

                return carry

            lax.fori_loop(1, 5, pair, 0)

    base1 = SEM_FIX

    def first(h, px, yy):
        at = base1 + h * 24
        return pltpu.make_async_remote_copy(
            src_ref=sp.at[h, yy, px, pl.ds(0, 128)], dst_ref=ra.at[h, x, yy],
            send_sem=xsem_s.at[at + 4 * px + yy], recv_sem=xsem_r.at[at + 4 * x + yy],
            device_id=(row, y * 4 + px), device_id_type=MESH,
        )

    def first_in(h, px, yy):
        at = base1 + h * 24
        return pltpu.make_async_remote_copy(
            src_ref=sp.at[h, yy, px, pl.ds(0, 128)], dst_ref=ra.at[h, px, yy],
            send_sem=xsem_s.at[at + 4 * px + yy], recv_sem=xsem_r.at[at + 4 * px + yy],
            device_id=(row, y * 4 + px), device_id_type=MESH,
        )

    def second(h, py, j):
        at = base1 + h * 24 + 16
        return pltpu.make_async_remote_copy(
            src_ref=sp.at[h, py, pl.ds(2 * j, 2), pl.ds(128, 128)],
            dst_ref=rb.at[h, y, pl.ds(2 * j, 2)],
            send_sem=xsem_s.at[at + 2 * py + j], recv_sem=xsem_r.at[at + 2 * y + j],
            device_id=(row, py * 4 + x), device_id_type=MESH,
        )

    def second_in(h, py, j):
        at = base1 + h * 24 + 16
        return pltpu.make_async_remote_copy(
            src_ref=sp.at[h, py, pl.ds(2 * j, 2), pl.ds(128, 128)],
            dst_ref=rb.at[h, py, pl.ds(2 * j, 2)],
            send_sem=xsem_s.at[at + 2 * py + j], recv_sem=xsem_r.at[at + 2 * py + j],
            device_id=(row, py * 4 + x), device_id_type=MESH,
        )

    s2, s3 = {}, {}

    def reduce2(h):
        for d in (1, 2, 3):
            for i in range(4):
                first_in(h, lax.rem(x + d, 4), i).wait_recv()
            for j in range(2):
                second_in(h, lax.rem(y + d, 4), j).wait_recv()
        for i in range(4):
            va = sp[h, i, x, 0:128, :]
            vb = sp[h, y, i, 128:256, :]
            for d in (1, 2, 3):
                va = va + ra[h, lax.rem(x + d, 4), i]
                vb = vb + rb[h, lax.rem(y + d, 4), i]
            sa[h, i] = va
            sb[h, i] = vb
        s2[h] = []
        for d in (1, 2, 3):
            s2[h].append(go(rcopy(sa.at[h, lax.rem(y + d, 4)], ra2.at[h, d - 1], yp(d))))
            s2[h].append(go(rcopy(sb.at[h, lax.rem(x + d, 4)], rb2.at[h, d - 1], xp(d))))

    def sent1(h):
        for d in (1, 2, 3):
            for i in range(4):
                first_in(h, lax.rem(x + d, 4), i).wait_send()
            for j in range(2):
                second_in(h, lax.rem(y + d, 4), j).wait_send()

    def gather1(h):
        for c in s2[h]:
            c.wait_recv()
        sfull[z, k, h, 0:128, :] = sa[h, y] + ra2[h, 0] + ra2[h, 1] + ra2[h, 2]
        sfull[z, k, h, 128:256, :] = sb[h, x] + rb2[h, 0] + rb2[h, 1] + rb2[h, 2]
        v = sfull.at[z, k, h]
        s3[h] = [go(rcopy(v, v, zp(d))) for d in (1, 2, 3)]
        s3[h].append(go(rcopy(v, v, sib)))

    def gather2(h):
        for d in (1, 2, 3):
            s3[h][d - 1].wait_recv()
            v = sfull.at[lax.rem(z + 4 - d, 4), k, h]
            s3[h].append(go(rcopy(v, v, sib)))

    rr = lax.broadcasted_iota(jnp.int32, (T, T), 0)
    cc = lax.broadcasted_iota(jnp.int32, (T, T), 1)
    eye = rr == cc
    phi = jnp.where(eye, 0.5, jnp.where(rr > cc, 1.0, 0.0)).astype(F32)
    ident = jnp.where(eye, 1.0, 0.0).astype(F32)
    checks = []
    lengths = []

    def block(q, r):
        i = BLK[q, r]
        return pl.ds(i * T, T)

    def factor(p):
        if p == 0:
            for q in range(PANELS):
                diag = jnp.where(eye, cw[block(q, q), :], 0.0)
                lengths.append(jnp.sum(diag, axis=0, keepdims=True))
        c0 = cw[block(p, p), :]
        diag = jnp.where(eye, c0, 0.0)
        left = jnp.sum(diag, axis=0, keepdims=True)
        dr = lax.rsqrt(left)
        dc = lax.rsqrt(jnp.sum(diag, axis=1, keepdims=True))
        scaled = c0 * dr * dc
        sh, sl = split(scaled)
        n0 = phi * (scaled - ident)
        wref[...] = ident - n0

        def it(i, carry):
            w = split(wref[...])
            t = split(dot3(w, (sh, sl)))
            e = dot3(t, w, 1, 1) - ident
            n = phi * e
            wref[...] = wref[...] - dot3(split(n), w)
            return jnp.sum(e * e, axis=0, keepdims=True)

        err = lax.fori_loop(0, NEWTON - 1, it, jnp.zeros((1, T), F32))
        checks.append(jnp.sum(err) < RESIDUAL)
        checks.append(jnp.min(left - SHARE * lengths[p]) > 0.0)
        w = wref[...] * dr
        hi, lo = split(w)
        wh_ref[p] = hi
        wl_ref[p] = lo
        for r in range(p, PANELS):
            c = split(cw[block(p, r), :])
            u = dot3((hi, lo), c)
            rp[r, p] = u
            if r > p:
                uh, ul = split(jnp.transpose(u))
                uth[BLK[p, r]] = uh
                utl[BLK[p, r]] = ul
        for q in range(p + 1, PANELS):
            for r in range(q, PANELS):
                upd = dot3((uth[BLK[p, q]], utl[BLK[p, q]]), split(rp[r, p]))
                cw[block(q, r), :] = cw[block(q, r), :] - upd
        for r in range(p):
            rp[r, p] = jnp.zeros((T, T), F32)

    def solve(h):
        xs = []
        for p in range(PANELS):
            acc = jnp.concatenate([sfull[p, s, h] for s in range(2)], axis=1)
            for q in range(p):
                acc = acc - dot3((uth[BLK[q, p]], utl[BLK[q, p]]), xs[q])
            got = dot3((wh_ref[p], wl_ref[p]), split(acc))
            if p < PANELS - 1:
                xs.append(split(got))
            for s in range(2):
                slot = col * 2 + s
                which = jnp.int32(0)
                is_panel = jnp.int32(0)
                for m in range(PANELS):
                    hit = owner_ref[m] == slot
                    which = jnp.where(hit, m, which)
                    is_panel = jnp.where(hit, 1, is_panel)
                mask = jnp.full((T, HW), is_panel, jnp.int32) == 1
                at = s * T + h * HW
                out_ref[p * T:(p + 1) * T, at:at + HW] = jnp.where(
                    mask, rp[which, p, :, h * HW:(h + 1) * HW], got[:, s * HW:(s + 1) * HW])

    products(0)
    forward_a(1)
    for c in g3:
        c.wait_recv()
    fa = pl.multiple_of(my_a + y * GS, GS)
    fb = pl.multiple_of(my_b + x * GS, GS)
    gfin_a = gza[0] + gza[1] + gza[2] + gza[3]
    gfin_b = gzb[0] + gzb[1] + gzb[2] + gzb[3]
    cw[pl.ds(fa, GS), :] = gfin_a
    cw[pl.ds(fb, GS), :] = gfin_b
    g4 = []
    for d in (1, 2, 3):
        v = cw.at[pl.ds(fa, GS)]
        g4.append(go(rcopy(v, v, yp(d))))
        v = cw.at[pl.ds(fb, GS)]
        g4.append(go(rcopy(v, v, xp(d))))
    sib_a(1)
    reduce2(0)
    finish_a(1)
    for c in g4:
        c.wait_recv()
    g5 = []
    for d in (1, 2, 3):
        v = cw.at[pl.ds(my_a, GC)]
        g5.append(go(rcopy(v, v, xp(d))))
        v = cw.at[pl.ds(my_b, GC)]
        g5.append(go(rcopy(v, v, yp(d))))
    products(1)
    gather1(0)
    for c in g5:
        c.wait_recv()
    v = cw.at[pl.ds(gk, GHALF)]
    g6 = go(rcopy(v, v, sib))
    gather2(0)
    g6.wait_recv()
    for c in g4 + g5 + [g6]:
        c.wait_send()
        left_early.append(id(c))
    factor(0)
    factor(1)
    reduce2(1)
    factor(2)
    gather1(1)
    factor(3)
    for c in s3[0][3:]:
        c.wait_recv()
    solve(0)
    gather2(1)
    for c in s3[1][3:]:
        c.wait_recv()
    solve(1)
    good = checks[0]
    for c in checks[1:]:
        good = jnp.logical_and(good, c)
    good_ref[0] = good.astype(jnp.int32)
    for c in sends:
        if id(c) not in left_early:
            c.wait_send()
    for h in range(H):
        sent1(h)


def fast(child_blocks, home_child, col_tiles, tile_owner):
    sem = SEM_FIX + 48
    vm = pltpu.VMEM
    vmem = pl.BlockSpec(memory_space=pltpu.VMEM)
    smem = pl.BlockSpec(memory_space=pltpu.SMEM)
    return pl.pallas_call(
        kernel,
        out_shape=(
            jax.ShapeDtypeStruct((PANELS * T, 2 * T), F32),
            jax.ShapeDtypeStruct((1,), jnp.int32),
        ),
        in_specs=[smem, smem, smem, vmem],
        out_specs=(vmem, smem),
        scratch_shapes=[
            vm((4, 2, H, OWN * ROWS, REST * HW), F32),
            vm((PANELS, OWN * ROWS, T), F32),
            vm((4, 2, OWN * ROWS, T), F32),
            vm((4, 2, 8, 128), jnp.int32),
            pltpu.SMEM((4, 2, 8, 128), jnp.int32),
            vm((REST + 1, 8 * 128, HW), BF),
            vm((REST + 1, 8 * 128, HW), BF),
            vm((T, 1024), BF),
            vm((T, 1024), BF),
            vm((1024, T), BF),
            vm((1024, T), BF),
            vm((H, 4, 4, T, HW), F32),
            vm((H, 4, 4, 128, HW), F32),
            vm((H, 4, 4, 128, HW), F32),
            vm((H, 4, 128, HW), F32),
            vm((H, 4, 128, HW), F32),
            vm((H, 3, 128, HW), F32),
            vm((H, 3, 128, HW), F32),
            vm((4, 2, H, T, HW), F32),
            vm((GROWS, T), F32),
            vm((GHALF, T), F32),
            vm((3, GC, T), F32),
            vm((3, GC, T), F32),
            vm((GC, T), F32),
            vm((GC, T), F32),
            vm((3, GS, T), F32),
            vm((3, GS, T), F32),
            vm((4, GS, T), F32),
            vm((4, GS, T), F32),
            vm((T, T), F32),
            vm((PANELS, T, T), BF),
            vm((PANELS, T, T), BF),
            vm((GROWS, T), F32),
            vm((len(BLOCKS), T, T), BF),
            vm((len(BLOCKS), T, T), BF),
            vm((PANELS, PANELS, T, T), F32),
            pltpu.SemaphoreType.DMA((sem,)),
            pltpu.SemaphoreType.DMA((sem,)),
            pltpu.SemaphoreType.DMA((1,)),
        ],
        compiler_params=pltpu.CompilerParams(
            collective_id=0, has_side_effects=True, vmem_limit_bytes=60 * 1024 * 1024
        ),
        cost_estimate=pl.CostEstimate(flops=10**10, bytes_accessed=10**7, transcendentals=0),
        name="front",
    )(home_child, col_tiles, tile_owner, child_blocks)


def total(x, axis):
    size = lax.axis_size(axis)
    step = 1
    while step < size:
        x = x + lax.ppermute(x, axis, [(i, i ^ step) for i in range(size)])
        step *= 2
    return x


def gathered(x, axis):
    size = lax.axis_size(axis)
    me = lax.axis_index(axis)
    step = 1
    while step < size:
        other = lax.ppermute(x, axis, [(i, i ^ step) for i in range(size)])
        low = (me // step) % 2 == 0
        x = jnp.concatenate([jnp.where(low, x, other), jnp.where(low, other, x)], axis=0)
        step *= 2
    return x


def broadcast(x, axis, root):
    mine = lax.axis_index(axis) == root
    return total(jnp.where(mine, x, jnp.zeros_like(x)), axis)


def storage_positions(home_child, col_tiles, tile_owner):
    count = col_tiles.shape[0]
    tiles_all = tile_owner.shape[0]
    picked = home_child[:, None] == jnp.arange(count, dtype=jnp.int32)[None, :]
    child_tiles = jnp.sum(jnp.where(picked[:, :, None], col_tiles[None, :, :], 0), axis=1)
    matches = child_tiles[:, :, None] == jnp.arange(tiles_all, dtype=jnp.int32)[None, None, :]
    return jnp.sum(jnp.where(matches, tile_owner[None, None, :], 0), axis=2)


def general(child_blocks, home_child, col_tiles, tile_owner):
    highest = lax.Precision.HIGHEST
    col_count = lax.axis_size("col")
    local_cols = FRONT_COLS // col_count
    held = local_cols // T
    my_col = lax.axis_index("col")
    first_held = my_col * held
    position = storage_positions(home_child, col_tiles, tile_owner)
    piece_blocks = gathered(child_blocks, "col")
    piece_slots = gathered(position, "col")
    count = piece_blocks.shape[0]
    local_tile = piece_slots - first_held
    mine = (local_tile[:, :, None] == jnp.arange(held, dtype=jnp.int32)[None, None, :]).astype(
        jnp.float32
    )
    shaped = piece_blocks.reshape(count, ROWS, CT, T)
    placed = jnp.einsum("nrjc,njk->nrkc", shaped, mine, precision=highest)
    placed = placed.reshape(count * ROWS, local_cols)
    front = placed
    identity = jnp.eye(T, dtype=jnp.float32)
    results = []
    for step in range(PANELS):
        stored_at = tile_owner[step]
        holder = stored_at // held
        offset = (stored_at - holder * held) * T
        is_holder = holder == my_col
        panel = lax.dynamic_slice_in_dim(front, offset, T, 1)
        panel = jnp.where(is_holder, panel, 0.0)
        gram_part = jnp.dot(panel.T, panel, precision=highest, preferred_element_type=jnp.float32)
        gram = total(gram_part, "row")
        gram = gram + jnp.where(is_holder, 0.0, identity)
        lower = jnp.linalg.cholesky(gram)
        basis = jax.scipy.linalg.solve_triangular(lower, panel.T, lower=True).T
        basis = broadcast(basis, "col", holder)
        local_proj = jnp.dot(basis.T, front, precision=highest, preferred_element_type=jnp.float32)
        projected = total(local_proj, "row")
        front = front - jnp.dot(
            basis, projected, precision=highest, preferred_element_type=jnp.float32
        )
        results.append(projected)
    stacked = jnp.concatenate(results, axis=0)
    return stacked


def body(child_blocks, home_child, col_tiles, tile_owner):
    args = (child_blocks, home_child, col_tiles, tile_owner)
    out, good = fast(*args)
    return lax.cond(good[0] == 1, lambda *a: out, general, *args)


def solution(mesh):
    return jax.shard_map(
        body,
        mesh=mesh,
        in_specs=(P(("row", "col"), None, None), P(("row", "col")), P(), P()),
        out_specs=P(None, "col"),
        check_vma=False,
    )
```

```python
import jax
import jax.numpy as jnp
from jax import lax
from jax.experimental import pallas as pl
from jax.experimental.pallas import tpu as pltpu
from jax.sharding import PartitionSpec as P

T = 256
TILES = 32
CT = 12
ROWS = 64
FRONT_COLS = 8192
PANELS = 4
OWN = 2
REST = CT - PANELS
H = 4
QW = T // H
HW = 2 * QW
NEWTON = 3
SEM_FIX = 140
RESIDUAL = 8e-5
SHARE = 0.1
F32 = jnp.float32
BF = jnp.bfloat16
MESH = pl.DeviceIdType.MESH
BLOCKS = [(q, r) for q in range(PANELS) for r in range(q, PANELS)]
BLK = {qr: i for i, qr in enumerate(BLOCKS)}
GROWS = len(BLOCKS) * T
GHALF = GROWS // 2
GQ = GHALF // 2
GC = GQ // 4
GS = GC // 4


def split(x):
    hi = x.astype(BF)
    lo = (x - hi.astype(F32)).astype(BF)
    return hi, lo


def dg(a, b, ca, cb):
    return lax.dot_general(a, b, (((ca,), (cb,)), ((), ())), preferred_element_type=F32)


def dot3(a, b, ca=1, cb=0):
    ah, al = a
    bh, bl = b
    return dg(ah, bh, ca, cb) + (dg(ah, bl, ca, cb) + dg(al, bh, ca, cb))


def kernel(
    home_ref, tiles_ref, owner_ref, blocks_ref,
    out_ref, good_ref,
    ag, pown, pg, tab, tab_s, agh, agl, pth, ptl, bh, bl, sp,
    ra, rb, sa, sb, ra2, rb2, sfull,
    gbuf, grc, ga, gb, gsa, gsb, ga2, gb2, gza, gzb,
    wref, wh_ref, wl_ref, cw, uth, utl, rp,
    xsem_s, xsem_r, lsem,
):
    row = lax.axis_index("row")
    col = lax.axis_index("col")
    z = row // 2
    k = row % 2
    y = col // 4
    x = col % 4
    sib = (z * 2 + (1 - k), col)

    def zp(d):
        return (lax.rem(z + d, 4) * 2 + k, col)

    def xp(d):
        return (row, y * 4 + lax.rem(x + d, 4))

    def yp(d):
        return (row, lax.rem(y + d, 4) * 4 + x)

    barrier = pltpu.get_barrier_semaphore()
    partners = [sib] + [f(d) for f in (zp, xp, yp) for d in (1, 2, 3)]
    for dev in partners:
        pl.semaphore_signal(barrier, inc=1, device_id=dev, device_id_type=MESH)

    counter = [0]

    def rcopy(src, dst, dev):
        i = counter[0]
        counter[0] += 1
        return pltpu.make_async_remote_copy(
            src_ref=src, dst_ref=dst, send_sem=xsem_s.at[i], recv_sem=xsem_r.at[i],
            device_id=dev, device_id_type=MESH,
        )

    sends = []
    left_early = []

    def go(copy):
        copy.start()
        sends.append(copy)
        return copy

    lane = lax.broadcasted_iota(jnp.int32, (8, 128), 1)
    sub = lax.broadcasted_iota(jnp.int32, (8, 128), 0)
    table = jnp.full((8, 128), REST, jnp.int32)
    place = []
    for c in range(OWN):
        home = home_ref[c]
        panel_at = [jnp.int32(0)] * PANELS
        rest_at = [jnp.int32(0)] * REST
        count = jnp.int32(0)
        for j in range(CT):
            t = tiles_ref[home, j]
            p = owner_ref[t]
            rest = t >= PANELS
            for m in range(PANELS):
                panel_at[m] = jnp.where(t == m, j, panel_at[m])
            for i in range(min(j + 1, REST)):
                rest_at[i] = jnp.where(jnp.logical_and(rest, count == i), j, rest_at[i])
            table = jnp.where(
                jnp.logical_and(jnp.logical_and(lane == p, sub == c), rest), count, table)
            count = count + rest.astype(jnp.int32)
        place.append((panel_at, rest_at))
    tab[z, k] = table
    for c in range(OWN):
        for m in range(PANELS):
            pown[m, c * ROWS:(c + 1) * ROWS, :] = blocks_ref[c, :, pl.ds(place[c][0][m] * T, T)]

    def low(shape):
        return lax.broadcasted_iota(jnp.int32, shape, 1) < QW

    def swap(v):
        return pltpu.roll(v, QW, 1)

    def pack(h):
        for c in range(OWN):
            for i in range(0, REST, 2):
                a, b = (
                    blocks_ref[c, :, pl.ds(place[c][1][i + n] * T + h // 2 * HW, HW)]
                    for n in range(2))
                both = (swap(a), b) if h % 2 else (a, swap(b))
                ag[z, k, h, c * ROWS:(c + 1) * ROWS, i * QW:(i + 2) * QW] = jnp.where(
                    low((ROWS, HW)), *both)

    pack(0)
    pack(1)
    pg[z, k] = pown[z]
    pl.semaphore_wait(barrier, len(partners))

    def rows(c):
        return pl.ds(c * ROWS, ROWS)

    ar, al_, asib = {}, {}, {}

    def start_sib(h):
        mine = ag.at[z, k, h]
        asib[h] = [go(rcopy(mine, mine, sib))]

    def start_near(h, c):
        me = ag.at[z, k, h, rows(c)]
        ar[h, c] = go(rcopy(me, me, zp(1)))
        other = ag.at[z, k, h, rows(1 - c)]
        al_[h, 1 - c] = go(rcopy(other, other, zp(3)))

    fr, fl = {}, {}
    left = lax.rem(z + 3, 4)
    right = lax.rem(z + 1, 4)
    far = lax.rem(z + 2, 4)

    def forward_a(h):
        ar[h, 0].wait_recv()
        v = ag.at[left, k, h, rows(0)]
        fr[h] = go(rcopy(v, v, zp(1)))
        al_[h, 1].wait_recv()
        v = ag.at[right, k, h, rows(1)]
        fl[h] = go(rcopy(v, v, zp(3)))

    def sib_a(h):
        ar[h, 1].wait_recv()
        v = ag.at[left, k, h]
        asib[h].append(go(rcopy(v, v, sib)))
        al_[h, 0].wait_recv()
        v = ag.at[right, k, h]
        asib[h].append(go(rcopy(v, v, sib)))

    def finish_a(h):
        fr[h].wait_recv()
        fl[h].wait_recv()
        v = ag.at[far, k, h]
        asib[h].append(go(rcopy(v, v, sib)))

    pz, tz, psib, tsib = [], [], [], []

    def start_p():
        for d in (1, 2, 3):
            pz.append(go(rcopy(pown.at[lax.rem(z + d, 4)], pg.at[z, k], zp(d))))
            tz.append(go(rcopy(tab.at[z, k], tab.at[z, k], zp(d))))
        psib.append(go(rcopy(pown.at[z], pg.at[z, k], sib)))
        tsib.append(go(rcopy(tab.at[z, k], tab.at[z, k], sib)))

    def forward_p():
        for i, d in enumerate((1, 2, 3)):
            src = lax.rem(z + 4 - d, 4)
            pz[i].wait_recv()
            tz[i].wait_recv()
            v = pg.at[src, k]
            psib.append(go(rcopy(v, v, sib)))
            t = tab.at[src, k]
            tsib.append(go(rcopy(t, t, sib)))

    def gram():
        halves = [split(pown[m]) for m in range(PANELS)]
        for i, (q, r) in enumerate(BLOCKS):
            gbuf[i * T:(i + 1) * T, :] = dot3(halves[q], halves[r], 0, 0)

    gk = pl.multiple_of(k * GHALF, GHALF)
    go_ = pl.multiple_of((1 - k) * GHALF, GHALF)

    def add_rows(dst, off, n, srcs):
        step = 160 if n % 160 == 0 else n

        def body(i, carry):
            o = pl.multiple_of(i * step, 8)
            acc = dst[pl.ds(off + o, step), :]
            for s in srcs:
                acc = acc + s[pl.ds(o, step), :]
            dst[pl.ds(off + o, step), :] = acc
            return carry

        lax.fori_loop(0, n // step, body, 0)

    base_b = pl.multiple_of(gk + GQ, GQ)
    my_a = pl.multiple_of(gk + x * GC, GC)
    my_b = pl.multiple_of(base_b + y * GC, GC)
    fa = pl.multiple_of(my_a + y * GS, GS)
    fb = pl.multiple_of(my_b + x * GS, GS)
    g = {n: [] for n in range(7)}

    def sum0():
        g[0].append(go(rcopy(gbuf.at[pl.ds(go_, GHALF)], grc, sib)))

    def sum1():
        g[0][0].wait_recv()
        add_rows(gbuf, gk, GHALF, [grc])
        for d in (1, 2, 3):
            ox = pl.multiple_of(gk + lax.rem(x + d, 4) * GC, GC)
            oy = pl.multiple_of(base_b + lax.rem(y + d, 4) * GC, GC)
            g[1].append(go(rcopy(gbuf.at[pl.ds(ox, GC)], ga.at[d - 1], xp(d))))
            g[1].append(go(rcopy(gbuf.at[pl.ds(oy, GC)], gb.at[d - 1], yp(d))))

    def sum2():
        for c in g[1]:
            c.wait_recv()
        gsa[...] = gbuf[pl.ds(my_a, GC), :] + ga[0] + ga[1] + ga[2]
        gsb[...] = gbuf[pl.ds(my_b, GC), :] + gb[0] + gb[1] + gb[2]
        for d in (1, 2, 3):
            oy = pl.multiple_of(lax.rem(y + d, 4) * GS, GS)
            ox = pl.multiple_of(lax.rem(x + d, 4) * GS, GS)
            g[2].append(go(rcopy(gsa.at[pl.ds(oy, GS)], ga2.at[d - 1], yp(d))))
            g[2].append(go(rcopy(gsb.at[pl.ds(ox, GS)], gb2.at[d - 1], xp(d))))

    def sum3():
        for c in g[2]:
            c.wait_recv()
        oya = pl.multiple_of(y * GS, GS)
        oxb = pl.multiple_of(x * GS, GS)
        gza[z] = gsa[pl.ds(oya, GS), :] + ga2[0] + ga2[1] + ga2[2]
        gzb[z] = gsb[pl.ds(oxb, GS), :] + gb2[0] + gb2[1] + gb2[2]
        for d in (1, 2, 3):
            g[3].append(go(rcopy(gza.at[z], gza.at[z], zp(d))))
            g[3].append(go(rcopy(gzb.at[z], gzb.at[z], zp(d))))

    def back4():
        for c in g[3]:
            c.wait_recv()
        cw[pl.ds(fa, GS), :] = gza[0] + gza[1] + gza[2] + gza[3]
        cw[pl.ds(fb, GS), :] = gzb[0] + gzb[1] + gzb[2] + gzb[3]
        for d in (1, 2, 3):
            v = cw.at[pl.ds(fa, GS)]
            g[4].append(go(rcopy(v, v, yp(d))))
            v = cw.at[pl.ds(fb, GS)]
            g[4].append(go(rcopy(v, v, xp(d))))

    def back5():
        for c in g[4]:
            c.wait_recv()
        for d in (1, 2, 3):
            v = cw.at[pl.ds(my_a, GC)]
            g[5].append(go(rcopy(v, v, xp(d))))
            v = cw.at[pl.ds(my_b, GC)]
            g[5].append(go(rcopy(v, v, yp(d))))

    def back6():
        for c in g[5]:
            c.wait_recv()
        v = cw.at[pl.ds(gk, GHALF)]
        g[6].append(go(rcopy(v, v, sib)))

    def gram_back():
        g[6][0].wait_recv()
        for c in g[4] + g[5] + g[6]:
            c.wait_send()
            left_early.append(id(c))

    def ready_p():
        for c in psib + tsib:
            c.wait_recv()
        tcopy = pltpu.make_async_copy(tab, tab_s, lsem.at[0])
        tcopy.start()
        for i in range(8):
            hi, lo = split(jnp.transpose(pg[i // 2, i % 2]))
            pth[:, i * 128:(i + 1) * 128] = hi
            ptl[:, i * 128:(i + 1) * 128] = lo
        tcopy.wait()
        zero = jnp.zeros((8 * 128, HW), BF)
        for i in range(2):
            agh[REST + i] = zero
            agl[REST + i] = zero

    def products(h):
        for c in asib[h]:
            c.wait_recv()

        def conv(i, carry):
            o = pl.multiple_of(i * 128, 128)
            for t in range(0, REST, 2):
                v = ag[i // 2, lax.rem(i, 2), h, :, t * QW:(t + 2) * QW]
                for n, w in enumerate((v, swap(v))):
                    hi, lo = split(w)
                    agh[t + n, pl.ds(o, 128), :] = hi
                    agl[t + n, pl.ds(o, 128), :] = lo
            return carry

        lax.fori_loop(0, 8, conv, 0)

        for part in range(2):
            j = x // 2 if part else 1 - x // 2

            def pair(b, carry, part=part, j=j):
                mask = low((ROWS, HW))
                rows_at = [lax.rem(y + 1 + 2 * b + u, 4) for u in range(2)]
                for u in range(2):
                    slot = (rows_at[u] * 4 + 2 * j) * 2 + k
                    for n in range(16):
                        at0 = tab_s[n // 4, (n // 2) % 2, n % 2, slot]
                        at1 = tab_s[n // 4, (n // 2) % 2, n % 2, slot + 2]
                        at1 = at1 + 1 - 2 * lax.rem(at1, 2)
                        rn = slice(n * ROWS, (n + 1) * ROWS)
                        cn = slice(u * HW, (u + 1) * HW)
                        bh[rn, cn] = jnp.where(mask, agh[at0, rn, :], agh[at1, rn, :])
                        bl[rn, cn] = jnp.where(mask, agl[at0, rn, :], agl[at1, rn, :])
                got = dot3((pth[...], ptl[...]), (bh[...], bl[...]))
                half = low((128, HW))
                for u in range(2):
                    top = got[0:128, u * HW:(u + 1) * HW]
                    bottom = got[128:256, u * HW:(u + 1) * HW]
                    yy = rows_at[u]
                    sp[h, yy, 2 * j] = jnp.where(half, top, swap(bottom))
                    sp[h, yy, 2 * j + 1] = jnp.where(half, swap(top), bottom)
                for u in range(2):
                    yy = rows_at[u]
                    if part:
                        first(h, 2 * j + 1 - lax.rem(x, 2), yy).start()
                    else:
                        first(h, 2 * j, yy).start()
                        first(h, 2 * j + 1, yy).start()
                second(h, rows_at[0], j).start()

                @pl.when(b == 0)
                def _():
                    second(h, rows_at[1], j).start()

                return carry

            lax.fori_loop(0, 2, pair, 0)

    base1 = SEM_FIX

    def first(h, px, yy):
        at = base1 + h * 24
        return pltpu.make_async_remote_copy(
            src_ref=sp.at[h, yy, px, pl.ds(0, 64)], dst_ref=ra.at[h, x, yy],
            send_sem=xsem_s.at[at + 4 * px + yy], recv_sem=xsem_r.at[at + 4 * x + yy],
            device_id=(row, y * 4 + px), device_id_type=MESH,
        )

    def first_in(h, px, yy):
        at = base1 + h * 24
        return pltpu.make_async_remote_copy(
            src_ref=sp.at[h, yy, px, pl.ds(0, 64)], dst_ref=ra.at[h, px, yy],
            send_sem=xsem_s.at[at + 4 * px + yy], recv_sem=xsem_r.at[at + 4 * px + yy],
            device_id=(row, y * 4 + px), device_id_type=MESH,
        )

    def second(h, py, j):
        at = base1 + h * 24 + 16
        return pltpu.make_async_remote_copy(
            src_ref=sp.at[h, py, pl.ds(2 * j, 2), pl.ds(64, 64)],
            dst_ref=rb.at[h, y, pl.ds(2 * j, 2)],
            send_sem=xsem_s.at[at + 2 * py + j], recv_sem=xsem_r.at[at + 2 * y + j],
            device_id=(row, py * 4 + x), device_id_type=MESH,
        )

    def second_in(h, py, j):
        at = base1 + h * 24 + 16
        return pltpu.make_async_remote_copy(
            src_ref=sp.at[h, py, pl.ds(2 * j, 2), pl.ds(64, 64)],
            dst_ref=rb.at[h, py, pl.ds(2 * j, 2)],
            send_sem=xsem_s.at[at + 2 * py + j], recv_sem=xsem_r.at[at + 2 * py + j],
            device_id=(row, py * 4 + x), device_id_type=MESH,
        )

    s2, s3 = {}, {}

    def reduce2(h):
        for d in (1, 2, 3):
            for i in range(4):
                first_in(h, lax.rem(x + d, 4), i).wait_recv()
            for j in range(2):
                second_in(h, lax.rem(y + d, 4), j).wait_recv()
        for i in range(4):
            va = sp[h, i, x, 0:64, :]
            vb = sp[h, y, i, 64:128, :]
            for d in (1, 2, 3):
                va = va + ra[h, lax.rem(x + d, 4), i]
                vb = vb + rb[h, lax.rem(y + d, 4), i]
            sa[h, i] = va
            sb[h, i] = vb
        s2[h] = []
        for d in (1, 2, 3):
            s2[h].append(go(rcopy(sa.at[h, lax.rem(y + d, 4)], ra2.at[h, d - 1], yp(d))))
            s2[h].append(go(rcopy(sb.at[h, lax.rem(x + d, 4)], rb2.at[h, d - 1], xp(d))))

    def sent1(h):
        for d in (1, 2, 3):
            for i in range(4):
                first_in(h, lax.rem(x + d, 4), i).wait_send()
            for j in range(2):
                second_in(h, lax.rem(y + d, 4), j).wait_send()

    def gather1(h):
        for c in s2[h]:
            c.wait_recv()
        sfull[z, k, h, 0:64, :] = sa[h, y] + ra2[h, 0] + ra2[h, 1] + ra2[h, 2]
        sfull[z, k, h, 64:128, :] = sb[h, x] + rb2[h, 0] + rb2[h, 1] + rb2[h, 2]
        v = sfull.at[z, k, h]
        s3[h] = [go(rcopy(v, v, zp(d))) for d in (1, 2, 3)]
        s3[h].append(go(rcopy(v, v, sib)))

    def gather2(h):
        for d in (1, 2, 3):
            s3[h][d - 1].wait_recv()
            v = sfull.at[lax.rem(z + 4 - d, 4), k, h]
            s3[h].append(go(rcopy(v, v, sib)))

    rr = lax.broadcasted_iota(jnp.int32, (T, T), 0)
    cc = lax.broadcasted_iota(jnp.int32, (T, T), 1)
    eye = rr == cc
    phi = jnp.where(eye, 0.5, jnp.where(rr > cc, 1.0, 0.0)).astype(F32)
    ident = jnp.where(eye, 1.0, 0.0).astype(F32)
    checks = []
    lengths = []

    def block(q, r):
        i = BLK[q, r]
        return pl.ds(i * T, T)

    def factor(p):
        if p == 0:
            for q in range(PANELS):
                diag = jnp.where(eye, cw[block(q, q), :], 0.0)
                lengths.append(jnp.sum(diag, axis=0, keepdims=True))
        c0 = cw[block(p, p), :]
        diag = jnp.where(eye, c0, 0.0)
        left = jnp.sum(diag, axis=0, keepdims=True)
        dr = lax.rsqrt(left)
        dc = lax.rsqrt(jnp.sum(diag, axis=1, keepdims=True))
        scaled = c0 * dr * dc
        sh, sl = split(scaled)
        n0 = phi * (scaled - ident)
        wref[...] = ident - n0

        def it(i, carry):
            w = split(wref[...])
            t = split(dot3(w, (sh, sl)))
            e = dot3(t, w, 1, 1) - ident
            n = phi * e
            wref[...] = wref[...] - dot3(split(n), w)
            return jnp.sum(e * e, axis=0, keepdims=True)

        err = lax.fori_loop(0, NEWTON - 1, it, jnp.zeros((1, T), F32))
        checks.append(jnp.sum(err) < RESIDUAL)
        checks.append(jnp.min(left - SHARE * lengths[p]) > 0.0)
        w = wref[...] * dr
        hi, lo = split(w)
        wh_ref[p] = hi
        wl_ref[p] = lo
        for r in range(p, PANELS):
            c = split(cw[block(p, r), :])
            u = dot3((hi, lo), c)
            rp[r, p] = u
            if r > p:
                uh, ul = split(jnp.transpose(u))
                uth[BLK[p, r]] = uh
                utl[BLK[p, r]] = ul
        for q in range(p + 1, PANELS):
            for r in range(q, PANELS):
                upd = dot3((uth[BLK[p, q]], utl[BLK[p, q]]), split(rp[r, p]))
                cw[block(q, r), :] = cw[block(q, r), :] - upd
        for r in range(p):
            rp[r, p] = jnp.zeros((T, T), F32)

    def solve(g):
        xs = []
        half = low((128, HW))
        for p in range(PANELS):
            cols = []
            for s in range(2):
                a, b = sfull[p, s, 2 * g], sfull[p, s, 2 * g + 1]
                cols.append(jnp.concatenate(
                    [jnp.where(half, a, swap(b)), jnp.where(half, swap(a), b)], axis=0))
            acc = jnp.concatenate(cols, axis=1)
            for q in range(p):
                acc = acc - dot3((uth[BLK[q, p]], utl[BLK[q, p]]), xs[q])
            got = dot3((wh_ref[p], wl_ref[p]), split(acc))
            if p < PANELS - 1:
                xs.append(split(got))
            for s in range(2):
                slot = col * 2 + s
                which = jnp.int32(0)
                is_panel = jnp.int32(0)
                for m in range(PANELS):
                    hit = owner_ref[m] == slot
                    which = jnp.where(hit, m, which)
                    is_panel = jnp.where(hit, 1, is_panel)
                mask = jnp.full((T, HW), is_panel, jnp.int32) == 1
                at = s * T + g * HW
                out_ref[p * T:(p + 1) * T, at:at + HW] = jnp.where(
                    mask, rp[which, p, :, g * HW:(g + 1) * HW], got[:, s * HW:(s + 1) * HW])

    def solved(g):
        for h in (2 * g, 2 * g + 1):
            for c in s3[h][3:]:
                c.wait_recv()
        solve(g)

    start_p()
    start_near(0, 0)
    gram()
    sum0()
    start_near(0, 1)
    sum1()
    start_near(1, 0)
    start_near(1, 1)
    start_sib(1)
    start_sib(0)
    forward_a(0)
    forward_p()
    pack(2)
    pack(3)
    start_sib(3)
    forward_a(1)
    start_near(3, 0)
    sum2()
    sib_a(1)
    sib_a(0)
    finish_a(0)
    sum3()
    ready_p()
    products(0)
    start_near(2, 0)
    start_near(2, 1)
    start_near(3, 1)
    finish_a(1)
    back4()
    products(1)
    forward_a(2)
    reduce2(0)
    forward_a(3)
    start_sib(2)
    back5()
    sib_a(2)
    reduce2(1)
    sib_a(3)
    finish_a(2)
    finish_a(3)
    products(2)
    gather1(0)
    back6()
    products(3)
    gather1(1)
    gram_back()
    factor(0)
    reduce2(2)
    factor(1)
    reduce2(3)
    gather2(1)
    gather1(2)
    factor(2)
    gather2(0)
    gather1(3)
    factor(3)
    solved(0)
    gather2(2)
    gather2(3)
    solved(1)
    good = checks[0]
    for c in checks[1:]:
        good = jnp.logical_and(good, c)
    good_ref[0] = good.astype(jnp.int32)
    for c in sends:
        if id(c) not in left_early:
            c.wait_send()
    for h in range(H):
        sent1(h)


def fast(child_blocks, home_child, col_tiles, tile_owner):
    sem = SEM_FIX + 24 * H
    vm = pltpu.VMEM
    vmem = pl.BlockSpec(memory_space=pltpu.VMEM)
    smem = pl.BlockSpec(memory_space=pltpu.SMEM)
    return pl.pallas_call(
        kernel,
        out_shape=(
            jax.ShapeDtypeStruct((PANELS * T, 2 * T), F32),
            jax.ShapeDtypeStruct((1,), jnp.int32),
        ),
        in_specs=[smem, smem, smem, vmem],
        out_specs=(vmem, smem),
        scratch_shapes=[
            vm((4, 2, H, OWN * ROWS, REST * QW), F32),
            vm((PANELS, OWN * ROWS, T), F32),
            vm((4, 2, OWN * ROWS, T), F32),
            vm((4, 2, 8, 128), jnp.int32),
            pltpu.SMEM((4, 2, 8, 128), jnp.int32),
            vm((REST + 2, 8 * 128, HW), BF),
            vm((REST + 2, 8 * 128, HW), BF),
            vm((T, 1024), BF),
            vm((T, 1024), BF),
            vm((1024, T), BF),
            vm((1024, T), BF),
            vm((H, 4, 4, 128, HW), F32),
            vm((H, 4, 4, 64, HW), F32),
            vm((H, 4, 4, 64, HW), F32),
            vm((H, 4, 64, HW), F32),
            vm((H, 4, 64, HW), F32),
            vm((H, 3, 64, HW), F32),
            vm((H, 3, 64, HW), F32),
            vm((4, 2, H, 128, HW), F32),
            vm((GROWS, T), F32),
            vm((GHALF, T), F32),
            vm((3, GC, T), F32),
            vm((3, GC, T), F32),
            vm((GC, T), F32),
            vm((GC, T), F32),
            vm((3, GS, T), F32),
            vm((3, GS, T), F32),
            vm((4, GS, T), F32),
            vm((4, GS, T), F32),
            vm((T, T), F32),
            vm((PANELS, T, T), BF),
            vm((PANELS, T, T), BF),
            vm((GROWS, T), F32),
            vm((len(BLOCKS), T, T), BF),
            vm((len(BLOCKS), T, T), BF),
            vm((PANELS, PANELS, T, T), F32),
            pltpu.SemaphoreType.DMA((sem,)),
            pltpu.SemaphoreType.DMA((sem,)),
            pltpu.SemaphoreType.DMA((1,)),
        ],
        compiler_params=pltpu.CompilerParams(
            collective_id=0, has_side_effects=True, vmem_limit_bytes=60 * 1024 * 1024
        ),
        cost_estimate=pl.CostEstimate(flops=10**10, bytes_accessed=10**7, transcendentals=0),
        name="front",
    )(home_child, col_tiles, tile_owner, child_blocks)


def total(x, axis):
    size = lax.axis_size(axis)
    step = 1
    while step < size:
        x = x + lax.ppermute(x, axis, [(i, i ^ step) for i in range(size)])
        step *= 2
    return x


def gathered(x, axis):
    size = lax.axis_size(axis)
    me = lax.axis_index(axis)
    step = 1
    while step < size:
        other = lax.ppermute(x, axis, [(i, i ^ step) for i in range(size)])
        low = (me // step) % 2 == 0
        x = jnp.concatenate([jnp.where(low, x, other), jnp.where(low, other, x)], axis=0)
        step *= 2
    return x


def broadcast(x, axis, root):
    mine = lax.axis_index(axis) == root
    return total(jnp.where(mine, x, jnp.zeros_like(x)), axis)


def storage_positions(home_child, col_tiles, tile_owner):
    count = col_tiles.shape[0]
    tiles_all = tile_owner.shape[0]
    picked = home_child[:, None] == jnp.arange(count, dtype=jnp.int32)[None, :]
    child_tiles = jnp.sum(jnp.where(picked[:, :, None], col_tiles[None, :, :], 0), axis=1)
    matches = child_tiles[:, :, None] == jnp.arange(tiles_all, dtype=jnp.int32)[None, None, :]
    return jnp.sum(jnp.where(matches, tile_owner[None, None, :], 0), axis=2)


def general(child_blocks, home_child, col_tiles, tile_owner):
    highest = lax.Precision.HIGHEST
    col_count = lax.axis_size("col")
    local_cols = FRONT_COLS // col_count
    held = local_cols // T
    my_col = lax.axis_index("col")
    first_held = my_col * held
    position = storage_positions(home_child, col_tiles, tile_owner)
    piece_blocks = gathered(child_blocks, "col")
    piece_slots = gathered(position, "col")
    count = piece_blocks.shape[0]
    local_tile = piece_slots - first_held
    mine = (local_tile[:, :, None] == jnp.arange(held, dtype=jnp.int32)[None, None, :]).astype(
        jnp.float32
    )
    shaped = piece_blocks.reshape(count, ROWS, CT, T)
    placed = jnp.einsum("nrjc,njk->nrkc", shaped, mine, precision=highest)
    placed = placed.reshape(count * ROWS, local_cols)
    front = placed
    identity = jnp.eye(T, dtype=jnp.float32)
    results = []
    for step in range(PANELS):
        stored_at = tile_owner[step]
        holder = stored_at // held
        offset = (stored_at - holder * held) * T
        is_holder = holder == my_col
        panel = lax.dynamic_slice_in_dim(front, offset, T, 1)
        panel = jnp.where(is_holder, panel, 0.0)
        gram_part = jnp.dot(panel.T, panel, precision=highest, preferred_element_type=jnp.float32)
        gram = total(gram_part, "row")
        gram = gram + jnp.where(is_holder, 0.0, identity)
        lower = jnp.linalg.cholesky(gram)
        basis = jax.scipy.linalg.solve_triangular(lower, panel.T, lower=True).T
        basis = broadcast(basis, "col", holder)
        local_proj = jnp.dot(basis.T, front, precision=highest, preferred_element_type=jnp.float32)
        projected = total(local_proj, "row")
        front = front - jnp.dot(
            basis, projected, precision=highest, preferred_element_type=jnp.float32
        )
        results.append(projected)
    stacked = jnp.concatenate(results, axis=0)
    return stacked


def body(child_blocks, home_child, col_tiles, tile_owner):
    args = (child_blocks, home_child, col_tiles, tile_owner)
    out, good = fast(*args)
    return lax.cond(good[0] == 1, lambda *a: out, general, *args)


def solution(mesh):
    return jax.shard_map(
        body,
        mesh=mesh,
        in_specs=(P(("row", "col"), None, None), P(("row", "col")), P(), P()),
        out_specs=P(None, "col"),
        check_vma=False,
    )
```

```python
import jax
import jax.numpy as jnp
from jax import lax
from jax.experimental import pallas as pl
from jax.experimental.pallas import tpu as pltpu
from jax.sharding import PartitionSpec as P

T = 256
TILES = 32
CT = 12
ROWS = 64
FRONT_COLS = 8192
PANELS = 4
OWN = 2
REST = CT - PANELS
H = 4
QW = T // H
HW = 2 * QW
NEWTON = 3
SEM_FIX = 140
RESIDUAL = 8e-5
SHARE = 0.1
F32 = jnp.float32
BF = jnp.bfloat16
MESH = pl.DeviceIdType.MESH
BLOCKS = [(q, r) for q in range(PANELS) for r in range(q, PANELS)]
BLK = {qr: i for i, qr in enumerate(BLOCKS)}
GROWS = len(BLOCKS) * T
GHALF = GROWS // 2
GQ = GHALF // 2
GC = GQ // 4
GS = GC // 4


def split(x):
    hi = x.astype(BF)
    lo = (x - hi.astype(F32)).astype(BF)
    return hi, lo


def dg(a, b, ca, cb):
    return lax.dot_general(a, b, (((ca,), (cb,)), ((), ())), preferred_element_type=F32)


def dot3(a, b, ca=1, cb=0):
    ah, al = a
    bh, bl = b
    return dg(ah, bh, ca, cb) + (dg(ah, bl, ca, cb) + dg(al, bh, ca, cb))


def kernel(
    home_ref, tiles_ref, owner_ref, blocks_ref,
    out_ref, good_ref,
    ag, pown, pg, tab, tab_s, agh, agl, pth, ptl, bh, bl, sp,
    ra, rb, sa, sb, ra2, rb2, sfull,
    gbuf, grc, ga, gb, gsa, gsb, ga2, gb2, gza, gzb,
    wref, wh_ref, wl_ref, cw, uth, utl, rp,
    xsem_s, xsem_r, lsem,
):
    row = lax.axis_index("row")
    col = lax.axis_index("col")
    z = row // 2
    k = row % 2
    y = col // 4
    x = col % 4
    sib = (z * 2 + (1 - k), col)

    def zp(d):
        return (lax.rem(z + d, 4) * 2 + k, col)

    def xp(d):
        return (row, y * 4 + lax.rem(x + d, 4))

    def yp(d):
        return (row, lax.rem(y + d, 4) * 4 + x)

    barrier = pltpu.get_barrier_semaphore()
    partners = [sib] + [f(d) for f in (zp, xp, yp) for d in (1, 2, 3)]
    for dev in partners:
        pl.semaphore_signal(barrier, inc=1, device_id=dev, device_id_type=MESH)

    counter = [0]

    def rcopy(src, dst, dev):
        i = counter[0]
        counter[0] += 1
        return pltpu.make_async_remote_copy(
            src_ref=src, dst_ref=dst, send_sem=xsem_s.at[i], recv_sem=xsem_r.at[i],
            device_id=dev, device_id_type=MESH,
        )

    sends = []
    left_early = []

    def go(copy):
        copy.start()
        sends.append(copy)
        return copy

    lane = lax.broadcasted_iota(jnp.int32, (8, 128), 1)
    sub = lax.broadcasted_iota(jnp.int32, (8, 128), 0)
    table = jnp.full((8, 128), REST, jnp.int32)
    place = []
    for c in range(OWN):
        home = home_ref[c]
        panel_at = [jnp.int32(0)] * PANELS
        rest_at = [jnp.int32(0)] * REST
        count = jnp.int32(0)
        for j in range(CT):
            t = tiles_ref[j, home]
            p = owner_ref[t]
            rest = t >= PANELS
            for m in range(PANELS):
                panel_at[m] = jnp.where(t == m, j, panel_at[m])
            for i in range(min(j + 1, REST)):
                rest_at[i] = jnp.where(jnp.logical_and(rest, count == i), j, rest_at[i])
            table = jnp.where(
                jnp.logical_and(jnp.logical_and(lane == p, sub == c), rest), count, table)
            count = count + rest.astype(jnp.int32)
        place.append((panel_at, rest_at))
    tab[z, k] = table
    for c in range(OWN):
        for m in range(PANELS):
            pown[m, c * ROWS:(c + 1) * ROWS, :] = blocks_ref[c, :, pl.ds(place[c][0][m] * T, T)]

    def low(shape):
        return lax.broadcasted_iota(jnp.int32, shape, 1) < QW

    def swap(v):
        return pltpu.roll(v, QW, 1)

    def pack(h):
        for c in range(OWN):
            for i in range(0, REST, 2):
                a, b = (
                    blocks_ref[c, :, pl.ds(place[c][1][i + n] * T + h // 2 * HW, HW)]
                    for n in range(2))
                both = (swap(a), b) if h % 2 else (a, swap(b))
                ag[z, k, h, c * ROWS:(c + 1) * ROWS, i * QW:(i + 2) * QW] = jnp.where(
                    low((ROWS, HW)), *both)

    pack(0)
    pack(1)
    pg[z, k] = pown[z]
    pl.semaphore_wait(barrier, len(partners))

    def rows(c):
        return pl.ds(c * ROWS, ROWS)

    ar, al_, asib = {}, {}, {}

    def start_sib(h):
        mine = ag.at[z, k, h]
        asib[h] = [go(rcopy(mine, mine, sib))]

    def start_near(h, c):
        me = ag.at[z, k, h, rows(c)]
        ar[h, c] = go(rcopy(me, me, zp(1)))
        other = ag.at[z, k, h, rows(1 - c)]
        al_[h, 1 - c] = go(rcopy(other, other, zp(3)))

    fr, fl = {}, {}
    left = lax.rem(z + 3, 4)
    right = lax.rem(z + 1, 4)
    far = lax.rem(z + 2, 4)

    def forward_a(h):
        ar[h, 0].wait_recv()
        v = ag.at[left, k, h, rows(0)]
        fr[h] = go(rcopy(v, v, zp(1)))
        al_[h, 1].wait_recv()
        v = ag.at[right, k, h, rows(1)]
        fl[h] = go(rcopy(v, v, zp(3)))

    def sib_a(h):
        ar[h, 1].wait_recv()
        v = ag.at[left, k, h]
        asib[h].append(go(rcopy(v, v, sib)))
        al_[h, 0].wait_recv()
        v = ag.at[right, k, h]
        asib[h].append(go(rcopy(v, v, sib)))

    def finish_a(h):
        fr[h].wait_recv()
        fl[h].wait_recv()
        v = ag.at[far, k, h]
        asib[h].append(go(rcopy(v, v, sib)))

    pz, tz, psib, tsib = [], [], [], []

    def start_p():
        for d in (1, 2, 3):
            pz.append(go(rcopy(pown.at[lax.rem(z + d, 4)], pg.at[z, k], zp(d))))
            tz.append(go(rcopy(tab.at[z, k], tab.at[z, k], zp(d))))
        psib.append(go(rcopy(pown.at[z], pg.at[z, k], sib)))
        tsib.append(go(rcopy(tab.at[z, k], tab.at[z, k], sib)))

    def forward_p():
        for i, d in enumerate((1, 2, 3)):
            src = lax.rem(z + 4 - d, 4)
            pz[i].wait_recv()
            tz[i].wait_recv()
            v = pg.at[src, k]
            psib.append(go(rcopy(v, v, sib)))
            t = tab.at[src, k]
            tsib.append(go(rcopy(t, t, sib)))

    def gram():
        halves = [split(pown[m]) for m in range(PANELS)]
        for i, (q, r) in enumerate(BLOCKS):
            gbuf[i * T:(i + 1) * T, :] = dot3(halves[q], halves[r], 0, 0)

    gk = pl.multiple_of(k * GHALF, GHALF)
    go_ = pl.multiple_of((1 - k) * GHALF, GHALF)

    def add_rows(dst, off, n, srcs):
        step = 160 if n % 160 == 0 else n

        def body(i, carry):
            o = pl.multiple_of(i * step, 8)
            acc = dst[pl.ds(off + o, step), :]
            for s in srcs:
                acc = acc + s[pl.ds(o, step), :]
            dst[pl.ds(off + o, step), :] = acc
            return carry

        lax.fori_loop(0, n // step, body, 0)

    base_b = pl.multiple_of(gk + GQ, GQ)
    my_a = pl.multiple_of(gk + x * GC, GC)
    my_b = pl.multiple_of(base_b + y * GC, GC)
    fa = pl.multiple_of(my_a + y * GS, GS)
    fb = pl.multiple_of(my_b + x * GS, GS)
    g = {n: [] for n in range(7)}

    def sum0():
        g[0].append(go(rcopy(gbuf.at[pl.ds(go_, GHALF)], grc, sib)))

    def sum1():
        g[0][0].wait_recv()
        add_rows(gbuf, gk, GHALF, [grc])
        for d in (1, 2, 3):
            ox = pl.multiple_of(gk + lax.rem(x + d, 4) * GC, GC)
            oy = pl.multiple_of(base_b + lax.rem(y + d, 4) * GC, GC)
            g[1].append(go(rcopy(gbuf.at[pl.ds(ox, GC)], ga.at[d - 1], xp(d))))
            g[1].append(go(rcopy(gbuf.at[pl.ds(oy, GC)], gb.at[d - 1], yp(d))))

    def sum2():
        for c in g[1]:
            c.wait_recv()
        gsa[...] = gbuf[pl.ds(my_a, GC), :] + ga[0] + ga[1] + ga[2]
        gsb[...] = gbuf[pl.ds(my_b, GC), :] + gb[0] + gb[1] + gb[2]
        for d in (1, 2, 3):
            oy = pl.multiple_of(lax.rem(y + d, 4) * GS, GS)
            ox = pl.multiple_of(lax.rem(x + d, 4) * GS, GS)
            g[2].append(go(rcopy(gsa.at[pl.ds(oy, GS)], ga2.at[d - 1], yp(d))))
            g[2].append(go(rcopy(gsb.at[pl.ds(ox, GS)], gb2.at[d - 1], xp(d))))

    def sum3():
        for c in g[2]:
            c.wait_recv()
        oya = pl.multiple_of(y * GS, GS)
        oxb = pl.multiple_of(x * GS, GS)
        gza[z] = gsa[pl.ds(oya, GS), :] + ga2[0] + ga2[1] + ga2[2]
        gzb[z] = gsb[pl.ds(oxb, GS), :] + gb2[0] + gb2[1] + gb2[2]
        for d in (1, 2, 3):
            g[3].append(go(rcopy(gza.at[z], gza.at[z], zp(d))))
            g[3].append(go(rcopy(gzb.at[z], gzb.at[z], zp(d))))

    def back4():
        for c in g[3]:
            c.wait_recv()
        cw[pl.ds(fa, GS), :] = gza[0] + gza[1] + gza[2] + gza[3]
        cw[pl.ds(fb, GS), :] = gzb[0] + gzb[1] + gzb[2] + gzb[3]
        for d in (1, 2, 3):
            v = cw.at[pl.ds(fa, GS)]
            g[4].append(go(rcopy(v, v, yp(d))))
            v = cw.at[pl.ds(fb, GS)]
            g[4].append(go(rcopy(v, v, xp(d))))

    def back5():
        for c in g[4]:
            c.wait_recv()
        for d in (1, 2, 3):
            v = cw.at[pl.ds(my_a, GC)]
            g[5].append(go(rcopy(v, v, xp(d))))
            v = cw.at[pl.ds(my_b, GC)]
            g[5].append(go(rcopy(v, v, yp(d))))

    def back6():
        for c in g[5]:
            c.wait_recv()
        v = cw.at[pl.ds(gk, GHALF)]
        g[6].append(go(rcopy(v, v, sib)))

    def gram_back():
        g[6][0].wait_recv()
        for c in g[4] + g[5] + g[6]:
            c.wait_send()
            left_early.append(id(c))

    def ready_p():
        for c in psib + tsib:
            c.wait_recv()
        tcopy = pltpu.make_async_copy(tab, tab_s, lsem.at[0])
        tcopy.start()
        for i in range(8):
            hi, lo = split(jnp.transpose(pg[i // 2, i % 2]))
            pth[:, i * 128:(i + 1) * 128] = hi
            ptl[:, i * 128:(i + 1) * 128] = lo
        tcopy.wait()
        zero = jnp.zeros((8 * 128, HW), BF)
        for i in range(2):
            agh[REST + i] = zero
            agl[REST + i] = zero

    def convert(h):
        for c in asib[h]:
            c.wait_recv()

        def conv(i, carry):
            o = pl.multiple_of(i * 128, 128)
            for t in range(0, REST, 2):
                v = ag[i // 2, lax.rem(i, 2), h, :, t * QW:(t + 2) * QW]
                for n, w in enumerate((v, swap(v))):
                    hi, lo = split(w)
                    agh[t + n, pl.ds(o, 128), :] = hi
                    agl[t + n, pl.ds(o, 128), :] = lo
            return carry

        lax.fori_loop(0, 8, conv, 0)

    def products(h, part):
        if part == 0:
            convert(h)
        j = x // 2 if part else 1 - x // 2

        def pair(b, carry):
            mask = low((ROWS, HW))
            rows_at = [lax.rem(y + 1 + 2 * b + u, 4) for u in range(2)]
            for u in range(2):
                slot = (rows_at[u] * 4 + 2 * j) * 2 + k
                for n in range(16):
                    at0 = tab_s[n // 4, (n // 2) % 2, n % 2, slot]
                    at1 = tab_s[n // 4, (n // 2) % 2, n % 2, slot + 2]
                    at1 = at1 + 1 - 2 * lax.rem(at1, 2)
                    rn = slice(n * ROWS, (n + 1) * ROWS)
                    cn = slice(u * HW, (u + 1) * HW)
                    bh[rn, cn] = jnp.where(mask, agh[at0, rn, :], agh[at1, rn, :])
                    bl[rn, cn] = jnp.where(mask, agl[at0, rn, :], agl[at1, rn, :])
            got = dot3((pth[...], ptl[...]), (bh[...], bl[...]))
            half = low((128, HW))
            for u in range(2):
                top = got[0:128, u * HW:(u + 1) * HW]
                bottom = got[128:256, u * HW:(u + 1) * HW]
                yy = rows_at[u]
                sp[h, yy, 2 * j] = jnp.where(half, top, swap(bottom))
                sp[h, yy, 2 * j + 1] = jnp.where(half, swap(top), bottom)
            for u in range(2):
                yy = rows_at[u]
                if part:
                    first(h, 2 * j + 1 - lax.rem(x, 2), yy).start()
                else:
                    first(h, 2 * j, yy).start()
                    first(h, 2 * j + 1, yy).start()
            second(h, rows_at[0], j).start()

            @pl.when(b == 0)
            def _():
                second(h, rows_at[1], j).start()

            return carry

        lax.fori_loop(0, 2, pair, 0)

    base1 = SEM_FIX

    def first(h, px, yy):
        at = base1 + h * 24
        return pltpu.make_async_remote_copy(
            src_ref=sp.at[h, yy, px, pl.ds(0, 64)], dst_ref=ra.at[h, x, yy],
            send_sem=xsem_s.at[at + 4 * px + yy], recv_sem=xsem_r.at[at + 4 * x + yy],
            device_id=(row, y * 4 + px), device_id_type=MESH,
        )

    def first_in(h, px, yy):
        at = base1 + h * 24
        return pltpu.make_async_remote_copy(
            src_ref=sp.at[h, yy, px, pl.ds(0, 64)], dst_ref=ra.at[h, px, yy],
            send_sem=xsem_s.at[at + 4 * px + yy], recv_sem=xsem_r.at[at + 4 * px + yy],
            device_id=(row, y * 4 + px), device_id_type=MESH,
        )

    def second(h, py, j):
        at = base1 + h * 24 + 16
        return pltpu.make_async_remote_copy(
            src_ref=sp.at[h, py, pl.ds(2 * j, 2), pl.ds(64, 64)],
            dst_ref=rb.at[h, y, pl.ds(2 * j, 2)],
            send_sem=xsem_s.at[at + 2 * py + j], recv_sem=xsem_r.at[at + 2 * y + j],
            device_id=(row, py * 4 + x), device_id_type=MESH,
        )

    def second_in(h, py, j):
        at = base1 + h * 24 + 16
        return pltpu.make_async_remote_copy(
            src_ref=sp.at[h, py, pl.ds(2 * j, 2), pl.ds(64, 64)],
            dst_ref=rb.at[h, py, pl.ds(2 * j, 2)],
            send_sem=xsem_s.at[at + 2 * py + j], recv_sem=xsem_r.at[at + 2 * py + j],
            device_id=(row, py * 4 + x), device_id_type=MESH,
        )

    s2, s3 = {}, {}

    def reduce2(h):
        for d in (1, 2, 3):
            for i in range(4):
                first_in(h, lax.rem(x + d, 4), i).wait_recv()
            for j in range(2):
                second_in(h, lax.rem(y + d, 4), j).wait_recv()
        for i in range(4):
            va = sp[h, i, x, 0:64, :]
            vb = sp[h, y, i, 64:128, :]
            for d in (1, 2, 3):
                va = va + ra[h, lax.rem(x + d, 4), i]
                vb = vb + rb[h, lax.rem(y + d, 4), i]
            sa[h, i] = va
            sb[h, i] = vb
        s2[h] = []
        for d in (1, 2, 3):
            s2[h].append(go(rcopy(sa.at[h, lax.rem(y + d, 4)], ra2.at[h, d - 1], yp(d))))
            s2[h].append(go(rcopy(sb.at[h, lax.rem(x + d, 4)], rb2.at[h, d - 1], xp(d))))

    def sent1(h):
        for d in (1, 2, 3):
            for i in range(4):
                first_in(h, lax.rem(x + d, 4), i).wait_send()
            for j in range(2):
                second_in(h, lax.rem(y + d, 4), j).wait_send()

    def gather1(h):
        for c in s2[h]:
            c.wait_recv()
        sfull[z, k, h, 0:64, :] = sa[h, y] + ra2[h, 0] + ra2[h, 1] + ra2[h, 2]
        sfull[z, k, h, 64:128, :] = sb[h, x] + rb2[h, 0] + rb2[h, 1] + rb2[h, 2]
        v = sfull.at[z, k, h]
        s3[h] = [go(rcopy(v, v, zp(d))) for d in (1, 2, 3)]
        s3[h].append(go(rcopy(v, v, sib)))

    def gather2(h):
        for d in (1, 2, 3):
            s3[h][d - 1].wait_recv()
            v = sfull.at[lax.rem(z + 4 - d, 4), k, h]
            s3[h].append(go(rcopy(v, v, sib)))

    rr = lax.broadcasted_iota(jnp.int32, (T, T), 0)
    cc = lax.broadcasted_iota(jnp.int32, (T, T), 1)
    eye = rr == cc
    phi = jnp.where(eye, 0.5, jnp.where(rr > cc, 1.0, 0.0)).astype(F32)
    ident = jnp.where(eye, 1.0, 0.0).astype(F32)
    checks = []
    lengths = []

    def block(q, r):
        i = BLK[q, r]
        return pl.ds(i * T, T)

    def factor(p):
        if p == 0:
            for q in range(PANELS):
                diag = jnp.where(eye, cw[block(q, q), :], 0.0)
                lengths.append(jnp.sum(diag, axis=0, keepdims=True))
        c0 = cw[block(p, p), :]
        diag = jnp.where(eye, c0, 0.0)
        left = jnp.sum(diag, axis=0, keepdims=True)
        dr = lax.rsqrt(left)
        dc = lax.rsqrt(jnp.sum(diag, axis=1, keepdims=True))
        scaled = c0 * dr * dc
        sh, sl = split(scaled)
        n0 = phi * (scaled - ident)
        wref[...] = ident - n0

        def it(i, carry):
            w = split(wref[...])
            t = split(dot3(w, (sh, sl)))
            e = dot3(t, w, 1, 1) - ident
            n = phi * e
            wref[...] = wref[...] - dot3(split(n), w)
            return jnp.sum(e * e, axis=0, keepdims=True)

        err = lax.fori_loop(0, NEWTON - 1, it, jnp.zeros((1, T), F32))
        checks.append(jnp.sum(err) < RESIDUAL)
        checks.append(jnp.min(left - SHARE * lengths[p]) > 0.0)
        w = wref[...] * dr
        hi, lo = split(w)
        wh_ref[p] = hi
        wl_ref[p] = lo
        for r in range(p, PANELS):
            c = split(cw[block(p, r), :])
            u = dot3((hi, lo), c)
            rp[r, p] = u
            if r > p:
                uh, ul = split(jnp.transpose(u))
                uth[BLK[p, r]] = uh
                utl[BLK[p, r]] = ul
        for q in range(p + 1, PANELS):
            for r in range(q, PANELS):
                upd = dot3((uth[BLK[p, q]], utl[BLK[p, q]]), split(rp[r, p]))
                cw[block(q, r), :] = cw[block(q, r), :] - upd
        for r in range(p):
            rp[r, p] = jnp.zeros((T, T), F32)

    def solve(g):
        xs = []
        half = low((128, HW))
        for p in range(PANELS):
            cols = []
            for s in range(2):
                a, b = sfull[p, s, 2 * g], sfull[p, s, 2 * g + 1]
                cols.append(jnp.concatenate(
                    [jnp.where(half, a, swap(b)), jnp.where(half, swap(a), b)], axis=0))
            acc = jnp.concatenate(cols, axis=1)
            for q in range(p):
                acc = acc - dot3((uth[BLK[q, p]], utl[BLK[q, p]]), xs[q])
            got = dot3((wh_ref[p], wl_ref[p]), split(acc))
            if p < PANELS - 1:
                xs.append(split(got))
            for s in range(2):
                slot = col * 2 + s
                which = jnp.int32(0)
                is_panel = jnp.int32(0)
                for m in range(PANELS):
                    hit = owner_ref[m] == slot
                    which = jnp.where(hit, m, which)
                    is_panel = jnp.where(hit, 1, is_panel)
                mask = jnp.full((T, HW), is_panel, jnp.int32) == 1
                at = s * T + g * HW
                out_ref[p * T:(p + 1) * T, at:at + HW] = jnp.where(
                    mask, rp[which, p, :, g * HW:(g + 1) * HW], got[:, s * HW:(s + 1) * HW])

    def solved(g):
        for h in (2 * g, 2 * g + 1):
            for c in s3[h][3:]:
                c.wait_recv()
        solve(g)

    start_near(0, 0)
    start_sib(1)
    start_p()
    gram()
    start_sib(0)
    sum0()
    start_near(1, 0)
    start_near(0, 1)
    pack(3)
    forward_a(0)
    sum1()
    pack(2)
    start_near(1, 1)
    forward_p()
    forward_a(1)
    start_sib(2)
    start_near(2, 0)
    start_near(3, 0)
    sum2()
    sib_a(0)
    finish_a(0)
    ready_p()
    products(0, 0)
    sib_a(1)
    products(0, 1)
    finish_a(1)
    sum3()
    start_near(2, 1)
    products(1, 0)
    start_sib(3)
    products(1, 1)
    back4()
    forward_a(2)
    reduce2(0)
    start_near(3, 1)
    reduce2(1)
    back5()
    forward_a(3)
    sib_a(2)
    finish_a(2)
    sib_a(3)
    products(2, 0)
    finish_a(3)
    products(2, 1)
    products(3, 0)
    gather1(0)
    back6()
    products(3, 1)
    gram_back()
    factor(0)
    gather1(1)
    reduce2(2)
    factor(1)
    reduce2(3)
    gather2(0)
    gather1(2)
    factor(2)
    gather2(1)
    gather1(3)
    factor(3)
    solved(0)
    gather2(2)
    gather2(3)
    solved(1)
    good = checks[0]
    for c in checks[1:]:
        good = jnp.logical_and(good, c)
    good_ref[0] = good.astype(jnp.int32)
    for c in sends:
        if id(c) not in left_early:
            c.wait_send()
    for h in range(H):
        sent1(h)


def fast(child_blocks, home_child, col_tiles, tile_owner):
    sem = SEM_FIX + 24 * H
    vm = pltpu.VMEM
    vmem = pl.BlockSpec(memory_space=pltpu.VMEM)
    smem = pl.BlockSpec(memory_space=pltpu.SMEM)
    return pl.pallas_call(
        kernel,
        out_shape=(
            jax.ShapeDtypeStruct((PANELS * T, 2 * T), F32),
            jax.ShapeDtypeStruct((1,), jnp.int32),
        ),
        in_specs=[smem, smem, smem, vmem],
        out_specs=(vmem, smem),
        scratch_shapes=[
            vm((4, 2, H, OWN * ROWS, REST * QW), F32),
            vm((PANELS, OWN * ROWS, T), F32),
            vm((4, 2, OWN * ROWS, T), F32),
            vm((4, 2, 8, 128), jnp.int32),
            pltpu.SMEM((4, 2, 8, 128), jnp.int32),
            vm((REST + 2, 8 * 128, HW), BF),
            vm((REST + 2, 8 * 128, HW), BF),
            vm((T, 1024), BF),
            vm((T, 1024), BF),
            vm((1024, T), BF),
            vm((1024, T), BF),
            vm((H, 4, 4, 128, HW), F32),
            vm((H, 4, 4, 64, HW), F32),
            vm((H, 4, 4, 64, HW), F32),
            vm((H, 4, 64, HW), F32),
            vm((H, 4, 64, HW), F32),
            vm((H, 3, 64, HW), F32),
            vm((H, 3, 64, HW), F32),
            vm((4, 2, H, 128, HW), F32),
            vm((GROWS, T), F32),
            vm((GHALF, T), F32),
            vm((3, GC, T), F32),
            vm((3, GC, T), F32),
            vm((GC, T), F32),
            vm((GC, T), F32),
            vm((3, GS, T), F32),
            vm((3, GS, T), F32),
            vm((4, GS, T), F32),
            vm((4, GS, T), F32),
            vm((T, T), F32),
            vm((PANELS, T, T), BF),
            vm((PANELS, T, T), BF),
            vm((GROWS, T), F32),
            vm((len(BLOCKS), T, T), BF),
            vm((len(BLOCKS), T, T), BF),
            vm((PANELS, PANELS, T, T), F32),
            pltpu.SemaphoreType.DMA((sem,)),
            pltpu.SemaphoreType.DMA((sem,)),
            pltpu.SemaphoreType.DMA((1,)),
        ],
        compiler_params=pltpu.CompilerParams(
            collective_id=0, has_side_effects=True, vmem_limit_bytes=60 * 1024 * 1024
        ),
        cost_estimate=pl.CostEstimate(flops=10**10, bytes_accessed=10**7, transcendentals=0),
        name="front",
    )(home_child, col_tiles.T, tile_owner, child_blocks)


def total(x, axis):
    size = lax.axis_size(axis)
    step = 1
    while step < size:
        x = x + lax.ppermute(x, axis, [(i, i ^ step) for i in range(size)])
        step *= 2
    return x


def gathered(x, axis):
    size = lax.axis_size(axis)
    me = lax.axis_index(axis)
    step = 1
    while step < size:
        other = lax.ppermute(x, axis, [(i, i ^ step) for i in range(size)])
        low = (me // step) % 2 == 0
        x = jnp.concatenate([jnp.where(low, x, other), jnp.where(low, other, x)], axis=0)
        step *= 2
    return x


def broadcast(x, axis, root):
    mine = lax.axis_index(axis) == root
    return total(jnp.where(mine, x, jnp.zeros_like(x)), axis)


def storage_positions(home_child, col_tiles, tile_owner):
    count = col_tiles.shape[0]
    tiles_all = tile_owner.shape[0]
    picked = home_child[:, None] == jnp.arange(count, dtype=jnp.int32)[None, :]
    child_tiles = jnp.sum(jnp.where(picked[:, :, None], col_tiles[None, :, :], 0), axis=1)
    matches = child_tiles[:, :, None] == jnp.arange(tiles_all, dtype=jnp.int32)[None, None, :]
    return jnp.sum(jnp.where(matches, tile_owner[None, None, :], 0), axis=2)


def general(child_blocks, home_child, col_tiles, tile_owner):
    highest = lax.Precision.HIGHEST
    col_count = lax.axis_size("col")
    local_cols = FRONT_COLS // col_count
    held = local_cols // T
    my_col = lax.axis_index("col")
    first_held = my_col * held
    position = storage_positions(home_child, col_tiles, tile_owner)
    piece_blocks = gathered(child_blocks, "col")
    piece_slots = gathered(position, "col")
    count = piece_blocks.shape[0]
    local_tile = piece_slots - first_held
    mine = (local_tile[:, :, None] == jnp.arange(held, dtype=jnp.int32)[None, None, :]).astype(
        jnp.float32
    )
    shaped = piece_blocks.reshape(count, ROWS, CT, T)
    placed = jnp.einsum("nrjc,njk->nrkc", shaped, mine, precision=highest)
    placed = placed.reshape(count * ROWS, local_cols)
    front = placed
    identity = jnp.eye(T, dtype=jnp.float32)
    results = []
    for step in range(PANELS):
        stored_at = tile_owner[step]
        holder = stored_at // held
        offset = (stored_at - holder * held) * T
        is_holder = holder == my_col
        panel = lax.dynamic_slice_in_dim(front, offset, T, 1)
        panel = jnp.where(is_holder, panel, 0.0)
        gram_part = jnp.dot(panel.T, panel, precision=highest, preferred_element_type=jnp.float32)
        gram = total(gram_part, "row")
        gram = gram + jnp.where(is_holder, 0.0, identity)
        lower = jnp.linalg.cholesky(gram)
        basis = jax.scipy.linalg.solve_triangular(lower, panel.T, lower=True).T
        basis = broadcast(basis, "col", holder)
        local_proj = jnp.dot(basis.T, front, precision=highest, preferred_element_type=jnp.float32)
        projected = total(local_proj, "row")
        front = front - jnp.dot(
            basis, projected, precision=highest, preferred_element_type=jnp.float32
        )
        results.append(projected)
    stacked = jnp.concatenate(results, axis=0)
    return stacked


def body(child_blocks, home_child, col_tiles, tile_owner):
    args = (child_blocks, home_child, col_tiles, tile_owner)
    out, good = fast(*args)
    return lax.cond(good[0] == 1, lambda *a: out, general, *args)


def solution(mesh):
    return jax.shard_map(
        body,
        mesh=mesh,
        in_specs=(P(("row", "col"), None, None), P(("row", "col")), P(), P()),
        out_specs=P(None, "col"),
        check_vma=False,
    )
```

```python
import jax
import jax.numpy as jnp
from jax import lax
from jax.experimental import pallas as pl
from jax.experimental.pallas import tpu as pltpu
from jax.sharding import PartitionSpec as P

T = 256
TILES = 32
CT = 12
ROWS = 64
FRONT_COLS = 8192
PANELS = 4
OWN = 2
REST = CT - PANELS
H = 4
QW = T // H
HW = 2 * QW
NEWTON = 3
SEM_FIX = 140
RESIDUAL = 8e-5
SHARE = 0.1
F32 = jnp.float32
BF = jnp.bfloat16
MESH = pl.DeviceIdType.MESH
BLOCKS = [(q, r) for q in range(PANELS) for r in range(q, PANELS)]
BLK = {qr: i for i, qr in enumerate(BLOCKS)}
GROWS = len(BLOCKS) * T
GHALF = GROWS // 2
GQ = GHALF // 2
GC = GQ // 4
GS = GC // 4


def split(x):
    hi = x.astype(BF)
    lo = (x - hi.astype(F32)).astype(BF)
    return hi, lo


def dg(a, b, ca, cb):
    return lax.dot_general(a, b, (((ca,), (cb,)), ((), ())), preferred_element_type=F32)


def dot3(a, b, ca=1, cb=0):
    ah, al = a
    bh, bl = b
    return dg(ah, bh, ca, cb) + (dg(ah, bl, ca, cb) + dg(al, bh, ca, cb))


def kernel(
    home_ref, tiles_ref, owner_ref, blocks_ref,
    out_ref, good_ref,
    ag, pown, pg, tab, tab_s, agh, agl, pth, ptl, bh, bl, sp,
    ra, rb, sa, sb, ra2, rb2, sfull,
    gbuf, grc, ga, gb, gsa, gsb, ga2, gb2, gza, gzb,
    wref, wh_ref, wl_ref, cw, uth, utl, rp,
    xsem_s, xsem_r, lsem,
):
    row = lax.axis_index("row")
    col = lax.axis_index("col")
    z = row // 2
    k = row % 2
    y = col // 4
    x = col % 4
    sib = (z * 2 + (1 - k), col)

    def zp(d):
        return (lax.rem(z + d, 4) * 2 + k, col)

    def xp(d):
        return (row, y * 4 + lax.rem(x + d, 4))

    def yp(d):
        return (row, lax.rem(y + d, 4) * 4 + x)

    barrier = pltpu.get_barrier_semaphore()
    partners = [sib] + [f(d) for f in (zp, xp, yp) for d in (1, 2, 3)]
    for dev in partners:
        pl.semaphore_signal(barrier, inc=1, device_id=dev, device_id_type=MESH)

    counter = [0]

    def rcopy(src, dst, dev):
        i = counter[0]
        counter[0] += 1
        return pltpu.make_async_remote_copy(
            src_ref=src, dst_ref=dst, send_sem=xsem_s.at[i], recv_sem=xsem_r.at[i],
            device_id=dev, device_id_type=MESH,
        )

    sends = []
    left_early = []

    def go(copy):
        copy.start()
        sends.append(copy)
        return copy

    lane = lax.broadcasted_iota(jnp.int32, (8, 128), 1)
    sub = lax.broadcasted_iota(jnp.int32, (8, 128), 0)
    table = jnp.full((8, 128), REST, jnp.int32)
    place = []
    for c in range(OWN):
        home = home_ref[c]
        panel_at = [jnp.int32(0)] * PANELS
        rest_at = [jnp.int32(0)] * REST
        count = jnp.int32(0)
        for j in range(CT):
            t = tiles_ref[j, home]
            p = owner_ref[t]
            rest = t >= PANELS
            for m in range(PANELS):
                panel_at[m] = jnp.where(t == m, j, panel_at[m])
            for i in range(min(j + 1, REST)):
                rest_at[i] = jnp.where(jnp.logical_and(rest, count == i), j, rest_at[i])
            table = jnp.where(
                jnp.logical_and(jnp.logical_and(lane == p, sub == c), rest), count, table)
            count = count + rest.astype(jnp.int32)
        place.append((panel_at, rest_at))
    tab[z, k] = table
    for c in range(OWN):
        for m in range(PANELS):
            pown[m, c * ROWS:(c + 1) * ROWS, :] = blocks_ref[c, :, pl.ds(place[c][0][m] * T, T)]

    def low(shape):
        return lax.broadcasted_iota(jnp.int32, shape, 1) < QW

    def swap(v):
        return pltpu.roll(v, QW, 1)

    def pack(h):
        for c in range(OWN):
            for i in range(0, REST, 2):
                a, b = (
                    blocks_ref[c, :, pl.ds(place[c][1][i + n] * T + h // 2 * HW, HW)]
                    for n in range(2))
                both = (swap(a), b) if h % 2 else (a, swap(b))
                ag[z, k, h, c * ROWS:(c + 1) * ROWS, i * QW:(i + 2) * QW] = jnp.where(
                    low((ROWS, HW)), *both)

    pack(0)
    pack(1)
    pg[z, k] = pown[z]
    pl.semaphore_wait(barrier, len(partners))

    def rows(c):
        return pl.ds(c * ROWS, ROWS)

    ar, al_, asib = {}, {}, {}

    def start_sib(h):
        mine = ag.at[z, k, h]
        asib[h] = [go(rcopy(mine, mine, sib))]

    def start_near(h, c):
        me = ag.at[z, k, h, rows(c)]
        ar[h, c] = go(rcopy(me, me, zp(1)))
        other = ag.at[z, k, h, rows(1 - c)]
        al_[h, 1 - c] = go(rcopy(other, other, zp(3)))

    fr, fl = {}, {}
    left = lax.rem(z + 3, 4)
    right = lax.rem(z + 1, 4)
    far = lax.rem(z + 2, 4)

    def forward_a(h):
        ar[h, 0].wait_recv()
        v = ag.at[left, k, h, rows(0)]
        fr[h] = go(rcopy(v, v, zp(1)))
        al_[h, 1].wait_recv()
        v = ag.at[right, k, h, rows(1)]
        fl[h] = go(rcopy(v, v, zp(3)))

    def sib_a(h):
        ar[h, 1].wait_recv()
        v = ag.at[left, k, h]
        asib[h].append(go(rcopy(v, v, sib)))
        al_[h, 0].wait_recv()
        v = ag.at[right, k, h]
        asib[h].append(go(rcopy(v, v, sib)))

    def finish_a(h):
        fr[h].wait_recv()
        fl[h].wait_recv()
        v = ag.at[far, k, h]
        asib[h].append(go(rcopy(v, v, sib)))

    pz, tz, psib, tsib = [], [], [], []

    def start_p():
        for d in (1, 2, 3):
            pz.append(go(rcopy(pown.at[lax.rem(z + d, 4)], pg.at[z, k], zp(d))))
            tz.append(go(rcopy(tab.at[z, k], tab.at[z, k], zp(d))))
        psib.append(go(rcopy(pown.at[z], pg.at[z, k], sib)))
        tsib.append(go(rcopy(tab.at[z, k], tab.at[z, k], sib)))

    def forward_p():
        for i, d in enumerate((1, 2, 3)):
            src = lax.rem(z + 4 - d, 4)
            pz[i].wait_recv()
            tz[i].wait_recv()
            v = pg.at[src, k]
            psib.append(go(rcopy(v, v, sib)))
            t = tab.at[src, k]
            tsib.append(go(rcopy(t, t, sib)))

    def gram():
        halves = [split(pown[m]) for m in range(PANELS)]
        for i, (q, r) in enumerate(BLOCKS):
            gbuf[i * T:(i + 1) * T, :] = dot3(halves[q], halves[r], 0, 0)

    gk = pl.multiple_of(k * GHALF, GHALF)
    go_ = pl.multiple_of((1 - k) * GHALF, GHALF)

    def add_rows(dst, off, n, srcs):
        step = 160 if n % 160 == 0 else n

        def body(i, carry):
            o = pl.multiple_of(i * step, 8)
            acc = dst[pl.ds(off + o, step), :]
            for s in srcs:
                acc = acc + s[pl.ds(o, step), :]
            dst[pl.ds(off + o, step), :] = acc
            return carry

        lax.fori_loop(0, n // step, body, 0)

    base_b = pl.multiple_of(gk + GQ, GQ)
    my_a = pl.multiple_of(gk + x * GC, GC)
    my_b = pl.multiple_of(base_b + y * GC, GC)
    fa = pl.multiple_of(my_a + y * GS, GS)
    fb = pl.multiple_of(my_b + x * GS, GS)
    g = {n: [] for n in range(7)}

    def sum0():
        g[0].append(go(rcopy(gbuf.at[pl.ds(go_, GHALF)], grc, sib)))

    def sum1():
        g[0][0].wait_recv()
        add_rows(gbuf, gk, GHALF, [grc])
        for d in (1, 2, 3):
            ox = pl.multiple_of(gk + lax.rem(x + d, 4) * GC, GC)
            oy = pl.multiple_of(base_b + lax.rem(y + d, 4) * GC, GC)
            g[1].append(go(rcopy(gbuf.at[pl.ds(ox, GC)], ga.at[d - 1], xp(d))))
            g[1].append(go(rcopy(gbuf.at[pl.ds(oy, GC)], gb.at[d - 1], yp(d))))

    def sum2():
        for c in g[1]:
            c.wait_recv()
        gsa[...] = gbuf[pl.ds(my_a, GC), :] + ga[0] + ga[1] + ga[2]
        gsb[...] = gbuf[pl.ds(my_b, GC), :] + gb[0] + gb[1] + gb[2]
        for d in (1, 2, 3):
            oy = pl.multiple_of(lax.rem(y + d, 4) * GS, GS)
            ox = pl.multiple_of(lax.rem(x + d, 4) * GS, GS)
            g[2].append(go(rcopy(gsa.at[pl.ds(oy, GS)], ga2.at[d - 1], yp(d))))
            g[2].append(go(rcopy(gsb.at[pl.ds(ox, GS)], gb2.at[d - 1], xp(d))))

    def sum3():
        for c in g[2]:
            c.wait_recv()
        oya = pl.multiple_of(y * GS, GS)
        oxb = pl.multiple_of(x * GS, GS)
        gza[z] = gsa[pl.ds(oya, GS), :] + ga2[0] + ga2[1] + ga2[2]
        gzb[z] = gsb[pl.ds(oxb, GS), :] + gb2[0] + gb2[1] + gb2[2]
        for d in (1, 2, 3):
            g[3].append(go(rcopy(gza.at[z], gza.at[z], zp(d))))
            g[3].append(go(rcopy(gzb.at[z], gzb.at[z], zp(d))))

    def back4():
        for c in g[3]:
            c.wait_recv()
        cw[pl.ds(fa, GS), :] = gza[0] + gza[1] + gza[2] + gza[3]
        cw[pl.ds(fb, GS), :] = gzb[0] + gzb[1] + gzb[2] + gzb[3]
        for d in (1, 2, 3):
            v = cw.at[pl.ds(fa, GS)]
            g[4].append(go(rcopy(v, v, yp(d))))
            v = cw.at[pl.ds(fb, GS)]
            g[4].append(go(rcopy(v, v, xp(d))))

    def back5():
        for c in g[4]:
            c.wait_recv()
        for d in (1, 2, 3):
            v = cw.at[pl.ds(my_a, GC)]
            g[5].append(go(rcopy(v, v, xp(d))))
            v = cw.at[pl.ds(my_b, GC)]
            g[5].append(go(rcopy(v, v, yp(d))))

    def back6():
        for c in g[5]:
            c.wait_recv()
        v = cw.at[pl.ds(gk, GHALF)]
        g[6].append(go(rcopy(v, v, sib)))

    def gram_back():
        g[6][0].wait_recv()
        for c in g[4] + g[5] + g[6]:
            c.wait_send()
            left_early.append(id(c))

    def ready_p():
        for c in psib + tsib:
            c.wait_recv()
        tcopy = pltpu.make_async_copy(tab, tab_s, lsem.at[0])
        tcopy.start()
        for i in range(8):
            hi, lo = split(jnp.transpose(pg[i // 2, i % 2]))
            pth[:, i * 128:(i + 1) * 128] = hi
            ptl[:, i * 128:(i + 1) * 128] = lo
        tcopy.wait()
        zero = jnp.zeros((8 * 128, HW), BF)
        for i in range(2):
            agh[REST + i] = zero
            agl[REST + i] = zero

    def convert(h):
        for c in asib[h]:
            c.wait_recv()

        def conv(i, carry):
            o = pl.multiple_of(i * 128, 128)
            for t in range(0, REST, 2):
                v = ag[i // 2, lax.rem(i, 2), h, :, t * QW:(t + 2) * QW]
                for n, w in enumerate((v, swap(v))):
                    hi, lo = split(w)
                    agh[t + n, pl.ds(o, 128), :] = hi
                    agl[t + n, pl.ds(o, 128), :] = lo
            return carry

        lax.fori_loop(0, 8, conv, 0)

    def products(h, part):
        if part == 0:
            convert(h)
        j = x // 2 if part else 1 - x // 2

        def pair(b, carry):
            mask = low((ROWS, HW))
            rows_at = [lax.rem(y + 1 + 2 * b + u, 4) for u in range(2)]
            for u in range(2):
                slot = (rows_at[u] * 4 + 2 * j) * 2 + k
                for n in range(16):
                    at0 = tab_s[n // 4, (n // 2) % 2, n % 2, slot]
                    at1 = tab_s[n // 4, (n // 2) % 2, n % 2, slot + 2]
                    at1 = at1 + 1 - 2 * lax.rem(at1, 2)
                    rn = slice(n * ROWS, (n + 1) * ROWS)
                    cn = slice(u * HW, (u + 1) * HW)
                    bh[rn, cn] = jnp.where(mask, agh[at0, rn, :], agh[at1, rn, :])
                    bl[rn, cn] = jnp.where(mask, agl[at0, rn, :], agl[at1, rn, :])
            got = dot3((pth[...], ptl[...]), (bh[...], bl[...]))
            half = low((128, HW))
            for u in range(2):
                top = got[0:128, u * HW:(u + 1) * HW]
                bottom = got[128:256, u * HW:(u + 1) * HW]
                yy = rows_at[u]
                sp[h, yy, 2 * j] = jnp.where(half, top, swap(bottom))
                sp[h, yy, 2 * j + 1] = jnp.where(half, swap(top), bottom)
            for u in range(2):
                yy = rows_at[u]
                if part:
                    first(h, 2 * j + 1 - lax.rem(x, 2), yy).start()
                else:
                    first(h, 2 * j, yy).start()
                    first(h, 2 * j + 1, yy).start()
            second(h, rows_at[0], j).start()

            @pl.when(b == 0)
            def _():
                second(h, rows_at[1], j).start()

            return carry

        lax.fori_loop(0, 2, pair, 0)

    base1 = SEM_FIX

    def first(h, px, yy):
        at = base1 + h * 24
        return pltpu.make_async_remote_copy(
            src_ref=sp.at[h, yy, px, pl.ds(0, 64)], dst_ref=ra.at[h, x, yy],
            send_sem=xsem_s.at[at + 4 * px + yy], recv_sem=xsem_r.at[at + 4 * x + yy],
            device_id=(row, y * 4 + px), device_id_type=MESH,
        )

    def first_in(h, px, yy):
        at = base1 + h * 24
        return pltpu.make_async_remote_copy(
            src_ref=sp.at[h, yy, px, pl.ds(0, 64)], dst_ref=ra.at[h, px, yy],
            send_sem=xsem_s.at[at + 4 * px + yy], recv_sem=xsem_r.at[at + 4 * px + yy],
            device_id=(row, y * 4 + px), device_id_type=MESH,
        )

    def second(h, py, j):
        at = base1 + h * 24 + 16
        return pltpu.make_async_remote_copy(
            src_ref=sp.at[h, py, pl.ds(2 * j, 2), pl.ds(64, 64)],
            dst_ref=rb.at[h, y, pl.ds(2 * j, 2)],
            send_sem=xsem_s.at[at + 2 * py + j], recv_sem=xsem_r.at[at + 2 * y + j],
            device_id=(row, py * 4 + x), device_id_type=MESH,
        )

    def second_in(h, py, j):
        at = base1 + h * 24 + 16
        return pltpu.make_async_remote_copy(
            src_ref=sp.at[h, py, pl.ds(2 * j, 2), pl.ds(64, 64)],
            dst_ref=rb.at[h, py, pl.ds(2 * j, 2)],
            send_sem=xsem_s.at[at + 2 * py + j], recv_sem=xsem_r.at[at + 2 * py + j],
            device_id=(row, py * 4 + x), device_id_type=MESH,
        )

    s2, s3 = {}, {}

    def reduce2(h):
        for d in (1, 2, 3):
            for i in range(4):
                first_in(h, lax.rem(x + d, 4), i).wait_recv()
            for j in range(2):
                second_in(h, lax.rem(y + d, 4), j).wait_recv()
        for i in range(4):
            va = sp[h, i, x, 0:64, :]
            vb = sp[h, y, i, 64:128, :]
            for d in (1, 2, 3):
                va = va + ra[h, lax.rem(x + d, 4), i]
                vb = vb + rb[h, lax.rem(y + d, 4), i]
            sa[h, i] = va
            sb[h, i] = vb
        s2[h] = []
        for d in (1, 2, 3):
            s2[h].append(go(rcopy(sa.at[h, lax.rem(y + d, 4)], ra2.at[h, d - 1], yp(d))))
            s2[h].append(go(rcopy(sb.at[h, lax.rem(x + d, 4)], rb2.at[h, d - 1], xp(d))))

    def sent1(h):
        for d in (1, 2, 3):
            for i in range(4):
                first_in(h, lax.rem(x + d, 4), i).wait_send()
            for j in range(2):
                second_in(h, lax.rem(y + d, 4), j).wait_send()

    def gather1(h):
        for c in s2[h]:
            c.wait_recv()
        sfull[z, k, h, 0:64, :] = sa[h, y] + ra2[h, 0] + ra2[h, 1] + ra2[h, 2]
        sfull[z, k, h, 64:128, :] = sb[h, x] + rb2[h, 0] + rb2[h, 1] + rb2[h, 2]
        v = sfull.at[z, k, h]
        s3[h] = [go(rcopy(v, v, zp(d))) for d in (1, 2, 3)]
        s3[h].append(go(rcopy(v, v, sib)))

    def gather2(h):
        for d in (1, 2, 3):
            s3[h][d - 1].wait_recv()
            v = sfull.at[lax.rem(z + 4 - d, 4), k, h]
            s3[h].append(go(rcopy(v, v, sib)))

    rr = lax.broadcasted_iota(jnp.int32, (T, T), 0)
    cc = lax.broadcasted_iota(jnp.int32, (T, T), 1)
    eye = rr == cc
    phi = jnp.where(eye, 0.5, jnp.where(rr > cc, 1.0, 0.0)).astype(F32)
    ident = jnp.where(eye, 1.0, 0.0).astype(F32)
    checks = []
    lengths = []

    def block(q, r):
        i = BLK[q, r]
        return pl.ds(i * T, T)

    def factor(p):
        if p == 0:
            for q in range(PANELS):
                diag = jnp.where(eye, cw[block(q, q), :], 0.0)
                lengths.append(jnp.sum(diag, axis=0, keepdims=True))
        c0 = cw[block(p, p), :]
        diag = jnp.where(eye, c0, 0.0)
        left = jnp.sum(diag, axis=0, keepdims=True)
        dr = lax.rsqrt(left)
        dc = lax.rsqrt(jnp.sum(diag, axis=1, keepdims=True))
        scaled = c0 * dr * dc
        sh, sl = split(scaled)
        n0 = phi * (scaled - ident)
        wref[...] = ident - n0

        def it(i, carry):
            w = split(wref[...])
            t = split(dot3(w, (sh, sl)))
            e = dot3(t, w, 1, 1) - ident
            n = phi * e
            wref[...] = wref[...] - dot3(split(n), w)
            return jnp.sum(e * e, axis=0, keepdims=True)

        err = lax.fori_loop(0, NEWTON - 1, it, jnp.zeros((1, T), F32))
        checks.append(jnp.sum(err) < RESIDUAL)
        checks.append(jnp.min(left - SHARE * lengths[p]) > 0.0)
        w = wref[...] * dr
        hi, lo = split(w)
        wh_ref[p] = hi
        wl_ref[p] = lo
        for r in range(p, PANELS):
            c = split(cw[block(p, r), :])
            u = dot3((hi, lo), c)
            rp[r, p] = u
            if r > p:
                uh, ul = split(jnp.transpose(u))
                uth[BLK[p, r]] = uh
                utl[BLK[p, r]] = ul
        for q in range(p + 1, PANELS):
            for r in range(q, PANELS):
                upd = dot3((uth[BLK[p, q]], utl[BLK[p, q]]), split(rp[r, p]))
                cw[block(q, r), :] = cw[block(q, r), :] - upd
        for r in range(p):
            rp[r, p] = jnp.zeros((T, T), F32)

    def solve(g):
        xs = []
        half = low((128, HW))
        for p in range(PANELS):
            cols = []
            for s in range(2):
                a, b = sfull[p, s, 2 * g], sfull[p, s, 2 * g + 1]
                cols.append(jnp.concatenate(
                    [jnp.where(half, a, swap(b)), jnp.where(half, swap(a), b)], axis=0))
            acc = jnp.concatenate(cols, axis=1)
            for q in range(p):
                acc = acc - dot3((uth[BLK[q, p]], utl[BLK[q, p]]), xs[q])
            got = dot3((wh_ref[p], wl_ref[p]), split(acc))
            if p < PANELS - 1:
                xs.append(split(got))
            for s in range(2):
                slot = col * 2 + s
                which = jnp.int32(0)
                is_panel = jnp.int32(0)
                for m in range(PANELS):
                    hit = owner_ref[m] == slot
                    which = jnp.where(hit, m, which)
                    is_panel = jnp.where(hit, 1, is_panel)
                mask = jnp.full((T, HW), is_panel, jnp.int32) == 1
                at = s * T + g * HW
                out_ref[p * T:(p + 1) * T, at:at + HW] = jnp.where(
                    mask, rp[which, p, :, g * HW:(g + 1) * HW], got[:, s * HW:(s + 1) * HW])

    def solved(g):
        for h in (2 * g, 2 * g + 1):
            for c in s3[h][3:]:
                c.wait_recv()
        solve(g)

    start_near(0, 0)
    start_sib(1)
    start_p()
    gram()
    start_sib(0)
    sum0()
    start_near(1, 0)
    start_near(0, 1)
    pack(3)
    forward_a(0)
    sum1()
    pack(2)
    start_near(1, 1)
    forward_p()
    forward_a(1)
    start_sib(2)
    start_near(2, 0)
    start_near(3, 0)
    sum2()
    sib_a(0)
    finish_a(0)
    ready_p()
    products(0, 0)
    sib_a(1)
    products(0, 1)
    finish_a(1)
    sum3()
    start_near(2, 1)
    products(1, 0)
    start_sib(3)
    products(1, 1)
    back4()
    forward_a(2)
    reduce2(0)
    start_near(3, 1)
    reduce2(1)
    back5()
    forward_a(3)
    sib_a(2)
    finish_a(2)
    sib_a(3)
    products(2, 0)
    finish_a(3)
    products(2, 1)
    products(3, 0)
    gather1(0)
    back6()
    products(3, 1)
    gram_back()
    factor(0)
    gather1(1)
    reduce2(2)
    factor(1)
    reduce2(3)
    gather2(0)
    gather1(2)
    factor(2)
    gather2(1)
    gather1(3)
    factor(3)
    solved(0)
    gather2(2)
    gather2(3)
    solved(1)
    good = checks[0]
    for c in checks[1:]:
        good = jnp.logical_and(good, c)
    good_ref[0] = good.astype(jnp.int32)
    for c in sends:
        if id(c) not in left_early:
            c.wait_send()
    for h in range(H):
        sent1(h)


def fast(child_blocks, home_child, col_tiles, tile_owner):
    sem = SEM_FIX + 24 * H
    vm = pltpu.VMEM
    vmem = pl.BlockSpec(memory_space=pltpu.VMEM)
    smem = pl.BlockSpec(memory_space=pltpu.SMEM)
    return pl.pallas_call(
        kernel,
        out_shape=(
            pltpu.VMEM((PANELS * T, 2 * T), F32),
            jax.ShapeDtypeStruct((1,), jnp.int32),
        ),
        in_specs=[smem, smem, smem, vmem],
        out_specs=(vmem, smem),
        scratch_shapes=[
            vm((4, 2, H, OWN * ROWS, REST * QW), F32),
            vm((PANELS, OWN * ROWS, T), F32),
            vm((4, 2, OWN * ROWS, T), F32),
            vm((4, 2, 8, 128), jnp.int32),
            pltpu.SMEM((4, 2, 8, 128), jnp.int32),
            vm((REST + 2, 8 * 128, HW), BF),
            vm((REST + 2, 8 * 128, HW), BF),
            vm((T, 1024), BF),
            vm((T, 1024), BF),
            vm((1024, T), BF),
            vm((1024, T), BF),
            vm((H, 4, 4, 128, HW), F32),
            vm((H, 4, 4, 64, HW), F32),
            vm((H, 4, 4, 64, HW), F32),
            vm((H, 4, 64, HW), F32),
            vm((H, 4, 64, HW), F32),
            vm((H, 3, 64, HW), F32),
            vm((H, 3, 64, HW), F32),
            vm((4, 2, H, 128, HW), F32),
            vm((GROWS, T), F32),
            vm((GHALF, T), F32),
            vm((3, GC, T), F32),
            vm((3, GC, T), F32),
            vm((GC, T), F32),
            vm((GC, T), F32),
            vm((3, GS, T), F32),
            vm((3, GS, T), F32),
            vm((4, GS, T), F32),
            vm((4, GS, T), F32),
            vm((T, T), F32),
            vm((PANELS, T, T), BF),
            vm((PANELS, T, T), BF),
            vm((GROWS, T), F32),
            vm((len(BLOCKS), T, T), BF),
            vm((len(BLOCKS), T, T), BF),
            vm((PANELS, PANELS, T, T), F32),
            pltpu.SemaphoreType.DMA((sem,)),
            pltpu.SemaphoreType.DMA((sem,)),
            pltpu.SemaphoreType.DMA((1,)),
        ],
        compiler_params=pltpu.CompilerParams(
            collective_id=0, has_side_effects=True, vmem_limit_bytes=52 * 1024 * 1024
        ),
        cost_estimate=pl.CostEstimate(flops=10**10, bytes_accessed=10**7, transcendentals=0),
        name="front",
    )(home_child, col_tiles.T, tile_owner, child_blocks)


def total(x, axis):
    size = lax.axis_size(axis)
    step = 1
    while step < size:
        x = x + lax.ppermute(x, axis, [(i, i ^ step) for i in range(size)])
        step *= 2
    return x


def gathered(x, axis):
    size = lax.axis_size(axis)
    me = lax.axis_index(axis)
    step = 1
    while step < size:
        other = lax.ppermute(x, axis, [(i, i ^ step) for i in range(size)])
        low = (me // step) % 2 == 0
        x = jnp.concatenate([jnp.where(low, x, other), jnp.where(low, other, x)], axis=0)
        step *= 2
    return x


def broadcast(x, axis, root):
    mine = lax.axis_index(axis) == root
    return total(jnp.where(mine, x, jnp.zeros_like(x)), axis)


def storage_positions(home_child, col_tiles, tile_owner):
    count = col_tiles.shape[0]
    tiles_all = tile_owner.shape[0]
    picked = home_child[:, None] == jnp.arange(count, dtype=jnp.int32)[None, :]
    child_tiles = jnp.sum(jnp.where(picked[:, :, None], col_tiles[None, :, :], 0), axis=1)
    matches = child_tiles[:, :, None] == jnp.arange(tiles_all, dtype=jnp.int32)[None, None, :]
    return jnp.sum(jnp.where(matches, tile_owner[None, None, :], 0), axis=2)


def general(child_blocks, home_child, col_tiles, tile_owner):
    highest = lax.Precision.HIGHEST
    col_count = lax.axis_size("col")
    local_cols = FRONT_COLS // col_count
    held = local_cols // T
    my_col = lax.axis_index("col")
    first_held = my_col * held
    position = storage_positions(home_child, col_tiles, tile_owner)
    piece_blocks = gathered(child_blocks, "col")
    piece_slots = gathered(position, "col")
    count = piece_blocks.shape[0]
    local_tile = piece_slots - first_held
    mine = (local_tile[:, :, None] == jnp.arange(held, dtype=jnp.int32)[None, None, :]).astype(
        jnp.float32
    )
    shaped = piece_blocks.reshape(count, ROWS, CT, T)
    placed = jnp.einsum("nrjc,njk->nrkc", shaped, mine, precision=highest)
    placed = placed.reshape(count * ROWS, local_cols)
    front = placed
    identity = jnp.eye(T, dtype=jnp.float32)
    results = []
    for step in range(PANELS):
        stored_at = tile_owner[step]
        holder = stored_at // held
        offset = (stored_at - holder * held) * T
        is_holder = holder == my_col
        panel = lax.dynamic_slice_in_dim(front, offset, T, 1)
        panel = jnp.where(is_holder, panel, 0.0)
        gram_part = jnp.dot(panel.T, panel, precision=highest, preferred_element_type=jnp.float32)
        gram = total(gram_part, "row")
        gram = gram + jnp.where(is_holder, 0.0, identity)
        lower = jnp.linalg.cholesky(gram)
        basis = jax.scipy.linalg.solve_triangular(lower, panel.T, lower=True).T
        basis = broadcast(basis, "col", holder)
        local_proj = jnp.dot(basis.T, front, precision=highest, preferred_element_type=jnp.float32)
        projected = total(local_proj, "row")
        front = front - jnp.dot(
            basis, projected, precision=highest, preferred_element_type=jnp.float32
        )
        results.append(projected)
    stacked = jnp.concatenate(results, axis=0)
    return stacked


def body(child_blocks, home_child, col_tiles, tile_owner):
    args = (child_blocks, home_child, col_tiles, tile_owner)
    out, good = fast(*args)
    return lax.cond(good[0] == 1, lambda *a: out, general, *args)


def solution(mesh):
    return jax.shard_map(
        body,
        mesh=mesh,
        in_specs=(P(("row", "col"), None, None), P(("row", "col")), P(), P()),
        out_specs=P(None, "col"),
        check_vma=False,
    )
```

```python
import jax
import jax.numpy as jnp
from jax import lax
from jax.experimental import pallas as pl
from jax.experimental.pallas import tpu as pltpu
from jax.sharding import PartitionSpec as P

T = 256
TILES = 32
CT = 12
ROWS = 64
FRONT_COLS = 8192
PANELS = 4
OWN = 2
REST = CT - PANELS
H = 4
QW = T // H
HW = 2 * QW
NEWTON = 3
SEM_FIX = 140
RESIDUAL = 8e-5
SHARE = 0.1
F32 = jnp.float32
BF = jnp.bfloat16
MESH = pl.DeviceIdType.MESH
BLOCKS = [(q, r) for q in range(PANELS) for r in range(q, PANELS)]
BLK = {qr: i for i, qr in enumerate(BLOCKS)}
GROWS = len(BLOCKS) * T
GHALF = GROWS // 2
GQ = GHALF // 2
GC = GQ // 4
GS = GC // 4


def split(x):
    hi = x.astype(BF)
    lo = (x - hi.astype(F32)).astype(BF)
    return hi, lo


def dg(a, b, ca, cb):
    return lax.dot_general(a, b, (((ca,), (cb,)), ((), ())), preferred_element_type=F32)


def dot3(a, b, ca=1, cb=0):
    ah, al = a
    bh, bl = b
    return dg(ah, bh, ca, cb) + (dg(ah, bl, ca, cb) + dg(al, bh, ca, cb))


def kernel(
    home_ref, tiles_ref, owner_ref, blocks_ref,
    out_ref, good_ref,
    ag, pown, pg, tab, tab_s, agh, agl, pth, ptl, bh, bl, sp,
    ra, rb, sa, sb, ra2, rb2, sfull,
    gbuf, grc, ga, gb, gsa, gsb, ga2, gb2, gza, gzb,
    wref, wh_ref, wl_ref, cw, uth, utl, rp,
    xsem_s, xsem_r, lsem,
):
    row = lax.axis_index("row")
    col = lax.axis_index("col")
    z = row // 2
    k = row % 2
    y = col // 4
    x = col % 4
    sib = (z * 2 + (1 - k), col)

    def zp(d):
        return (lax.rem(z + d, 4) * 2 + k, col)

    def xp(d):
        return (row, y * 4 + lax.rem(x + d, 4))

    def yp(d):
        return (row, lax.rem(y + d, 4) * 4 + x)

    barrier = pltpu.get_barrier_semaphore()
    partners = [sib] + [f(d) for f in (zp, xp, yp) for d in (1, 2, 3)]
    for dev in partners:
        pl.semaphore_signal(barrier, inc=1, device_id=dev, device_id_type=MESH)

    counter = [0]

    def rcopy(src, dst, dev):
        i = counter[0]
        counter[0] += 1
        return pltpu.make_async_remote_copy(
            src_ref=src, dst_ref=dst, send_sem=xsem_s.at[i], recv_sem=xsem_r.at[i],
            device_id=dev, device_id_type=MESH,
        )

    sends = []
    left_early = []

    def go(copy):
        copy.start()
        sends.append(copy)
        return copy

    lane = lax.broadcasted_iota(jnp.int32, (8, 128), 1)
    sub = lax.broadcasted_iota(jnp.int32, (8, 128), 0)
    table = jnp.full((8, 128), REST, jnp.int32)
    place = []
    for c in range(OWN):
        home = home_ref[c]
        panel_at = [jnp.int32(0)] * PANELS
        rest_at = [jnp.int32(0)] * REST
        count = jnp.int32(0)
        for j in range(CT):
            t = tiles_ref[j, home]
            p = owner_ref[t]
            rest = t >= PANELS
            for m in range(PANELS):
                panel_at[m] = jnp.where(t == m, j, panel_at[m])
            for i in range(min(j + 1, REST)):
                rest_at[i] = jnp.where(jnp.logical_and(rest, count == i), j, rest_at[i])
            table = jnp.where(
                jnp.logical_and(jnp.logical_and(lane == p, sub == c), rest), count, table)
            count = count + rest.astype(jnp.int32)
        place.append((panel_at, rest_at))
    tab[z, k] = table
    for c in range(OWN):
        for m in range(PANELS):
            pown[m, c * ROWS:(c + 1) * ROWS, :] = blocks_ref[c, :, pl.ds(place[c][0][m] * T, T)]

    def low(shape):
        return lax.broadcasted_iota(jnp.int32, shape, 1) < QW

    def swap(v):
        return pltpu.roll(v, QW, 1)

    def pack(h):
        for c in range(OWN):
            for i in range(0, REST, 2):
                a, b = (
                    blocks_ref[c, :, pl.ds(place[c][1][i + n] * T + h // 2 * HW, HW)]
                    for n in range(2))
                both = (swap(a), b) if h % 2 else (a, swap(b))
                ag[z, k, h, c * ROWS:(c + 1) * ROWS, i * QW:(i + 2) * QW] = jnp.where(
                    low((ROWS, HW)), *both)

    pack(0)
    pack(1)
    pg[z, k] = pown[z]
    pl.semaphore_wait(barrier, len(partners))

    def rows(c):
        return pl.ds(c * ROWS, ROWS)

    ar, al_, asib = {}, {}, {}

    def start_sib(h):
        mine = ag.at[z, k, h]
        asib[h] = [go(rcopy(mine, mine, sib))]

    def start_near(h, c):
        me = ag.at[z, k, h, rows(c)]
        ar[h, c] = go(rcopy(me, me, zp(1)))
        other = ag.at[z, k, h, rows(1 - c)]
        al_[h, 1 - c] = go(rcopy(other, other, zp(3)))

    fr, fl = {}, {}
    left = lax.rem(z + 3, 4)
    right = lax.rem(z + 1, 4)
    far = lax.rem(z + 2, 4)

    def forward_a(h):
        ar[h, 0].wait_recv()
        v = ag.at[left, k, h, rows(0)]
        fr[h] = go(rcopy(v, v, zp(1)))
        al_[h, 1].wait_recv()
        v = ag.at[right, k, h, rows(1)]
        fl[h] = go(rcopy(v, v, zp(3)))

    def sib_a(h):
        ar[h, 1].wait_recv()
        v = ag.at[left, k, h]
        asib[h].append(go(rcopy(v, v, sib)))
        al_[h, 0].wait_recv()
        v = ag.at[right, k, h]
        asib[h].append(go(rcopy(v, v, sib)))

    def finish_a(h):
        fr[h].wait_recv()
        fl[h].wait_recv()
        v = ag.at[far, k, h]
        asib[h].append(go(rcopy(v, v, sib)))

    pz, tz, psib, tsib = [], [], [], []

    def start_p():
        for d in (1, 2, 3):
            pz.append(go(rcopy(pown.at[lax.rem(z + d, 4)], pg.at[z, k], zp(d))))
            tz.append(go(rcopy(tab.at[z, k], tab.at[z, k], zp(d))))
        psib.append(go(rcopy(pown.at[z], pg.at[z, k], sib)))
        tsib.append(go(rcopy(tab.at[z, k], tab.at[z, k], sib)))

    def forward_p():
        for i, d in enumerate((1, 2, 3)):
            src = lax.rem(z + 4 - d, 4)
            pz[i].wait_recv()
            tz[i].wait_recv()
            v = pg.at[src, k]
            psib.append(go(rcopy(v, v, sib)))
            t = tab.at[src, k]
            tsib.append(go(rcopy(t, t, sib)))

    def gram():
        halves = [split(pown[m]) for m in range(PANELS)]
        for i, (q, r) in enumerate(BLOCKS):
            gbuf[i * T:(i + 1) * T, :] = dot3(halves[q], halves[r], 0, 0)

    gk = pl.multiple_of(k * GHALF, GHALF)
    go_ = pl.multiple_of((1 - k) * GHALF, GHALF)

    def add_rows(dst, off, n, srcs):
        step = 160 if n % 160 == 0 else n

        def body(i, carry):
            o = pl.multiple_of(i * step, 8)
            acc = dst[pl.ds(off + o, step), :]
            for s in srcs:
                acc = acc + s[pl.ds(o, step), :]
            dst[pl.ds(off + o, step), :] = acc
            return carry

        lax.fori_loop(0, n // step, body, 0)

    base_b = pl.multiple_of(gk + GQ, GQ)
    my_a = pl.multiple_of(gk + x * GC, GC)
    my_b = pl.multiple_of(base_b + y * GC, GC)
    fa = pl.multiple_of(my_a + y * GS, GS)
    fb = pl.multiple_of(my_b + x * GS, GS)
    g = {n: [] for n in range(7)}

    def sum0():
        g[0].append(go(rcopy(gbuf.at[pl.ds(go_, GHALF)], grc, sib)))

    def sum1():
        g[0][0].wait_recv()
        add_rows(gbuf, gk, GHALF, [grc])
        for d in (1, 2, 3):
            ox = pl.multiple_of(gk + lax.rem(x + d, 4) * GC, GC)
            oy = pl.multiple_of(base_b + lax.rem(y + d, 4) * GC, GC)
            g[1].append(go(rcopy(gbuf.at[pl.ds(ox, GC)], ga.at[d - 1], xp(d))))
            g[1].append(go(rcopy(gbuf.at[pl.ds(oy, GC)], gb.at[d - 1], yp(d))))

    def sum2():
        for c in g[1]:
            c.wait_recv()
        gsa[...] = gbuf[pl.ds(my_a, GC), :] + ga[0] + ga[1] + ga[2]
        gsb[...] = gbuf[pl.ds(my_b, GC), :] + gb[0] + gb[1] + gb[2]
        for d in (1, 2, 3):
            oy = pl.multiple_of(lax.rem(y + d, 4) * GS, GS)
            ox = pl.multiple_of(lax.rem(x + d, 4) * GS, GS)
            g[2].append(go(rcopy(gsa.at[pl.ds(oy, GS)], ga2.at[d - 1], yp(d))))
            g[2].append(go(rcopy(gsb.at[pl.ds(ox, GS)], gb2.at[d - 1], xp(d))))

    def sum3():
        for c in g[2]:
            c.wait_recv()
        oya = pl.multiple_of(y * GS, GS)
        oxb = pl.multiple_of(x * GS, GS)
        gza[z] = gsa[pl.ds(oya, GS), :] + ga2[0] + ga2[1] + ga2[2]
        gzb[z] = gsb[pl.ds(oxb, GS), :] + gb2[0] + gb2[1] + gb2[2]
        for d in (1, 2, 3):
            g[3].append(go(rcopy(gza.at[z], gza.at[z], zp(d))))
            g[3].append(go(rcopy(gzb.at[z], gzb.at[z], zp(d))))

    def back4():
        for c in g[3]:
            c.wait_recv()
        cw[pl.ds(fa, GS), :] = gza[0] + gza[1] + gza[2] + gza[3]
        cw[pl.ds(fb, GS), :] = gzb[0] + gzb[1] + gzb[2] + gzb[3]
        for d in (1, 2, 3):
            v = cw.at[pl.ds(fa, GS)]
            g[4].append(go(rcopy(v, v, yp(d))))
            v = cw.at[pl.ds(fb, GS)]
            g[4].append(go(rcopy(v, v, xp(d))))

    def back5():
        for c in g[4]:
            c.wait_recv()
        for d in (1, 2, 3):
            v = cw.at[pl.ds(my_a, GC)]
            g[5].append(go(rcopy(v, v, xp(d))))
            v = cw.at[pl.ds(my_b, GC)]
            g[5].append(go(rcopy(v, v, yp(d))))

    def back6():
        for c in g[5]:
            c.wait_recv()
        v = cw.at[pl.ds(gk, GHALF)]
        g[6].append(go(rcopy(v, v, sib)))

    def gram_back():
        g[6][0].wait_recv()
        for c in g[4] + g[5] + g[6]:
            c.wait_send()
            left_early.append(id(c))

    def ready_p():
        for c in psib + tsib:
            c.wait_recv()
        tcopy = pltpu.make_async_copy(tab, tab_s, lsem.at[0])
        tcopy.start()
        for i in range(8):
            hi, lo = split(jnp.transpose(pg[i // 2, i % 2]))
            pth[:, i * 128:(i + 1) * 128] = hi
            ptl[:, i * 128:(i + 1) * 128] = lo
        tcopy.wait()
        zero = jnp.zeros((8 * 128, HW), BF)
        for i in range(2):
            agh[REST + i] = zero
            agl[REST + i] = zero

    def convert(h):
        for c in asib[h]:
            c.wait_recv()

        def conv(i, carry):
            o = pl.multiple_of(i * 128, 128)
            for t in range(0, REST, 2):
                v = ag[i // 2, lax.rem(i, 2), h, :, t * QW:(t + 2) * QW]
                for n, w in enumerate((v, swap(v))):
                    hi, lo = split(w)
                    agh[t + n, pl.ds(o, 128), :] = hi
                    agl[t + n, pl.ds(o, 128), :] = lo
            return carry

        lax.fori_loop(0, 8, conv, 0)

    def products(h, part):
        if part == 0:
            convert(h)
        j = x // 2 if part else 1 - x // 2

        def pair(b, carry):
            mask = low((ROWS, HW))
            rows_at = [lax.rem(y + 1 + 2 * b + u, 4) for u in range(2)]
            for u in range(2):
                slot = (rows_at[u] * 4 + 2 * j) * 2 + k
                for n in range(16):
                    at0 = tab_s[n // 4, (n // 2) % 2, n % 2, slot]
                    at1 = tab_s[n // 4, (n // 2) % 2, n % 2, slot + 2]
                    at1 = at1 + 1 - 2 * lax.rem(at1, 2)
                    rn = slice(n * ROWS, (n + 1) * ROWS)
                    cn = slice(u * HW, (u + 1) * HW)
                    bh[rn, cn] = jnp.where(mask, agh[at0, rn, :], agh[at1, rn, :])
                    bl[rn, cn] = jnp.where(mask, agl[at0, rn, :], agl[at1, rn, :])
            got = dot3((pth[...], ptl[...]), (bh[...], bl[...]))
            half = low((128, HW))
            for u in range(2):
                top = got[0:128, u * HW:(u + 1) * HW]
                bottom = got[128:256, u * HW:(u + 1) * HW]
                yy = rows_at[u]
                sp[h, yy, 2 * j] = jnp.where(half, top, swap(bottom))
                sp[h, yy, 2 * j + 1] = jnp.where(half, swap(top), bottom)
            for u in range(2):
                yy = rows_at[u]
                if part:
                    first(h, 2 * j + 1 - lax.rem(x, 2), yy).start()
                else:
                    first(h, 2 * j, yy).start()
                    first(h, 2 * j + 1, yy).start()
            second(h, rows_at[0], j).start()

            @pl.when(b == 0)
            def _():
                second(h, rows_at[1], j).start()

            return carry

        lax.fori_loop(0, 2, pair, 0)

    base1 = SEM_FIX

    def first(h, px, yy):
        at = base1 + h * 24
        return pltpu.make_async_remote_copy(
            src_ref=sp.at[h, yy, px, pl.ds(0, 64)], dst_ref=ra.at[h, x, yy],
            send_sem=xsem_s.at[at + 4 * px + yy], recv_sem=xsem_r.at[at + 4 * x + yy],
            device_id=(row, y * 4 + px), device_id_type=MESH,
        )

    def first_in(h, px, yy):
        at = base1 + h * 24
        return pltpu.make_async_remote_copy(
            src_ref=sp.at[h, yy, px, pl.ds(0, 64)], dst_ref=ra.at[h, px, yy],
            send_sem=xsem_s.at[at + 4 * px + yy], recv_sem=xsem_r.at[at + 4 * px + yy],
            device_id=(row, y * 4 + px), device_id_type=MESH,
        )

    def second(h, py, j):
        at = base1 + h * 24 + 16
        return pltpu.make_async_remote_copy(
            src_ref=sp.at[h, py, pl.ds(2 * j, 2), pl.ds(64, 64)],
            dst_ref=rb.at[h, y, pl.ds(2 * j, 2)],
            send_sem=xsem_s.at[at + 2 * py + j], recv_sem=xsem_r.at[at + 2 * y + j],
            device_id=(row, py * 4 + x), device_id_type=MESH,
        )

    def second_in(h, py, j):
        at = base1 + h * 24 + 16
        return pltpu.make_async_remote_copy(
            src_ref=sp.at[h, py, pl.ds(2 * j, 2), pl.ds(64, 64)],
            dst_ref=rb.at[h, py, pl.ds(2 * j, 2)],
            send_sem=xsem_s.at[at + 2 * py + j], recv_sem=xsem_r.at[at + 2 * py + j],
            device_id=(row, py * 4 + x), device_id_type=MESH,
        )

    s2, s3 = {}, {}

    def reduce2(h):
        for d in (1, 2, 3):
            for i in range(4):
                first_in(h, lax.rem(x + d, 4), i).wait_recv()
            for j in range(2):
                second_in(h, lax.rem(y + d, 4), j).wait_recv()
        for i in range(4):
            va = sp[h, i, x, 0:64, :]
            vb = sp[h, y, i, 64:128, :]
            for d in (1, 2, 3):
                va = va + ra[h, lax.rem(x + d, 4), i]
                vb = vb + rb[h, lax.rem(y + d, 4), i]
            sa[h, i] = va
            sb[h, i] = vb
        s2[h] = []
        for d in (1, 2, 3):
            s2[h].append(go(rcopy(sa.at[h, lax.rem(y + d, 4)], ra2.at[h, d - 1], yp(d))))
            s2[h].append(go(rcopy(sb.at[h, lax.rem(x + d, 4)], rb2.at[h, d - 1], xp(d))))

    def sent1(h):
        for d in (1, 2, 3):
            for i in range(4):
                first_in(h, lax.rem(x + d, 4), i).wait_send()
            for j in range(2):
                second_in(h, lax.rem(y + d, 4), j).wait_send()

    def gather1(h):
        for c in s2[h]:
            c.wait_recv()
        sfull[z, k, h, 0:64, :] = sa[h, y] + ra2[h, 0] + ra2[h, 1] + ra2[h, 2]
        sfull[z, k, h, 64:128, :] = sb[h, x] + rb2[h, 0] + rb2[h, 1] + rb2[h, 2]
        v = sfull.at[z, k, h]
        s3[h] = [go(rcopy(v, v, zp(d))) for d in (1, 2, 3)]
        s3[h].append(go(rcopy(v, v, sib)))

    def gather2(h):
        for d in (1, 2, 3):
            s3[h][d - 1].wait_recv()
            v = sfull.at[lax.rem(z + 4 - d, 4), k, h]
            s3[h].append(go(rcopy(v, v, sib)))

    rr = lax.broadcasted_iota(jnp.int32, (T, T), 0)
    cc = lax.broadcasted_iota(jnp.int32, (T, T), 1)
    eye = rr == cc
    phi = jnp.where(eye, 0.5, jnp.where(rr > cc, 1.0, 0.0)).astype(F32)
    ident = jnp.where(eye, 1.0, 0.0).astype(F32)
    checks = []
    lengths = []

    def block(q, r):
        i = BLK[q, r]
        return pl.ds(i * T, T)

    def factor(p):
        if p == 0:
            for q in range(PANELS):
                diag = jnp.where(eye, cw[block(q, q), :], 0.0)
                lengths.append(jnp.sum(diag, axis=0, keepdims=True))
        c0 = cw[block(p, p), :]
        diag = jnp.where(eye, c0, 0.0)
        left = jnp.sum(diag, axis=0, keepdims=True)
        dr = lax.rsqrt(left)
        dc = lax.rsqrt(jnp.sum(diag, axis=1, keepdims=True))
        scaled = c0 * dr * dc
        sh, sl = split(scaled)
        n0 = phi * (scaled - ident)
        wref[...] = ident - n0

        def it(i, carry):
            w = split(wref[...])
            t = split(dot3(w, (sh, sl)))
            e = dot3(t, w, 1, 1) - ident
            n = phi * e
            wref[...] = wref[...] - dot3(split(n), w)
            return jnp.sum(e * e, axis=0, keepdims=True)

        err = lax.fori_loop(0, NEWTON - 1, it, jnp.zeros((1, T), F32))
        checks.append(jnp.sum(err) < RESIDUAL)
        checks.append(jnp.min(left - SHARE * lengths[p]) > 0.0)
        w = wref[...] * dr
        hi, lo = split(w)
        wh_ref[p] = hi
        wl_ref[p] = lo
        for r in range(p, PANELS):
            c = split(cw[block(p, r), :])
            u = dot3((hi, lo), c)
            rp[r, p] = u
            if r > p:
                uh, ul = split(jnp.transpose(u))
                uth[BLK[p, r]] = uh
                utl[BLK[p, r]] = ul
        for q in range(p + 1, PANELS):
            for r in range(q, PANELS):
                upd = dot3((uth[BLK[p, q]], utl[BLK[p, q]]), split(rp[r, p]))
                cw[block(q, r), :] = cw[block(q, r), :] - upd
        for r in range(p):
            rp[r, p] = jnp.zeros((T, T), F32)

    def solve(g):
        xs = []
        half = low((128, HW))
        for p in range(PANELS):
            cols = []
            for s in range(2):
                a, b = sfull[p, s, 2 * g], sfull[p, s, 2 * g + 1]
                cols.append(jnp.concatenate(
                    [jnp.where(half, a, swap(b)), jnp.where(half, swap(a), b)], axis=0))
            acc = jnp.concatenate(cols, axis=1)
            for q in range(p):
                acc = acc - dot3((uth[BLK[q, p]], utl[BLK[q, p]]), xs[q])
            got = dot3((wh_ref[p], wl_ref[p]), split(acc))
            if p < PANELS - 1:
                xs.append(split(got))
            for s in range(2):
                slot = col * 2 + s
                which = jnp.int32(0)
                is_panel = jnp.int32(0)
                for m in range(PANELS):
                    hit = owner_ref[m] == slot
                    which = jnp.where(hit, m, which)
                    is_panel = jnp.where(hit, 1, is_panel)
                mask = jnp.full((T, HW), is_panel, jnp.int32) == 1
                at = s * T + g * HW
                out_ref[p * T:(p + 1) * T, at:at + HW] = jnp.where(
                    mask, rp[which, p, :, g * HW:(g + 1) * HW], got[:, s * HW:(s + 1) * HW])

    def solved(g):
        for h in (2 * g, 2 * g + 1):
            for c in s3[h][3:]:
                c.wait_recv()
        solve(g)

    start_near(0, 0)
    gram()
    sum0()
    start_p()
    start_near(1, 0)
    sum1()
    start_sib(0)
    start_near(0, 1)
    pack(2)
    forward_a(0)
    start_near(1, 1)
    forward_p()
    forward_a(1)
    sum2()
    ready_p()
    pack(3)
    sib_a(0)
    start_sib(1)
    finish_a(0)
    sib_a(1)
    sum3()
    products(0, 0)
    start_sib(2)
    start_sib(3)
    start_near(3, 0)
    start_near(2, 0)
    start_near(3, 1)
    products(0, 1)
    finish_a(1)
    start_near(2, 1)
    back4()
    products(1, 0)
    products(1, 1)
    reduce2(0)
    back5()
    forward_a(2)
    forward_a(3)
    sib_a(3)
    reduce2(1)
    sib_a(2)
    finish_a(2)
    products(2, 0)
    gather1(0)
    finish_a(3)
    products(2, 1)
    back6()
    products(3, 0)
    gather1(1)
    products(3, 1)
    gram_back()
    factor(0)
    reduce2(2)
    factor(1)
    gather2(0)
    reduce2(3)
    gather2(1)
    gather1(2)
    factor(2)
    gather1(3)
    factor(3)
    solved(0)
    gather2(2)
    gather2(3)
    solved(1)
    good = checks[0]
    for c in checks[1:]:
        good = jnp.logical_and(good, c)
    good_ref[0] = good.astype(jnp.int32)
    for c in sends:
        if id(c) not in left_early:
            c.wait_send()
    for h in range(H):
        sent1(h)


def fast(child_blocks, home_child, col_tiles, tile_owner):
    sem = SEM_FIX + 24 * H
    vm = pltpu.VMEM
    vmem = pl.BlockSpec(memory_space=pltpu.VMEM)
    smem = pl.BlockSpec(memory_space=pltpu.SMEM)
    return pl.pallas_call(
        kernel,
        out_shape=(
            pltpu.VMEM((PANELS * T, 2 * T), F32),
            jax.ShapeDtypeStruct((1,), jnp.int32),
        ),
        in_specs=[smem, smem, smem, vmem],
        out_specs=(vmem, smem),
        scratch_shapes=[
            vm((4, 2, H, OWN * ROWS, REST * QW), F32),
            vm((PANELS, OWN * ROWS, T), F32),
            vm((4, 2, OWN * ROWS, T), F32),
            vm((4, 2, 8, 128), jnp.int32),
            pltpu.SMEM((4, 2, 8, 128), jnp.int32),
            vm((REST + 2, 8 * 128, HW), BF),
            vm((REST + 2, 8 * 128, HW), BF),
            vm((T, 1024), BF),
            vm((T, 1024), BF),
            vm((1024, T), BF),
            vm((1024, T), BF),
            vm((H, 4, 4, 128, HW), F32),
            vm((H, 4, 4, 64, HW), F32),
            vm((H, 4, 4, 64, HW), F32),
            vm((H, 4, 64, HW), F32),
            vm((H, 4, 64, HW), F32),
            vm((H, 3, 64, HW), F32),
            vm((H, 3, 64, HW), F32),
            vm((4, 2, H, 128, HW), F32),
            vm((GROWS, T), F32),
            vm((GHALF, T), F32),
            vm((3, GC, T), F32),
            vm((3, GC, T), F32),
            vm((GC, T), F32),
            vm((GC, T), F32),
            vm((3, GS, T), F32),
            vm((3, GS, T), F32),
            vm((4, GS, T), F32),
            vm((4, GS, T), F32),
            vm((T, T), F32),
            vm((PANELS, T, T), BF),
            vm((PANELS, T, T), BF),
            vm((GROWS, T), F32),
            vm((len(BLOCKS), T, T), BF),
            vm((len(BLOCKS), T, T), BF),
            vm((PANELS, PANELS, T, T), F32),
            pltpu.SemaphoreType.DMA((sem,)),
            pltpu.SemaphoreType.DMA((sem,)),
            pltpu.SemaphoreType.DMA((1,)),
        ],
        compiler_params=pltpu.CompilerParams(
            collective_id=0, has_side_effects=True, vmem_limit_bytes=52 * 1024 * 1024
        ),
        cost_estimate=pl.CostEstimate(flops=10**10, bytes_accessed=10**7, transcendentals=0),
        name="front",
    )(home_child, col_tiles.T, tile_owner, child_blocks)


def total(x, axis):
    size = lax.axis_size(axis)
    step = 1
    while step < size:
        x = x + lax.ppermute(x, axis, [(i, i ^ step) for i in range(size)])
        step *= 2
    return x


def gathered(x, axis):
    size = lax.axis_size(axis)
    me = lax.axis_index(axis)
    step = 1
    while step < size:
        other = lax.ppermute(x, axis, [(i, i ^ step) for i in range(size)])
        low = (me // step) % 2 == 0
        x = jnp.concatenate([jnp.where(low, x, other), jnp.where(low, other, x)], axis=0)
        step *= 2
    return x


def broadcast(x, axis, root):
    mine = lax.axis_index(axis) == root
    return total(jnp.where(mine, x, jnp.zeros_like(x)), axis)


def storage_positions(home_child, col_tiles, tile_owner):
    count = col_tiles.shape[0]
    tiles_all = tile_owner.shape[0]
    picked = home_child[:, None] == jnp.arange(count, dtype=jnp.int32)[None, :]
    child_tiles = jnp.sum(jnp.where(picked[:, :, None], col_tiles[None, :, :], 0), axis=1)
    matches = child_tiles[:, :, None] == jnp.arange(tiles_all, dtype=jnp.int32)[None, None, :]
    return jnp.sum(jnp.where(matches, tile_owner[None, None, :], 0), axis=2)


def general(child_blocks, home_child, col_tiles, tile_owner):
    highest = lax.Precision.HIGHEST
    col_count = lax.axis_size("col")
    local_cols = FRONT_COLS // col_count
    held = local_cols // T
    my_col = lax.axis_index("col")
    first_held = my_col * held
    position = storage_positions(home_child, col_tiles, tile_owner)
    piece_blocks = gathered(child_blocks, "col")
    piece_slots = gathered(position, "col")
    count = piece_blocks.shape[0]
    local_tile = piece_slots - first_held
    mine = (local_tile[:, :, None] == jnp.arange(held, dtype=jnp.int32)[None, None, :]).astype(
        jnp.float32
    )
    shaped = piece_blocks.reshape(count, ROWS, CT, T)
    placed = jnp.einsum("nrjc,njk->nrkc", shaped, mine, precision=highest)
    placed = placed.reshape(count * ROWS, local_cols)
    front = placed
    identity = jnp.eye(T, dtype=jnp.float32)
    results = []
    for step in range(PANELS):
        stored_at = tile_owner[step]
        holder = stored_at // held
        offset = (stored_at - holder * held) * T
        is_holder = holder == my_col
        panel = lax.dynamic_slice_in_dim(front, offset, T, 1)
        panel = jnp.where(is_holder, panel, 0.0)
        gram_part = jnp.dot(panel.T, panel, precision=highest, preferred_element_type=jnp.float32)
        gram = total(gram_part, "row")
        gram = gram + jnp.where(is_holder, 0.0, identity)
        lower = jnp.linalg.cholesky(gram)
        basis = jax.scipy.linalg.solve_triangular(lower, panel.T, lower=True).T
        basis = broadcast(basis, "col", holder)
        local_proj = jnp.dot(basis.T, front, precision=highest, preferred_element_type=jnp.float32)
        projected = total(local_proj, "row")
        front = front - jnp.dot(
            basis, projected, precision=highest, preferred_element_type=jnp.float32
        )
        results.append(projected)
    stacked = jnp.concatenate(results, axis=0)
    return stacked


def body(child_blocks, home_child, col_tiles, tile_owner):
    args = (child_blocks, home_child, col_tiles, tile_owner)
    out, good = fast(*args)
    return lax.cond(good[0] == 1, lambda *a: out, general, *args)


def solution(mesh):
    return jax.shard_map(
        body,
        mesh=mesh,
        in_specs=(P(("row", "col"), None, None), P(("row", "col")), P(), P()),
        out_specs=P(None, "col"),
        check_vma=False,
    )
```
